32 devices in a mesh: dp: 8 (over y, x, core), sp: 4 (over z).
Axes of the slice: x: 2, y: 2, z: 4, core: 2. Of those that a mesh axis runs over, the one named last changes fastest.
Arguments:
- layer_input: bfloat16 [8, 512, 2048], P('dp', 'sp'), may hold values from -6 to 6
- lengths: int32 [8], P('dp'), may hold values from 128 to 512, as said below
- cotangent: bfloat16 [8, 512, 2048], P('dp', 'sp'), may hold values from -6 to 6
- ln1_gain: bfloat16 [2048], P(('dp', 'sp')), may hold values from 0.5 to 1.5
- ln1_bias: bfloat16 [2048], P(('dp', 'sp')), may hold values from -3 to 3
- ln2_gain: bfloat16 [2048], P(('dp', 'sp')), may hold values from 0.5 to 1.5
- ln2_bias: bfloat16 [2048], P(('dp', 'sp')), may hold values from -3 to 3
- qkv_weight: bfloat16 [2048, 6144], P('dp', 'sp'), may hold values from -0.125 to 0.125
- qkv_bias: bfloat16 [6144], P(('dp', 'sp')), may hold values from -3 to 3
- out_weight: bfloat16 [2048, 2048], P('sp', 'dp'), may hold values from -1 to 1
- gate_weight: bfloat16 [2048, 5632], P('dp', 'sp'), may hold values from -0.125 to 0.125
- up_weight: bfloat16 [2048, 5632], P('dp', 'sp'), may hold values from -0.125 to 0.125
- down_weight: bfloat16 [2048, 5632], P('dp', 'sp'), may hold values from -0.078125 to 0.078125
Outputs:
- layer_output: bfloat16 [8, 512, 2048], P('dp', 'sp')
- input_grad: float32 [8, 512, 2048], P('dp', 'sp')
- ln1_gain_grad: float32 [2048], P(('dp', 'sp'))
- ln1_bias_grad: float32 [2048], P(('dp', 'sp'))
- ln2_gain_grad: float32 [2048], P(('dp', 'sp'))
- ln2_bias_grad: float32 [2048], P(('dp', 'sp'))
- qkv_weight_grad: float32 [2048, 6144], P('dp', 'sp')
- qkv_bias_grad: float32 [6144], P(('dp', 'sp'))
- out_weight_grad: float32 [2048, 2048], P('sp', 'dp')
- gate_weight_grad: float32 [2048, 5632], P('dp', 'sp')
- up_weight_grad: float32 [2048, 5632], P('dp', 'sp')
- down_weight_grad: float32 [2048, 5632], P('dp', 'sp')
The draws below stay inside these ranges and needn't reach their ends.
Inputs may be any that keep to these rules, and one draw needn't show every extreme that they name: Row r holds one sequence in its first lengths[r] slots; some row is full in every draw.
All inputs are finite; a program needn't handle non-finite values.
Results may differ from the reference program's by a relative error of at most 0.015.
Values may be sent and summed in bfloat16 or wider, within the bound.
A program may use at most 192 MiB of HBM per device.

```python
import jax
import jax.numpy as jnp
from jax import lax

D = 2048
HEADS = 32
FF = 5632
HEAD_DIM = 64
ROT = 16
MIN_LEN = 128
SEQ = 512
ROWS = 8


def draw_lengths(key, part):
    levels = (SEQ // MIN_LEN).bit_length() - 1
    key_expo, key_jitter, key_pick = jax.random.split(key, 3)
    exponent = jax.random.randint(key_expo, (ROWS,), 0, levels + 1)
    base_len = jnp.left_shift(jnp.full((ROWS,), MIN_LEN, jnp.int32), exponent.astype(jnp.int32))
    jitter = jax.random.randint(key_jitter, (ROWS,), 0, base_len)
    length = jnp.minimum(base_len + jitter, SEQ).astype(jnp.int32)
    picked = jax.random.randint(key_pick, (), 0, ROWS)
    return jnp.where(jnp.arange(ROWS) == picked, SEQ, length).astype(jnp.int32)


def block_scale(stream_key, shape, cuts, smallest, high):
    level = 1.0
    for axis_at, shards_of in cuts:
        steps = jax.random.uniform(jax.random.fold_in(jax.random.fold_in(stream_key, 6), axis_at), (shards_of,), jnp.float32, smallest / len(cuts), high / len(cuts))
        level = level * jnp.repeat(jnp.exp(steps), shape[axis_at] // shards_of).reshape((-1,) + (1,) * (len(shape) - 1 - axis_at))
    return level


def normal_values(rng, shape, spread, limit, cuts=(), held_as=jnp.bfloat16):
    array = spread * jax.random.normal(rng, shape, jnp.float32)
    if cuts:
        array = array * block_scale(rng, shape, cuts, -0.22, 0.18)
    return jnp.clip(array, -limit, limit).astype(held_as)


def setup_inputs(seed: int = 0) -> dict:
    key_of = jax.random.split(jax.random.key(seed), 14)
    layer_input = normal_values(key_of[0], (ROWS, SEQ, D), 1.0, 6.0, ((0, 8), (1, 4)))
    lengths = draw_lengths(jax.random.fold_in(key_of[13], 71), 0)
    cotangent = normal_values(key_of[2], (ROWS, SEQ, D), 1.0, 6.0, ((0, 8), (1, 4)))
    ln1_gain = jnp.clip(1.0 + 0.1 * jax.random.normal(key_of[3], (D,), jnp.float32), 0.5, 1.5).astype(jnp.bfloat16)
    ln1_bias = normal_values(key_of[4], (D,), 0.3, 3.0, ((0, 32),))
    ln2_gain = jnp.clip(1.0 + 0.1 * jax.random.normal(key_of[5], (D,), jnp.float32), 0.5, 1.5).astype(jnp.bfloat16)
    ln2_bias = normal_values(key_of[6], (D,), 0.3, 3.0, ((0, 32),))
    qkv_weight = normal_values(key_of[7], (D, 3 * D), D ** -0.5, 0.125, ((0, 8), (1, 4)))
    qkv_bias = normal_values(key_of[8], (3 * D,), 0.5, 3.0, ((0, 32),))
    out_weight = normal_values(key_of[9], (D, D), (D // 64) ** -0.5, 1.0, ((0, 4), (1, 8)))
    gate_weight = normal_values(key_of[10], (D, FF), D ** -0.5, 0.125, ((0, 8), (1, 4)))
    up_weight = normal_values(key_of[11], (D, FF), D ** -0.5, 0.125, ((0, 8), (1, 4)))
    down_weight = normal_values(key_of[12], (D, FF), FF ** -0.5, 0.078125, ((0, 8), (1, 4)))
    return dict(layer_input=layer_input, lengths=lengths, cotangent=cotangent, ln1_gain=ln1_gain, ln1_bias=ln1_bias, ln2_gain=ln2_gain, ln2_bias=ln2_bias, qkv_weight=qkv_weight, qkv_bias=qkv_bias, out_weight=out_weight, gate_weight=gate_weight, up_weight=up_weight, down_weight=down_weight)


eps_norm = 1e-05
theta = 10000.0
neg_large = -1e+30
highest = lax.Precision.HIGHEST

@jax.custom_vjp
def low(v):
    return lax.optimization_barrier(v.astype(jnp.bfloat16)).astype(jnp.float32)

@jax.custom_vjp
def low_back(v):
    return v

def low_keep(v):
    return (low(v), None)

def low_pass(kept, grad):
    return (grad,)

def back_keep(v):
    return (v, None)

def back_low(kept, grad):
    return (low(grad),)
low.defvjp(low_keep, low_pass)
low_back.defvjp(back_keep, back_low)

def matmul(left, right):
    return jnp.dot(left, right, precision=highest, preferred_element_type=jnp.float32)

def layer_norm(hidden, gain, bias):
    centre = hidden - lax.optimization_barrier(jnp.mean(hidden, axis=-1, keepdims=True))
    variance = lax.optimization_barrier(jnp.mean(centre * centre, axis=-1, keepdims=True))
    return centre * lax.rsqrt(variance + eps_norm) * gain + bias

def rotate(tensor, cosine, sine):
    half_rot = ROT // 2
    first = tensor[..., :half_rot]
    second = tensor[..., half_rot:ROT]
    return jnp.concatenate([first * cosine - second * sine, second * cosine + first * sine, tensor[..., ROT:]], axis=-1)

def forward(params, hidden, length):
    gain_one, bias_one, gain_two, bias_two, w_qkv, b_qkv, w_out, w_gate, w_up, w_down = params
    positions = jnp.arange(SEQ, dtype=jnp.int32)
    valid = (positions < length).astype(jnp.float32)[:, None]
    normed_one = low(layer_norm(hidden, gain_one, bias_one))
    qkv_raw = low_back(matmul(normed_one, w_qkv) + b_qkv).reshape(SEQ, HEADS, 3, HEAD_DIM)
    freq = theta ** (-(jnp.arange(ROT // 2, dtype=jnp.float32) * 2.0) / ROT)
    angles = positions.astype(jnp.float32)[:, None] * freq[None, :]
    cosine = jnp.cos(angles)[:, None, :]
    sine = jnp.sin(angles)[:, None, :]
    queries = low_back(low(rotate(qkv_raw[:, :, 0], cosine, sine)))
    keys = low_back(low(rotate(qkv_raw[:, :, 1], cosine, sine)))
    values = low_back(low(qkv_raw[:, :, 2]))
    softmax_scale = HEAD_DIM ** (-0.5)
    block_rows = min(512, SEQ)

    def attend(block_index):
        first_row = block_index * block_rows
        query_block = lax.dynamic_slice_in_dim(queries, first_row, block_rows, 0)
        scores = low_back(jnp.einsum('qhd,khd->hqk', query_block, keys, precision=highest) * softmax_scale)
        query_pos = first_row + jnp.arange(block_rows, dtype=jnp.int32)
        allowed = (positions[None, :] <= query_pos[:, None]) & (positions < length)[None, :]
        scores = jnp.where(allowed[None], scores, neg_large)
        attn_weights = low(jax.nn.softmax(scores, axis=-1))
        return jnp.einsum('hqk,khd->qhd', attn_weights, values, precision=highest)
    attended = lax.map(jax.checkpoint(attend), jnp.arange(SEQ // block_rows, dtype=jnp.int32))
    attended = low_back(low(attended.reshape(SEQ, D)))
    branch = low_back(matmul(attended, w_out))
    resid = hidden + branch
    normed_two = low(layer_norm(resid, gain_two, bias_two))
    gate = low_back(matmul(normed_two, w_gate))
    up_proj = low_back(matmul(normed_two, w_up))
    hidden_act = low(jax.nn.silu(gate) * up_proj)
    mixed = low_back(matmul(hidden_act, w_down.T))
    return valid * (resid + mixed)

def reference(layer_input, lengths, cotangent, ln1_gain, ln1_bias, ln2_gain, ln2_bias, qkv_weight, qkv_bias, out_weight, gate_weight, up_weight, down_weight):
    params = (ln1_gain.astype(jnp.float32), ln1_bias.astype(jnp.float32), ln2_gain.astype(jnp.float32), ln2_bias.astype(jnp.float32), qkv_weight.astype(jnp.float32), qkv_bias.astype(jnp.float32), out_weight.astype(jnp.float32), gate_weight.astype(jnp.float32), up_weight.astype(jnp.float32), down_weight.astype(jnp.float32))

    def one_row(totals, row_data):
        row_input, row_length, row_cot = row_data

        def apply(param_set, hidden):
            return forward(param_set, hidden, row_length)
        result, pullback = jax.vjp(apply, params, row_input.astype(jnp.float32))
        param_grads, input_grads = pullback(row_cot.astype(jnp.float32))
        totals = jax.tree.map(lambda left, right: left + right, totals, param_grads)
        return (totals, (result.astype(jnp.bfloat16), input_grads))
    zeros = jax.tree.map(jnp.zeros_like, params)
    totals, (results, input_grads) = lax.scan(one_row, zeros, (layer_input, lengths, cotangent))
    return (results, input_grads, totals[0], totals[1], totals[2], totals[3], totals[4], totals[5], totals[6], totals[7], totals[8], totals[9])
```

```python
import functools

import jax
import jax.numpy as jnp
import numpy as np
from jax import lax
from jax.experimental import pallas as pl
from jax.experimental.pallas import tpu as pltpu
from jax.sharding import PartitionSpec as P

HEAD_DIM = 64
ROT = 16
F32 = jnp.float32
BF16 = jnp.bfloat16
MESH = pl.DeviceIdType.MESH


eps_norm = 1e-05
theta = 10000.0
neg_large = -1e30


def norm_forward(hidden, gain, bias):
    centre = hidden - jnp.mean(hidden, axis=-1, keepdims=True)
    rstd = lax.rsqrt(jnp.mean(centre * centre, axis=-1, keepdims=True) + eps_norm)
    normed = centre * rstd
    return (normed * gain + bias, normed, rstd)


def norm_backward(grad, normed, rstd, gain):
    gain_grad = jnp.sum(grad * normed, axis=0)
    bias_grad = jnp.sum(grad, axis=0)
    scaled = grad * gain
    input_part = rstd * (
        scaled
        - jnp.mean(scaled, axis=-1, keepdims=True)
        - normed * jnp.mean(scaled * normed, axis=-1, keepdims=True)
    )
    return (input_part, gain_grad, bias_grad)


def rotate(tensor, cosine, sine, direction):
    half_rot = ROT // 2
    first = tensor[..., :half_rot]
    second = tensor[..., half_rot:ROT]
    cos_part = cosine[None, :, None, :]
    sin_part = sine[None, :, None, :] * direction
    return jnp.concatenate(
        [
            first * cos_part - second * sin_part,
            second * cos_part + first * sin_part,
            tensor[..., ROT:],
        ],
        axis=-1,
    )


def rotary_tables(position_list):
    freq = theta ** (-(jnp.arange(ROT // 2, dtype=jnp.float32) * 2.0) / ROT)
    angles = position_list.astype(jnp.float32)[:, None] * freq[None, :]
    return (jnp.cos(angles), jnp.sin(angles))


def contract_rows(left, right):
    return lax.dot_general(
        left, right, (((0,), (0,)), ((), ())), preferred_element_type=jnp.float32
    )


def contract_cols(left, right):
    return lax.dot_general(
        left, right, (((1,), (1,)), ((), ())), preferred_element_type=jnp.float32
    )


def block_scores(query_block, keys, first_row, length, block_rows):
    softmax_scale = HEAD_DIM ** (-0.5)
    key_pos = jnp.arange(keys.shape[0], dtype=jnp.int32)
    query_pos = first_row + jnp.arange(block_rows, dtype=jnp.int32)
    scores = (
        jnp.einsum("qhd,khd->hqk", query_block, keys, preferred_element_type=jnp.float32)
        * softmax_scale
    )
    allowed = (key_pos[None, :] <= query_pos[:, None]) & (key_pos < length)[None, :]
    return jnp.where(allowed[None], scores, neg_large)


def attend_forward(queries, keys, values, length, block_rows):

    def one_block(block_index):
        first_row = block_index * block_rows
        query_block = lax.dynamic_slice_in_dim(queries, first_row, block_rows, 0)
        scores = block_scores(query_block, keys, first_row, length, block_rows)
        top_score = jnp.max(scores, axis=-1, keepdims=True)
        total = jnp.sum(jnp.exp(scores - top_score), axis=-1, keepdims=True)
        log_total = top_score + jnp.log(total)
        attn_weights = jnp.exp(scores - log_total).astype(jnp.bfloat16)
        result = jnp.einsum(
            "hqk,khd->qhd", attn_weights, values, preferred_element_type=jnp.float32
        )
        return (result.astype(jnp.bfloat16), log_total[..., 0])

    results, log_totals = lax.map(
        one_block, jnp.arange(queries.shape[0] // block_rows, dtype=jnp.int32)
    )
    return (results.reshape(queries.shape), log_totals)


def attend_backward(queries, keys, values, grad_out, log_totals, length, block_rows):
    softmax_scale = HEAD_DIM ** (-0.5)

    def one_block(carry, block_index):
        key_grad, value_grad = carry
        first_row = block_index * block_rows
        query_block = lax.dynamic_slice_in_dim(queries, first_row, block_rows, 0)
        grad_block = lax.dynamic_slice_in_dim(grad_out, first_row, block_rows, 0)
        scores = block_scores(query_block, keys, first_row, length, block_rows)
        weights_full = jnp.exp(scores - log_totals[block_index][..., None])
        attn_weights = weights_full.astype(jnp.bfloat16)
        weight_grad = jnp.einsum(
            "qhd,khd->hqk", grad_block, values, preferred_element_type=jnp.float32
        )
        delta = jnp.sum(weight_grad * weights_full, axis=-1, keepdims=True)
        score_grad = (weights_full * (weight_grad - delta)).astype(jnp.bfloat16)
        query_grad = (
            jnp.einsum("hqk,khd->qhd", score_grad, keys, preferred_element_type=jnp.float32)
            * softmax_scale
        )
        key_grad = (
            key_grad
            + jnp.einsum(
                "hqk,qhd->khd", score_grad, query_block, preferred_element_type=jnp.float32
            )
            * softmax_scale
        )
        value_grad = value_grad + jnp.einsum(
            "hqk,qhd->khd", attn_weights, grad_block, preferred_element_type=jnp.float32
        )
        return ((key_grad, value_grad), query_grad)

    zeros = jnp.zeros(keys.shape, jnp.float32)
    (key_grad, value_grad), query_grad = lax.scan(
        one_block, (zeros, zeros), jnp.arange(queries.shape[0] // block_rows, dtype=jnp.int32)
    )
    return (query_grad.reshape(queries.shape), key_grad, value_grad)


def feed_forward(tokens, grads_out, w_gate, w_up, w_down):
    gate = jnp.dot(tokens, w_gate, preferred_element_type=jnp.float32)
    up_proj = jnp.dot(tokens, w_up, preferred_element_type=jnp.float32)
    sigmoid_gate = jax.nn.sigmoid(gate)
    silu_gate = gate * sigmoid_gate
    hidden_act = (silu_gate * up_proj).astype(jnp.bfloat16)
    mixed = contract_cols(hidden_act, w_down)
    act_grad = jnp.dot(grads_out, w_down, preferred_element_type=jnp.float32)
    up_grad = (act_grad * silu_gate).astype(jnp.bfloat16)
    gate_grad = (act_grad * up_proj * sigmoid_gate * (1.0 + gate * (1.0 - sigmoid_gate))).astype(
        jnp.bfloat16
    )
    token_grad = contract_cols(gate_grad, w_gate) + contract_cols(up_grad, w_up)
    weight_grads = (
        contract_rows(tokens, gate_grad),
        contract_rows(tokens, up_grad),
        contract_rows(grads_out, hidden_act),
    )
    return (mixed, token_grad, weight_grads)


def per_device(
    layer_input,
    lengths,
    cotangent,
    ln1_gain,
    ln1_bias,
    ln2_gain,
    ln2_bias,
    qkv_weight,
    qkv_bias,
    out_weight,
    gate_weight,
    up_weight,
    down_weight,
):
    row_count, slot_count, width = layer_input.shape
    sp_count = lax.axis_size("sp")
    sp_index = lax.axis_index("sp")
    tokens_dev = row_count * slot_count
    seq_len = slot_count * sp_count
    block_rows = min(512, seq_len)
    local_width = width // sp_count
    local_heads = local_width // HEAD_DIM
    local_cols = 3 * local_width
    positions = sp_index * slot_count + jnp.arange(slot_count, dtype=jnp.int32)
    valid = (positions[None, :] < lengths[:, None]).astype(jnp.float32).reshape(tokens_dev, 1)
    small = (
        lax.all_gather(ln1_gain, ("dp", "sp"), axis=0, tiled=True),
        lax.all_gather(ln1_bias, ("dp", "sp"), axis=0, tiled=True),
        lax.all_gather(ln2_gain, ("dp", "sp"), axis=0, tiled=True),
        lax.all_gather(ln2_bias, ("dp", "sp"), axis=0, tiled=True),
        lax.all_gather(qkv_bias, ("dp", "sp"), axis=0, tiled=True),
    )
    gain_one = small[0].astype(jnp.float32)
    bias_one = small[1].astype(jnp.float32)
    gain_two = small[2].astype(jnp.float32)
    bias_two = small[3].astype(jnp.float32)
    b_qkv = small[4].astype(jnp.float32)
    qkv_cols, out_rows, gate_cols, up_cols, down_cols = (
        lax.all_gather(qkv_weight, "dp", axis=0, tiled=True),
        lax.all_gather(out_weight, "dp", axis=1, tiled=True),
        lax.all_gather(gate_weight, "dp", axis=0, tiled=True),
        lax.all_gather(up_weight, "dp", axis=0, tiled=True),
        lax.all_gather(down_weight, "dp", axis=0, tiled=True),
    )
    w_gate, w_up, w_down = (gate_cols, up_cols, down_cols)
    hidden_in = layer_input.astype(jnp.float32).reshape(tokens_dev, width)
    normed_one, unit_one, rstd_one = norm_forward(hidden_in, gain_one, bias_one)
    normed_one = normed_one.astype(jnp.bfloat16)
    cosine, sine = rotary_tables(jnp.arange(seq_len, dtype=jnp.int32))
    row_normed = lax.all_gather(
        normed_one.reshape(row_count, slot_count, width), "sp", axis=1, tiled=True
    ).reshape(row_count * seq_len, width)
    bias_local = lax.dynamic_slice_in_dim(b_qkv, sp_index * local_cols, local_cols)
    qkv_raw = (
        jnp.dot(row_normed, qkv_cols, preferred_element_type=jnp.float32) + bias_local
    ).reshape(row_count, seq_len, local_heads, 3, HEAD_DIM)
    query_heads = (
        rotate(qkv_raw[:, :, :, 0], cosine, sine, 1.0)
        .astype(jnp.bfloat16)
        .reshape(row_count, seq_len, local_width)
    )
    key_heads = (
        rotate(qkv_raw[:, :, :, 1], cosine, sine, 1.0)
        .astype(jnp.bfloat16)
        .reshape(row_count, seq_len, local_width)
    )
    value_heads = qkv_raw[:, :, :, 2].astype(jnp.bfloat16).reshape(row_count, seq_len, local_width)
    head_shape = (seq_len, local_heads, HEAD_DIM)

    def forward_row(row_data):
        row_query, row_key, row_value, row_length = row_data
        return attend_forward(
            row_query.reshape(head_shape),
            row_key.reshape(head_shape),
            row_value.reshape(head_shape),
            row_length,
            block_rows,
        )

    attended_heads, log_totals = lax.map(
        forward_row, (query_heads, key_heads, value_heads, lengths)
    )
    attended_heads = attended_heads.reshape(row_count, seq_len, local_width)
    attended_flat = attended_heads.reshape(row_count * seq_len, local_width)
    branch_part = jnp.dot(attended_flat, out_rows, preferred_element_type=jnp.float32).reshape(
        row_count, seq_len, width
    )
    branch = lax.psum_scatter(branch_part, "sp", scatter_dimension=1, tiled=True).reshape(
        tokens_dev, width
    )
    resid = hidden_in + branch
    normed_two, unit_two, rstd_two = norm_forward(resid, gain_two, bias_two)
    normed_two = normed_two.astype(jnp.bfloat16)
    out_grad = (cotangent.astype(jnp.float32).reshape(tokens_dev, width) * valid).astype(
        jnp.bfloat16
    )
    row_tokens, row_grads = (
        lax.all_gather(normed_two.reshape(row_count, slot_count, width), "sp", axis=1, tiled=True),
        lax.all_gather(out_grad.reshape(row_count, slot_count, width), "sp", axis=1, tiled=True),
    )
    mixed_part, token_grad_part, mlp_grads = feed_forward(
        row_tokens.reshape(row_count * seq_len, width),
        row_grads.reshape(row_count * seq_len, width),
        w_gate,
        w_up,
        w_down,
    )
    mixed, normed_two_grad = (
        lax.psum_scatter(
            mixed_part.reshape(row_count, seq_len, width), "sp", scatter_dimension=1, tiled=True
        ),
        lax.psum_scatter(
            token_grad_part.reshape(row_count, seq_len, width),
            "sp",
            scatter_dimension=1,
            tiled=True,
        ),
    )
    mixed = mixed.reshape(tokens_dev, width)
    normed_two_grad = normed_two_grad.reshape(tokens_dev, width)
    layer_output = (
        (valid * (resid + mixed)).astype(jnp.bfloat16).reshape(row_count, slot_count, width)
    )
    resid_part, gain_two_grad, bias_two_grad = norm_backward(
        normed_two_grad, unit_two, rstd_two, gain_two
    )
    resid_grad = out_grad.astype(jnp.float32) + resid_part
    branch_grad = resid_grad.astype(jnp.bfloat16)
    row_branch = lax.all_gather(
        branch_grad.reshape(row_count, slot_count, width), "sp", axis=1, tiled=True
    ).reshape(row_count * seq_len, width)
    out_weight_grad = contract_rows(attended_flat, row_branch)
    attended_grad_heads = (
        contract_cols(row_branch, out_rows)
        .astype(jnp.bfloat16)
        .reshape(row_count, seq_len, local_width)
    )

    def backward_row(row_data):
        row_query, row_key, row_value, row_grad, row_totals, row_length = row_data
        query_grad, key_grad, value_grad = attend_backward(
            row_query.reshape(head_shape),
            row_key.reshape(head_shape),
            row_value.reshape(head_shape),
            row_grad.reshape(head_shape),
            row_totals,
            row_length,
            block_rows,
        )
        return (
            query_grad.astype(jnp.bfloat16).reshape(seq_len, local_width),
            key_grad.astype(jnp.bfloat16).reshape(seq_len, local_width),
            value_grad.astype(jnp.bfloat16).reshape(seq_len, local_width),
        )

    query_grads, key_grads, value_grads = lax.map(
        backward_row,
        (query_heads, key_heads, value_heads, attended_grad_heads, log_totals, lengths),
    )
    row_shape = (row_count, seq_len, local_heads, HEAD_DIM)
    query_raw = rotate(query_grads.astype(jnp.float32).reshape(row_shape), cosine, sine, -1.0)
    key_raw = rotate(key_grads.astype(jnp.float32).reshape(row_shape), cosine, sine, -1.0)
    value_raw = value_grads.astype(jnp.float32).reshape(row_shape)
    qkv_grad = (
        jnp.stack([query_raw, key_raw, value_raw], axis=3)
        .reshape(row_count * seq_len, local_cols)
        .astype(jnp.bfloat16)
    )
    bias_local_grad = jnp.sum(qkv_grad.astype(jnp.float32), axis=0)
    qkv_bias_full = lax.dynamic_update_slice(
        jnp.zeros((3 * width,), jnp.float32), bias_local_grad, (sp_index * local_cols,)
    )
    qkv_weight_grad = contract_rows(row_normed, qkv_grad)
    normed_part = contract_cols(qkv_grad, qkv_cols).reshape(row_count, seq_len, width)
    normed_one_grad = (
        lax.psum_scatter(normed_part.astype(jnp.bfloat16), "sp", scatter_dimension=1, tiled=True)
        .astype(jnp.float32)
        .reshape(tokens_dev, width)
    )
    input_part, gain_one_grad, bias_one_grad = norm_backward(
        normed_one_grad, unit_one, rstd_one, gain_one
    )
    input_grad = (resid_grad + input_part).reshape(row_count, slot_count, width)
    small_sums = (
        lax.psum_scatter(gain_one_grad, ("dp", "sp"), scatter_dimension=0, tiled=True),
        lax.psum_scatter(bias_one_grad, ("dp", "sp"), scatter_dimension=0, tiled=True),
        lax.psum_scatter(gain_two_grad, ("dp", "sp"), scatter_dimension=0, tiled=True),
        lax.psum_scatter(bias_two_grad, ("dp", "sp"), scatter_dimension=0, tiled=True),
        lax.psum_scatter(qkv_bias_full, ("dp", "sp"), scatter_dimension=0, tiled=True),
    )
    row_sums = (
        lax.psum_scatter(
            qkv_weight_grad.astype(jnp.bfloat16), "dp", scatter_dimension=0, tiled=True
        ).astype(jnp.float32),
        lax.psum_scatter(
            out_weight_grad.astype(jnp.bfloat16), "dp", scatter_dimension=1, tiled=True
        ).astype(jnp.float32),
        lax.psum_scatter(
            mlp_grads[0].astype(jnp.bfloat16), "dp", scatter_dimension=0, tiled=True
        ).astype(jnp.float32),
        lax.psum_scatter(
            mlp_grads[1].astype(jnp.bfloat16), "dp", scatter_dimension=0, tiled=True
        ).astype(jnp.float32),
        lax.psum_scatter(
            mlp_grads[2].astype(jnp.bfloat16), "dp", scatter_dimension=0, tiled=True
        ).astype(jnp.float32),
    )
    return (
        layer_output,
        input_grad,
        small_sums[0],
        small_sums[1],
        small_sums[2],
        small_sums[3],
        row_sums[0],
        small_sums[4],
        row_sums[1],
        row_sums[2],
        row_sums[3],
        row_sums[4],
    )


def dot_nn(left, right):
    return lax.dot_general(left, right, (((1,), (0,)), ((), ())), preferred_element_type=F32)


def dot_nt(left, right):
    return lax.dot_general(left, right, (((1,), (1,)), ((), ())), preferred_element_type=F32)


def dot_tn(left, right):
    return lax.dot_general(left, right, (((0,), (0,)), ((), ())), preferred_element_type=F32)


def iota(shape, dim):
    return lax.broadcasted_iota(jnp.int32, shape, dim)


def tile(index, size):
    return pl.ds(pl.multiple_of(index * size, size), size)


def normalize(hidden):
    centre = hidden - jnp.mean(hidden, axis=-1, keepdims=True)
    rstd = lax.rsqrt(jnp.mean(centre * centre, axis=-1, keepdims=True) + eps_norm)
    return centre * rstd, rstd


class Plan:
    def __init__(self, dp, sp, slots, width, ff_cols):
        self.dp, self.sp, self.slots, self.width = dp, sp, slots, width
        self.chips = dp // 2
        self.chunk = 2 * slots
        self.tokens = sp * self.chunk
        self.seq = sp * slots
        self.shard = width // dp
        self.head_cols = width // sp // 2
        self.pairs = self.head_cols // 128
        self.qkv_cols = 3 * self.head_cols
        self.ff_cols = ff_cols
        lanes = ff_cols // 128
        self.ff_wide = -(-lanes // 2) * 128
        self.ff_slim = ff_cols - self.ff_wide
        self.count_send = 0
        self.count_recv = 0

    def sems(self, send, recv):
        at = (self.count_send, self.count_recv)
        self.count_send += send
        self.count_recv += recv
        return at


def layer_kernel(plan, sem_at, *refs):
    (
        x_in, cot_in, small_in, cos_in, sin_in, wqkv_in, wout_in, wg_in, wu_in, wd_in,
        out_ref, grad_ref, sums_ref, rg_qkv, rg_out, rg_gate, rg_up, rg_down, n1_hbm,
        ssem, rsem, lsem,
        w_qkv, w_out, w_gate, w_up, w_down,
        buf_a, buf_b, buf_c,
        part, part_x, part_r, mix, mix_x, mix_r,
        q_ref, k_ref, v_ref, att, datt, dqkv, raw,
        act, dgate, dup, kacc, vacc,
        resid, acc, dres,
        small, vecs, qbias, lens, colsum, biassum, send_sum, recv_sum, z_sum,
    ) = refs
    sp, dp, slots, width, chunk = plan.sp, plan.dp, plan.slots, plan.width, plan.chunk
    d = lax.axis_index("dp")
    z = lax.axis_index("sp")
    c = d % 2
    oc = 1 - c
    chip = d // 2
    sib = (d + 1 - 2 * c, z)
    first_row = c * slots
    last = sp - 1

    def remote(src, dst, si, ri, dev):
        return pltpu.make_async_remote_copy(
            src_ref=src, dst_ref=dst, send_sem=ssem.at[si], recv_sem=rsem.at[ri],
            device_id=dev, device_id_type=MESH,
        )

    def wait_send(src, si):
        remote(src, src, si, 0, sib).wait_send()

    def wait_recv(dst, ri):
        remote(dst, dst, 0, ri, sib).wait_recv()

    def block(buf, t, core):
        return buf.at[pl.ds(pl.multiple_of(t * chunk + core * slots, slots), slots)]

    def rows_of(buf, t):
        return buf.at[tile(t, chunk)]

    def slot_block(buf, t):
        return buf.at[tile(t, slots)]

    barrier = pltpu.get_barrier_semaphore()
    for i in range(1, dp):
        pl.semaphore_signal(barrier, inc=1, device_id=((d + i) % dp, z), device_id_type=MESH)
    for i in range(1, sp):
        pl.semaphore_signal(barrier, inc=1, device_id=(d, (z + i) % sp), device_id_type=MESH)
    pl.semaphore_wait(barrier, dp + sp - 2)

    class Gather:
        def __init__(self, name, buf):
            self.s, self.r = sem_at[name]
            self.buf = buf

        def start(self, own):
            s, r = self.s, self.r
            dst = block(self.buf, z, c)

            @pl.when(z < last)
            def _():
                remote(own, dst, s, r + z, (d, z + 1)).start()

            @pl.when(z > 0)
            def _():
                remote(own, dst, s + 1, r + z, (d, z - 1)).start()

            remote(own, dst, s + 2 + sp + z, r + sp + z, sib).start()

        def hop(self, k):
            s, r = self.s, self.r
            for sign in (-1, 1):
                t = z + sign * k
                nxt = z - sign
                blk = block(self.buf, t, c)

                @pl.when((t >= 0) & (t <= last))
                def _():
                    wait_recv(blk, r + t)

                    @pl.when((nxt >= 0) & (nxt <= last))
                    def _():
                        remote(blk, blk, s + 2 + t, r + t, (d, nxt)).start()

                    remote(blk, blk, s + 2 + sp + t, r + sp + t, sib).start()

        def need(self, t):
            wait_recv(block(self.buf, t, oc), self.r + sp + t)

        def drain(self, own):
            s = self.s

            @pl.when(z < last)
            def _():
                wait_send(own, s)

            @pl.when(z > 0)
            def _():
                wait_send(own, s + 1)

            for t in range(sp):
                wait_send(own, s + 2 + sp + t)

                @pl.when(((t < z) & (z < last)) | ((t > z) & (z > 0)))
                def _():
                    wait_send(own, s + 2 + t)

    def order(i):
        low = jnp.minimum(z, last - z)
        k = jnp.where(i <= 2 * low, (i + 1) // 2, i - low)
        paired = jnp.where(i % 2 == 1, z - k, z + k)
        single = jnp.where(z < last - z, z + k, z - k)
        return jnp.where(i <= 2 * low, paired, single)

    def add_into(dst, terms):
        @pl.loop(0, slots // 32)
        def _(i):
            sl = tile(i, 32)
            total = dst[sl, :].astype(F32)
            for term in terms:
                total = total + term[sl, :].astype(F32)
            dst[sl, :] = total.astype(dst.dtype)

    class Scatter:
        def __init__(self, name, parts, from_core, from_line):
            self.s, self.r = sem_at[name]
            self.p, self.x, self.l = parts, from_core, from_line

        def core(self, t):
            remote(
                block(self.p, t, oc), slot_block(self.x, t), self.s + t, self.r + t, sib
            ).start()

        def send(self, t, from_end, nbr, slot):
            mine = block(self.p, t, c)
            xs = slot_block(self.x, t)
            wait_recv(xs, self.r + t)

            @pl.when(from_end)
            def _():
                add_into(mine, [xs])

            @pl.when(jnp.logical_not(from_end))
            def _():
                ls = slot_block(self.l, t)
                wait_recv(ls, self.r + sp + t)
                add_into(mine, [xs, ls])

            remote(
                mine, slot_block(self.l, slot), self.s + sp + t, self.r + sp + slot, (d, nbr)
            ).start()

        def step(self, n):
            left = n - (last - z)

            @pl.when((left >= 0) & (left < z))
            def _():
                self.send(left, z == last, z - 1, left)

            right = n - z

            @pl.when((right >= 0) & (right < last - z))
            def _():
                t = last - right
                self.send(t, z == 0, z + 1, jnp.where(t == z + 1, sp, t))

        def final(self, total):
            mine = block(self.p, z, c)
            xs = slot_block(self.x, z)
            wait_recv(xs, self.r + z)

            @pl.loop(0, slots // 32)
            def _(i):
                sl = tile(i, 32)
                total[sl, :] = mine[sl, :].astype(F32) + xs[sl, :].astype(F32)

            @pl.when(z < last)
            def _():
                ls = slot_block(self.l, z)
                wait_recv(ls, self.r + sp + z)
                add_into(total, [ls])

            @pl.when(z > 0)
            def _():
                ls = slot_block(self.l, sp)
                wait_recv(ls, self.r + sp + sp)
                add_into(total, [ls])

        def drain(self):
            for t in range(sp):
                wait_send(slot_block(self.x, t), self.s + t)

                @pl.when(t != z)
                def _():
                    wait_send(slot_block(self.x, t), self.s + sp + t)

    def chip_target(q):
        cx, cy = chip % 2, chip // 2
        if q % 2:
            cx = 1 - cx
        if q // 2:
            cy = 1 - cy
        return 2 * cx + 4 * cy

    def weight_window(name, src, core):
        if name == "out":
            half = plan.head_cols
            return src.at[pl.ds(core * half, half), :]
        if name == "qkv":
            return src.at[:, pl.ds(core * plan.qkv_cols, plan.qkv_cols)]
        return src.at[:, pl.ds(core * plan.ff_wide, plan.ff_slim if core else plan.ff_wide)]

    def weight_place(name, dst, owner, core):
        if name == "out":
            return dst.at[:, tile(owner, plan.shard)]
        if name == "qkv":
            return dst.at[tile(owner, plan.shard), :]
        return dst.at[tile(owner, plan.shard), pl.ds(0, plan.ff_slim if core else plan.ff_wide)]

    def weight_send(name, src, dst):
        s, r = sem_at["w_" + name]
        for q in (1, 2, 3, 0):
            for core in (0, 1):
                target = chip_target(q) + core
                here = weight_window(name, src, core)
                there = weight_place(name, dst, d, core)
                if q:
                    remote(here, there, s + 2 * q + core, r + d, (target, z)).start()
                else:

                    @pl.when(c != core)
                    def _():
                        remote(here, there, s + 2 * q + core, r + d, (target, z)).start()

                    @pl.when(c == core)
                    def _():
                        pltpu.make_async_copy(here, there, lsem.at[WEIGHTS.index(name)]).start()

    def weight_wait(name, src, dst):
        _, r = sem_at["w_" + name]
        for core in (0, 1):

            @pl.when(c == core)
            def _():
                for i in range(1, dp):
                    other = (d + i) % dp
                    wait_recv(weight_place(name, dst, other, core), r + other)
                pltpu.make_async_copy(
                    weight_window(name, src, core), weight_place(name, dst, d, core),
                    lsem.at[WEIGHTS.index(name)],
                ).wait()

    def weight_drain(name, src):
        s, _ = sem_at["w_" + name]
        for q in range(4):
            for core in (0, 1):
                here = weight_window(name, src, core)
                if q:
                    wait_send(here, s + 2 * q + core)
                else:

                    @pl.when(c != core)
                    def _():
                        wait_send(here, s + 2 * q + core)

    def wgrad_piece(name, src, owner, core):
        if name == "out":
            return src.at[:, tile(owner, plan.shard)]
        if name == "qkv":
            return src.at[tile(owner, plan.shard), :]
        return src.at[tile(owner, plan.shard), pl.ds(0, plan.ff_slim if core else plan.ff_wide)]

    def wgrad_place(name, dst, from_chip, core):
        if name == "out":
            return dst.at[from_chip, pl.ds(core * plan.head_cols, plan.head_cols), :]
        if name == "qkv":
            return dst.at[from_chip, :, pl.ds(core * plan.qkv_cols, plan.qkv_cols)]
        return dst.at[
            from_chip, :, pl.ds(core * plan.ff_wide, plan.ff_slim if core else plan.ff_wide)
        ]

    def wgrad_send(name, src, dst):
        s, r = sem_at["g_" + name]
        for core in (0, 1):

            @pl.when(c == core)
            def _():
                there = wgrad_place(name, dst, chip, core)
                for q in (1, 2, 3, 0):
                    for other_core in (0, 1):
                        target = chip_target(q) + other_core
                        here = wgrad_piece(name, src, target, core)
                        if q or other_core != core:
                            remote(
                                here, there, s + 2 * q + other_core, r + d, (target, z)
                            ).start()
                        else:
                            pltpu.make_async_copy(
                                here, there, lsem.at[len(WEIGHTS) + WEIGHTS.index(name)]
                            ).start()

    def wgrad_finish(name, src, dst):
        s, r = sem_at["g_" + name]
        for core in (0, 1):

            @pl.when(c == core)
            def _():
                for q in range(4):
                    for other_core in (0, 1):
                        target = chip_target(q) + other_core
                        here = wgrad_piece(name, src, target, core)
                        if q or other_core != core:
                            wait_send(here, s + 2 * q + other_core)
                            wait_recv(
                                wgrad_place(name, dst, target // 2, other_core), r + target
                            )
                        else:
                            pltpu.make_async_copy(
                                here, wgrad_place(name, dst, chip, core),
                                lsem.at[len(WEIGHTS) + WEIGHTS.index(name)],
                            ).wait()

    gather_x = Gather("ag_x", buf_a)
    gather_d = Gather("ag_d", buf_c)
    gather_n = Gather("ag_n", buf_a)
    gather_b = Gather("ag_b", buf_b)
    scatter_o = Scatter("rs_o", part, part_x, part_r)
    scatter_n = Scatter("rs_n", part, part_x, part_r)
    scatter_i = Scatter("rs_i", part, part_x, part_r)
    scatter_m = Scatter("rs_m", mix, mix_x, mix_r)

    gather_x.start(x_in)
    sz, rz = sem_at["sm_z"]
    sd, rd = sem_at["sm_d"]
    small[d, z] = small_in[...]
    for i in range(1, sp):
        peer = (z + i) % sp
        remote(small_in, small.at[d, z], sz + i, rz + z, (d, peer)).start()
    weight_send("qkv", wqkv_in, w_qkv)
    weight_send("out", wout_in, w_out)

    block(buf_a, z, c)[...] = x_in[...]
    own_len = small_in[7:8, 0:1]

    @pl.loop(0, slots // 32)
    def _(i):
        sl = tile(i, 32)
        pos = (iota((32, 1), 0) + (z * slots + i * 32)).astype(F32)
        keep = jnp.where(pos < own_len, 1.0, 0.0)
        block(buf_c, z, c)[sl, :] = (cot_in[sl, :].astype(F32) * keep).astype(BF16)

    @pl.when(c == 1)
    def _():
        pad = plan.ff_wide - plan.ff_slim
        for ref in (w_gate, w_up, w_down):
            ref[:, plan.ff_slim :] = jnp.zeros((width, pad), BF16)

    for i in range(1, sp):
        peer = (z + i) % sp
        wait_recv(small.at[d, peer], rz + peer)
    for i in range(1, dp):
        peer = (d + i) % dp
        remote(small.at[d], small.at[d], sd + i, rd + d, (peer, z)).start()
    for i in range(1, dp):
        peer = (d + i) % dp
        wait_recv(small.at[peer], rd + peer)
    per_dp = width // dp // 128
    for i in range(dp):
        for h in range(per_dp):
            at = (i * per_dp + h) * 128
            vecs[:, at : at + 128] = small[i, 2 * h] + small[i, 2 * h + 1]
    bias_at = 2 * z + c
    for h in range(sp // 2):
        for k in range(3):
            at = h * 384 + k * 128
            qbias[0:1, at : at + 128] = (
                small[bias_at, 2 * h, 4 + k : 5 + k, :] + small[bias_at, 2 * h + 1, 4 + k : 5 + k, :]
            )
    for r in range(2):
        lens[r : r + 1, :] = small[2 * chip + r, 0, 7:8, :]

    n1 = buf_b
    gain_one, bias_one = vecs[0:1, :], vecs[1:2, :]

    @pl.loop(0, sp)
    def _(i):
        @pl.when(i > 0)
        def _():
            gather_x.hop(i)

        t = order(i)
        gather_x.need(t)
        src, dst = rows_of(buf_a, t), rows_of(n1, t)

        @pl.loop(0, chunk // 32)
        def _(j):
            sl = tile(j, 32)
            unit, _ = normalize(src[sl, :].astype(F32))
            dst[sl, :] = (unit * vecs[0:1, :] + vecs[1:2, :]).astype(BF16)

    gather_d.start(block(buf_c, z, c))
    n1_copy = pltpu.make_async_copy(n1, n1_hbm, lsem.at[2 * len(WEIGHTS)])
    n1_copy.start()

    weight_wait("qkv", wqkv_in, w_qkv)
    weight_send("gate", wg_in, w_gate)
    low = iota((1, 128), 1) < 64
    first_half = iota((1, 128), 1) % 64 < ROT // 2

    def rotated(v, cosine, sine):
        swapped = jnp.where(
            first_half, pltpu.roll(v, 128 - ROT // 2, 1), pltpu.roll(v, ROT // 2, 1)
        )
        return v * cosine + swapped * sine

    @pl.loop(0, sp)
    def _(t):
        src = rows_of(n1, t)

        @pl.loop(0, plan.qkv_cols // 256)
        def _(n):
            sl = tile(n, 256)
            raw[:, sl] = dot_nn(src[...], w_qkv[:, sl]) + qbias[0:1, sl]

        here = tile(t, slots)
        cosine, sine = cos_in[here, :], sin_in[here, :]
        for r in range(2):
            rs = slice(r * slots, (r + 1) * slots)
            for p in range(plan.pairs):
                v0 = raw[rs, p * 384 : p * 384 + 128]
                v1 = raw[rs, p * 384 + 128 : p * 384 + 256]
                v2 = raw[rs, p * 384 + 256 : p * 384 + 384]
                r0 = rotated(v0, cosine, sine)
                r1 = rotated(v1, cosine, sine)
                r2 = rotated(v2, cosine, sine)
                q_ref[r, p, here, :] = jnp.where(low, r0, r1).astype(BF16)
                k_ref[r, p, here, :] = pltpu.roll(jnp.where(low, r2, r0), 64, 1).astype(BF16)
                v_ref[r, p, here, :] = jnp.where(low, v1, v2).astype(BF16)

    q_rows = min(256, plan.seq)
    q_blocks = plan.seq // q_rows
    per_q = q_rows // slots
    scale = HEAD_DIM ** (-0.5)

    def weights_of(r, p, h, qb):
        keys_to = (qb + 1) * q_rows
        mask = low if h == 0 else jnp.logical_not(low)
        qh = jnp.where(mask, q_ref[r, p, qb * q_rows : keys_to, :], 0).astype(BF16)
        scores = dot_nt(k_ref[r, p, 0:keys_to, :], qh) * scale
        key_pos = iota((keys_to, q_rows), 0)
        query_pos = iota((keys_to, q_rows), 1) + qb * q_rows
        length = lens[pl.ds(r, 1), 0:1]
        allowed = (key_pos <= query_pos) & (key_pos.astype(F32) < length)
        scores = jnp.where(allowed, scores, neg_large)
        expo = jnp.exp(scores - jnp.max(scores, axis=0, keepdims=True))
        return expo * (1.0 / jnp.sum(expo, axis=0, keepdims=True))

    def att_rows(r, t):
        return pl.ds(pl.multiple_of(t * chunk + r * slots, slots), slots)

    def attention(r, p):
        for qb in range(q_blocks):
            outs = []
            for h in range(2):
                probs = weights_of(r, p, h, qb).astype(BF16)
                outs.append(dot_tn(probs, v_ref[r, p, 0 : (qb + 1) * q_rows, :]))
            both = jnp.where(low, outs[0], outs[1]).astype(BF16)
            for i in range(per_q):
                att[att_rows(r, qb * per_q + i), p * 128 : (p + 1) * 128] = both[
                    i * slots : (i + 1) * slots
                ]

    @pl.loop(0, 2)
    def _(r):
        for p in range(plan.pairs):
            attention(r, p)

    gather_d.hop(1)
    gather_x.drain(x_in)

    weight_wait("out", wout_in, w_out)
    weight_send("up", wu_in, w_up)
    weight_send("down", wd_in, w_down)

    def far_first(i):
        return jnp.where(z < last - z, last - i, i)

    @pl.loop(0, sp)
    def _(i):
        t = far_first(i)
        src, dst = rows_of(att, t), rows_of(part, t)

        @pl.loop(0, width // 256)
        def _(n):
            sl = tile(n, 256)
            dst[:, sl] = dot_nn(src[...], w_out[:, sl]).astype(BF16)

        scatter_o.core(t)

    scatter_o.step(0)
    for k in range(1, sp - 1):
        scatter_o.step(k)
        gather_d.hop(k + 1)
    scatter_o.final(acc)

    own_n = block(buf_a, z, c)

    @pl.loop(0, slots // 32)
    def _(i):
        sl = tile(i, 32)
        hidden = x_in[sl, :].astype(F32) + acc[sl, :]
        resid[sl, :] = hidden
        unit, _ = normalize(hidden)
        own_n[sl, :] = (unit * vecs[2:3, :] + vecs[3:4, :]).astype(BF16)

    gather_n.start(own_n)
    for i in range(sp):
        gather_d.need(i)
    scatter_o.drain()
    n1_copy.wait()

    weight_wait("gate", wg_in, w_gate)
    weight_wait("up", wu_in, w_up)
    weight_wait("down", wd_in, w_down)

    @pl.loop(0, sp)
    def _(i):
        @pl.when(i > 0)
        def _():
            gather_n.hop(i)

        t = order(i)
        gather_n.need(t)
        tok, gout = rows_of(buf_a, t), rows_of(buf_c, t)
        act_t, dg_t, du_t = rows_of(act, t), rows_of(dgate, t), rows_of(dup, t)
        part_t, mix_t = rows_of(part, t), rows_of(mix, t)

        @pl.loop(0, plan.ff_wide // 256)
        def _(n):
            sl = tile(n, 256)
            gate = dot_nn(tok[...], w_gate[:, sl])
            up = dot_nn(tok[...], w_up[:, sl])
            d_act = dot_nn(gout[...], w_down[:, sl])
            sig = jax.nn.sigmoid(gate)
            silu = gate * sig
            act_t[:, sl] = (silu * up).astype(BF16)
            du_t[:, sl] = (d_act * silu).astype(BF16)
            dg_t[:, sl] = (d_act * up * sig * (1.0 + gate * (1.0 - sig))).astype(BF16)

        @pl.loop(0, width // 256)
        def _(n):
            sl = tile(n, 256)
            part_t[:, sl] = (
                dot_nt(dg_t[...], w_gate[sl, :]) + dot_nt(du_t[...], w_up[sl, :])
            ).astype(BF16)
            mix_t[:, sl] = dot_nt(act_t[...], w_down[sl, :]).astype(BF16)

        scatter_n.core(t)
        scatter_m.core(t)

    def wgrad(tokens, cols, dst):
        @pl.loop(0, width // 256)
        def _(n):
            sl = tile(n, 256)
            dst[sl, :] = dot_tn(tokens[:, sl], cols[...]).astype(BF16)

    scatter_n.step(0)
    weight_drain("down", wd_in)
    wgrad(buf_c, act, w_down)
    wgrad_send("down", w_down, rg_down)
    scatter_n.step(1)
    wgrad(buf_a, dgate, w_gate)
    wgrad_send("gate", w_gate, rg_gate)
    for k in range(2, sp - 1):
        scatter_n.step(k)
    wgrad(buf_a, dup, w_up)
    wgrad_send("up", w_up, rg_up)
    scatter_n.final(acc)

    gather_n.drain(own_n)
    n1_back = pltpu.make_async_copy(n1_hbm, buf_a, lsem.at[2 * len(WEIGHTS) + 1])
    n1_back.start()
    colsum[...] = jnp.zeros_like(colsum)
    own_d, own_b = block(buf_c, z, c), block(buf_b, z, c)

    def norm_back(grad, hidden, gain, row):
        unit, rstd = normalize(hidden)
        colsum[row : row + 1, :] += jnp.sum(grad * unit, axis=0, keepdims=True)
        colsum[row + 1 : row + 2, :] += jnp.sum(grad, axis=0, keepdims=True)
        scaled = grad * gain
        return rstd * (
            scaled
            - jnp.mean(scaled, axis=-1, keepdims=True)
            - unit * jnp.mean(scaled * unit, axis=-1, keepdims=True)
        )

    @pl.loop(0, slots // 32)
    def _(i):
        sl = tile(i, 32)
        back = own_d[sl, :].astype(F32) + norm_back(acc[sl, :], resid[sl, :], vecs[2:3, :], 2)
        dres[sl, :] = back
        own_b[sl, :] = back.astype(BF16)

    gather_b.start(own_b)
    scatter_n.drain()
    scatter_m.step(0)

    @pl.loop(0, sp)
    def _(i):
        @pl.when(i > 0)
        def _():
            gather_b.hop(i)

        @pl.when((i > 0) & (i < last))
        def _():
            scatter_m.step(i)

        t = order(i)
        gather_b.need(t)
        datt[tile(t, chunk), :] = dot_nt(rows_of(buf_b, t)[...], w_out[...]).astype(BF16)

    biassum[...] = jnp.zeros_like(biassum)

    def attention_back(r, p):
        cols = slice(p * 128, (p + 1) * 128)
        for qb in range(q_blocks):
            keys_to = (qb + 1) * q_rows
            dav = jnp.concatenate(
                [datt[att_rows(r, qb * per_q + i), cols] for i in range(per_q)], axis=0
            )
            qv = q_ref[r, p, qb * q_rows : keys_to, :]
            dq, dk, dv = [], [], []
            for h in range(2):
                mask = low if h == 0 else jnp.logical_not(low)
                probs = weights_of(r, p, h, qb)
                dprobs = dot_nt(v_ref[r, p, 0:keys_to, :], jnp.where(mask, dav, 0).astype(BF16))
                delta = jnp.sum(dprobs * probs, axis=0, keepdims=True)
                dscores = (probs * (dprobs - delta)).astype(BF16)
                dv.append(dot_nn(probs.astype(BF16), dav))
                dk.append(dot_nn(dscores, qv))
                dq.append(dot_tn(dscores, k_ref[r, p, 0:keys_to, :]))
            dq_both = (jnp.where(low, dq[0], dq[1]) * scale).astype(BF16)
            dk_both = jnp.where(low, dk[0], dk[1])
            dv_both = jnp.where(low, dv[0], dv[1])
            if qb == 0:
                kacc[0:keys_to, :] = dk_both
                vacc[0:keys_to, :] = dv_both
            else:
                kept = keys_to - q_rows
                kacc[0:kept, :] += dk_both[0:kept]
                vacc[0:kept, :] += dv_both[0:kept]
                kacc[kept:keys_to, :] = dk_both[kept:keys_to]
                vacc[kept:keys_to, :] = dv_both[kept:keys_to]
            q_ref[r, p, qb * q_rows : keys_to, :] = dq_both
        for t in range(sp):
            ts = slice(t * slots, (t + 1) * slots)
            dqv = q_ref[r, p, ts, :].astype(F32)
            dkv = (kacc[ts, :] * scale).astype(BF16).astype(F32)
            dvv = vacc[ts, :].astype(BF16).astype(F32)
            swapped = pltpu.roll(dkv, 64, 1)
            cosine, sine = cos_in[ts, :], -sin_in[ts, :]
            g0 = rotated(jnp.where(low, dqv, swapped), cosine, sine)
            g1 = jnp.where(low, dvv, rotated(dqv, cosine, sine))
            g2 = jnp.where(low, rotated(swapped, cosine, sine), dvv)
            for k, g in enumerate((g0, g1, g2)):
                g = g.astype(BF16)
                dqkv[att_rows(r, t), p * 384 + k * 128 : p * 384 + (k + 1) * 128] = g
                row = 3 * p + k
                biassum[row : row + 1, :] += jnp.sum(g.astype(F32), axis=0, keepdims=True)

    @pl.loop(0, 2)
    def _(r):
        for p in range(plan.pairs):
            attention_back(r, p)

    @pl.loop(0, sp)
    def _(i):
        t = far_first(i)
        dst, src = rows_of(part, t), rows_of(dqkv, t)

        @pl.loop(0, width // 256)
        def _(n):
            sl = tile(n, 256)
            dst[:, sl] = dot_nt(src[...], w_qkv[sl, :]).astype(BF16)

        scatter_i.core(t)

    scatter_i.step(0)
    n1_back.wait()
    wgrad(buf_a, dqkv, w_qkv)
    wgrad_send("qkv", w_qkv, rg_qkv)
    scatter_i.step(1)

    @pl.loop(0, width // 256)
    def _(n):
        sl = tile(n, 256)
        w_out[:, sl] = dot_tn(att[...], buf_b[:, sl]).astype(BF16)

    wgrad_send("out", w_out, rg_out)
    for k in range(2, sp - 1):
        scatter_i.step(k)
    scatter_m.final(acc)

    @pl.loop(0, slots // 32)
    def _(i):
        sl = tile(i, 32)
        pos = (iota((32, 1), 0) + (z * slots + i * 32)).astype(F32)
        keep = jnp.where(pos < small_in[7:8, 0:1], 1.0, 0.0)
        out_ref[sl, :] = (keep * (resid[sl, :] + acc[sl, :])).astype(BF16)

    scatter_i.final(acc)

    @pl.loop(0, slots // 32)
    def _(i):
        sl = tile(i, 32)
        back = norm_back(acc[sl, :], x_in[sl, :].astype(F32), vecs[0:1, :], 0)
        grad_ref[sl, :] = dres[sl, :] + back

    per = plan.shard
    for i in range(dp):
        send_sum[i, :, 0:per] = colsum[:, i * per : (i + 1) * per]
        send_sum[i, :, per : per + 128] = biassum[...]
    sa, ra = sem_at["su_d"]
    sb, rb = sem_at["su_z"]
    recv_sum[d] = send_sum[d]
    for i in range(1, dp):
        peer = (d + i) % dp
        remote(send_sum.at[peer], recv_sum.at[d], sa + i, ra + d, (peer, z)).start()
    for i in range(1, dp):
        peer = (d + i) % dp
        wait_recv(recv_sum.at[peer], ra + peer)
    norm_total = recv_sum[0, :, 0:per]
    for i in range(1, dp):
        norm_total = norm_total + recv_sum[i, :, 0:per]
    bias_total = recv_sum[c, :, per : per + 128]
    for i in range(1, dp // 2):
        bias_total = bias_total + recv_sum[2 * i + c, :, per : per + 128]
    z_sum[z, :, 0:per] = norm_total
    z_sum[z, :, per : per + 128] = bias_total
    for i in range(1, sp):
        peer = (z + i) % sp
        remote(z_sum.at[z], z_sum.at[z], sb + i, rb + z, (d, peer)).start()
    for i in range(1, sp):
        peer = (z + i) % sp
        wait_recv(z_sum.at[peer], rb + peer)
    norm_total = z_sum[0, :, 0:per]
    for i in range(1, sp):
        norm_total = norm_total + z_sum[i, :, 0:per]
    sums_ref[:, 0:per] = norm_total
    sums_ref[:, per : per + 128] = z_sum[chip, :, per : per + 128]

    for name, src, dst in (
        ("down", w_down, rg_down), ("gate", w_gate, rg_gate), ("up", w_up, rg_up),
        ("qkv", w_qkv, rg_qkv), ("out", w_out, rg_out),
    ):
        wgrad_finish(name, src, dst)
    for name, src in (("qkv", wqkv_in), ("out", wout_in), ("gate", wg_in), ("up", wu_in)):
        weight_drain(name, src)
    gather_d.drain(own_d)
    gather_b.drain(own_b)
    scatter_m.drain()
    scatter_i.drain()
    for i in range(1, sp):
        wait_send(small_in, sz + i)
        wait_send(z_sum.at[z], sb + i)
    for i in range(1, dp):
        wait_send(small.at[d], sd + i)
        wait_send(send_sum.at[0], sa + i)


WEIGHTS = ("qkv", "out", "gate", "up", "down")


def rotary_lanes(seq_len):
    half = ROT // 2
    freq = theta ** (-(np.arange(half, dtype=np.float32) * np.float32(2.0)) / np.float32(ROT))
    angles = np.arange(seq_len, dtype=np.float32)[:, None] * freq.astype(np.float32)[None, :]
    cosine, sine = np.cos(angles), np.sin(angles)
    cos_head = np.ones((seq_len, HEAD_DIM), np.float32)
    sin_head = np.zeros((seq_len, HEAD_DIM), np.float32)
    cos_head[:, :half], cos_head[:, half:ROT] = cosine, cosine
    sin_head[:, :half], sin_head[:, half:ROT] = -sine, sine
    return np.tile(cos_head, (1, 2)), np.tile(sin_head, (1, 2))


def per_device_fast(
    layer_input, lengths, cotangent, ln1_gain, ln1_bias, ln2_gain, ln2_bias,
    qkv_weight, qkv_bias, out_weight, gate_weight, up_weight, down_weight,
):
    dp, sp = lax.axis_size("dp"), lax.axis_size("sp")
    z = lax.axis_index("sp")
    _, slots, width = layer_input.shape
    plan = Plan(dp, sp, slots, width, gate_weight.shape[1])
    sem_at = {}
    for name in WEIGHTS:
        sem_at["w_" + name] = plan.sems(8, dp)
        sem_at["g_" + name] = plan.sems(8, dp)
    for name in ("ag_x", "ag_d", "ag_n", "ag_b"):
        sem_at[name] = plan.sems(2 + 2 * sp, 2 * sp)
    for name in ("rs_o", "rs_n", "rs_i", "rs_m"):
        sem_at[name] = plan.sems(2 * sp, 2 * sp + 1)
    for name in ("sm_z", "su_z"):
        sem_at[name] = plan.sems(sp, sp)
    for name in ("sm_d", "su_d"):
        sem_at[name] = plan.sems(dp, dp)

    even = z % 2 == 0
    norms = jnp.stack([ln1_gain, ln1_bias, ln2_gain, ln2_bias]).astype(F32)
    none = jnp.zeros_like(norms)
    norm_rows = jnp.where(
        even, jnp.concatenate([norms, none], 1), jnp.concatenate([none, norms], 1)
    )
    bias = qkv_bias.astype(F32)
    none = jnp.zeros_like(bias)
    bias_rows = jnp.where(
        even, jnp.concatenate([bias, none]), jnp.concatenate([none, bias])
    ).reshape(3, 128)
    len_row = jnp.broadcast_to(lengths.astype(F32)[:, None], (1, 128))
    small = jnp.concatenate([norm_rows, bias_rows, len_row], axis=0)
    cosine, sine = rotary_lanes(sp * slots)

    vmem = pl.BlockSpec(memory_space=pltpu.VMEM)
    hbm = pl.BlockSpec(memory_space=pl.ANY)
    out_shape = [
        jax.ShapeDtypeStruct((slots, width), BF16),
        jax.ShapeDtypeStruct((slots, width), F32),
        jax.ShapeDtypeStruct((8, plan.shard + 128), F32),
        jax.ShapeDtypeStruct((plan.chips,) + qkv_weight.shape, BF16),
        jax.ShapeDtypeStruct((plan.chips,) + out_weight.shape, BF16),
        jax.ShapeDtypeStruct((plan.chips,) + gate_weight.shape, BF16),
        jax.ShapeDtypeStruct((plan.chips,) + up_weight.shape, BF16),
        jax.ShapeDtypeStruct((plan.chips,) + down_weight.shape, BF16),
        jax.ShapeDtypeStruct((plan.tokens, width), BF16),
    ]
    tokens, heads, ff = plan.tokens, plan.head_cols, plan.ff_wide
    scratch = [
        pltpu.SemaphoreType.DMA((plan.count_send,)),
        pltpu.SemaphoreType.DMA((plan.count_recv,)),
        pltpu.SemaphoreType.DMA((2 * len(WEIGHTS) + 2,)),
        pltpu.VMEM((width, plan.qkv_cols), BF16),
        pltpu.VMEM((heads, width), BF16),
        pltpu.VMEM((width, ff), BF16),
        pltpu.VMEM((width, ff), BF16),
        pltpu.VMEM((width, ff), BF16),
        pltpu.VMEM((tokens, width), BF16),
        pltpu.VMEM((tokens, width), BF16),
        pltpu.VMEM((tokens, width), BF16),
        pltpu.VMEM((tokens, width), BF16),
        pltpu.VMEM((sp * slots, width), BF16),
        pltpu.VMEM(((sp + 1) * slots, width), BF16),
        pltpu.VMEM((tokens, width), BF16),
        pltpu.VMEM((sp * slots, width), BF16),
        pltpu.VMEM(((sp + 1) * slots, width), BF16),
        pltpu.VMEM((2, plan.pairs, plan.seq, 128), BF16),
        pltpu.VMEM((2, plan.pairs, plan.seq, 128), BF16),
        pltpu.VMEM((2, plan.pairs, plan.seq, 128), BF16),
        pltpu.VMEM((tokens, heads), BF16),
        pltpu.VMEM((tokens, heads), BF16),
        pltpu.VMEM((tokens, plan.qkv_cols), BF16),
        pltpu.VMEM((plan.chunk, plan.qkv_cols), F32),
        pltpu.VMEM((tokens, ff), BF16),
        pltpu.VMEM((tokens, ff), BF16),
        pltpu.VMEM((tokens, ff), BF16),
        pltpu.VMEM((plan.seq, 128), F32),
        pltpu.VMEM((plan.seq, 128), F32),
        pltpu.VMEM((slots, width), F32),
        pltpu.VMEM((slots, width), F32),
        pltpu.VMEM((slots, width), F32),
        pltpu.VMEM((dp, sp, 8, 128), F32),
        pltpu.VMEM((8, width), F32),
        pltpu.VMEM((8, plan.qkv_cols), F32),
        pltpu.VMEM((8, 128), F32),
        pltpu.VMEM((8, width), F32),
        pltpu.VMEM((8, 128), F32),
        pltpu.VMEM((dp, 8, plan.shard + 128), F32),
        pltpu.VMEM((dp, 8, plan.shard + 128), F32),
        pltpu.VMEM((sp, 8, plan.shard + 128), F32),
    ]
    outs = pl.pallas_call(
        functools.partial(layer_kernel, plan, sem_at),
        out_shape=out_shape,
        in_specs=[vmem] * 5 + [hbm] * 5,
        out_specs=[vmem] * 3 + [hbm] * 6,
        scratch_shapes=scratch,
        compiler_params=pltpu.CompilerParams(
            collective_id=0, has_side_effects=True, vmem_limit_bytes=63 * 1024 * 1024
        ),
    )(
        layer_input[0], cotangent[0], small, jnp.asarray(cosine), jnp.asarray(sine),
        qkv_weight, out_weight, gate_weight, up_weight, down_weight,
    )
    sums = outs[2]
    own = lax.dynamic_slice_in_dim(sums[:4, : plan.shard], z * (plan.shard // sp), plan.shard // sp, 1)
    bias_grad = lax.dynamic_slice_in_dim(
        sums[:, plan.shard :].reshape(-1), z * qkv_bias.shape[0], qkv_bias.shape[0]
    )
    grads = [jnp.sum(g.astype(F32), axis=0) for g in outs[3:8]]
    return (
        outs[0][None], outs[1][None], own[0], own[1], own[2], own[3],
        grads[0], bias_grad, grads[1], grads[2], grads[3], grads[4],
    )


def solution(mesh):
    placed = (
        P("dp", "sp", None),
        P("dp"),
        P("dp", "sp", None),
        P(("dp", "sp")),
        P(("dp", "sp")),
        P(("dp", "sp")),
        P(("dp", "sp")),
        P("dp", "sp"),
        P(("dp", "sp")),
        P("sp", "dp"),
        P("dp", "sp"),
        P("dp", "sp"),
        P("dp", "sp"),
    )
    fast = mesh.shape["dp"] == 8 and mesh.shape["sp"] == 4
    return jax.shard_map(
        per_device_fast if fast else per_device,
        mesh=mesh,
        in_specs=placed,
        out_specs=(
            P("dp", "sp", None),
            P("dp", "sp", None),
            P(("dp", "sp")),
            P(("dp", "sp")),
            P(("dp", "sp")),
            P(("dp", "sp")),
            P("dp", "sp"),
            P(("dp", "sp")),
            P("sp", "dp"),
            P("dp", "sp"),
            P("dp", "sp"),
            P("dp", "sp"),
        ),
        check_vma=False,
    )
```

```python
import functools

import jax
import jax.numpy as jnp
import numpy as np
from jax import lax
from jax.experimental import pallas as pl
from jax.experimental.pallas import tpu as pltpu
from jax.sharding import PartitionSpec as P

HEAD_DIM = 64
ROT = 16
F32 = jnp.float32
BF16 = jnp.bfloat16
MESH = pl.DeviceIdType.MESH


eps_norm = 1e-05
theta = 10000.0
neg_large = -1e30


def norm_forward(hidden, gain, bias):
    centre = hidden - jnp.mean(hidden, axis=-1, keepdims=True)
    rstd = lax.rsqrt(jnp.mean(centre * centre, axis=-1, keepdims=True) + eps_norm)
    normed = centre * rstd
    return (normed * gain + bias, normed, rstd)


def norm_backward(grad, normed, rstd, gain):
    gain_grad = jnp.sum(grad * normed, axis=0)
    bias_grad = jnp.sum(grad, axis=0)
    scaled = grad * gain
    input_part = rstd * (
        scaled
        - jnp.mean(scaled, axis=-1, keepdims=True)
        - normed * jnp.mean(scaled * normed, axis=-1, keepdims=True)
    )
    return (input_part, gain_grad, bias_grad)


def rotate(tensor, cosine, sine, direction):
    half_rot = ROT // 2
    first = tensor[..., :half_rot]
    second = tensor[..., half_rot:ROT]
    cos_part = cosine[None, :, None, :]
    sin_part = sine[None, :, None, :] * direction
    return jnp.concatenate(
        [
            first * cos_part - second * sin_part,
            second * cos_part + first * sin_part,
            tensor[..., ROT:],
        ],
        axis=-1,
    )


def rotary_tables(position_list):
    freq = theta ** (-(jnp.arange(ROT // 2, dtype=jnp.float32) * 2.0) / ROT)
    angles = position_list.astype(jnp.float32)[:, None] * freq[None, :]
    return (jnp.cos(angles), jnp.sin(angles))


def contract_rows(left, right):
    return lax.dot_general(
        left, right, (((0,), (0,)), ((), ())), preferred_element_type=jnp.float32
    )


def contract_cols(left, right):
    return lax.dot_general(
        left, right, (((1,), (1,)), ((), ())), preferred_element_type=jnp.float32
    )


def block_scores(query_block, keys, first_row, length, block_rows):
    softmax_scale = HEAD_DIM ** (-0.5)
    key_pos = jnp.arange(keys.shape[0], dtype=jnp.int32)
    query_pos = first_row + jnp.arange(block_rows, dtype=jnp.int32)
    scores = (
        jnp.einsum("qhd,khd->hqk", query_block, keys, preferred_element_type=jnp.float32)
        * softmax_scale
    )
    allowed = (key_pos[None, :] <= query_pos[:, None]) & (key_pos < length)[None, :]
    return jnp.where(allowed[None], scores, neg_large)


def attend_forward(queries, keys, values, length, block_rows):

    def one_block(block_index):
        first_row = block_index * block_rows
        query_block = lax.dynamic_slice_in_dim(queries, first_row, block_rows, 0)
        scores = block_scores(query_block, keys, first_row, length, block_rows)
        top_score = jnp.max(scores, axis=-1, keepdims=True)
        total = jnp.sum(jnp.exp(scores - top_score), axis=-1, keepdims=True)
        log_total = top_score + jnp.log(total)
        attn_weights = jnp.exp(scores - log_total).astype(jnp.bfloat16)
        result = jnp.einsum(
            "hqk,khd->qhd", attn_weights, values, preferred_element_type=jnp.float32
        )
        return (result.astype(jnp.bfloat16), log_total[..., 0])

    results, log_totals = lax.map(
        one_block, jnp.arange(queries.shape[0] // block_rows, dtype=jnp.int32)
    )
    return (results.reshape(queries.shape), log_totals)


def attend_backward(queries, keys, values, grad_out, log_totals, length, block_rows):
    softmax_scale = HEAD_DIM ** (-0.5)

    def one_block(carry, block_index):
        key_grad, value_grad = carry
        first_row = block_index * block_rows
        query_block = lax.dynamic_slice_in_dim(queries, first_row, block_rows, 0)
        grad_block = lax.dynamic_slice_in_dim(grad_out, first_row, block_rows, 0)
        scores = block_scores(query_block, keys, first_row, length, block_rows)
        weights_full = jnp.exp(scores - log_totals[block_index][..., None])
        attn_weights = weights_full.astype(jnp.bfloat16)
        weight_grad = jnp.einsum(
            "qhd,khd->hqk", grad_block, values, preferred_element_type=jnp.float32
        )
        delta = jnp.sum(weight_grad * weights_full, axis=-1, keepdims=True)
        score_grad = (weights_full * (weight_grad - delta)).astype(jnp.bfloat16)
        query_grad = (
            jnp.einsum("hqk,khd->qhd", score_grad, keys, preferred_element_type=jnp.float32)
            * softmax_scale
        )
        key_grad = (
            key_grad
            + jnp.einsum(
                "hqk,qhd->khd", score_grad, query_block, preferred_element_type=jnp.float32
            )
            * softmax_scale
        )
        value_grad = value_grad + jnp.einsum(
            "hqk,qhd->khd", attn_weights, grad_block, preferred_element_type=jnp.float32
        )
        return ((key_grad, value_grad), query_grad)

    zeros = jnp.zeros(keys.shape, jnp.float32)
    (key_grad, value_grad), query_grad = lax.scan(
        one_block, (zeros, zeros), jnp.arange(queries.shape[0] // block_rows, dtype=jnp.int32)
    )
    return (query_grad.reshape(queries.shape), key_grad, value_grad)


def feed_forward(tokens, grads_out, w_gate, w_up, w_down):
    gate = jnp.dot(tokens, w_gate, preferred_element_type=jnp.float32)
    up_proj = jnp.dot(tokens, w_up, preferred_element_type=jnp.float32)
    sigmoid_gate = jax.nn.sigmoid(gate)
    silu_gate = gate * sigmoid_gate
    hidden_act = (silu_gate * up_proj).astype(jnp.bfloat16)
    mixed = contract_cols(hidden_act, w_down)
    act_grad = jnp.dot(grads_out, w_down, preferred_element_type=jnp.float32)
    up_grad = (act_grad * silu_gate).astype(jnp.bfloat16)
    gate_grad = (act_grad * up_proj * sigmoid_gate * (1.0 + gate * (1.0 - sigmoid_gate))).astype(
        jnp.bfloat16
    )
    token_grad = contract_cols(gate_grad, w_gate) + contract_cols(up_grad, w_up)
    weight_grads = (
        contract_rows(tokens, gate_grad),
        contract_rows(tokens, up_grad),
        contract_rows(grads_out, hidden_act),
    )
    return (mixed, token_grad, weight_grads)


def per_device(
    layer_input,
    lengths,
    cotangent,
    ln1_gain,
    ln1_bias,
    ln2_gain,
    ln2_bias,
    qkv_weight,
    qkv_bias,
    out_weight,
    gate_weight,
    up_weight,
    down_weight,
):
    row_count, slot_count, width = layer_input.shape
    sp_count = lax.axis_size("sp")
    sp_index = lax.axis_index("sp")
    tokens_dev = row_count * slot_count
    seq_len = slot_count * sp_count
    block_rows = min(512, seq_len)
    local_width = width // sp_count
    local_heads = local_width // HEAD_DIM
    local_cols = 3 * local_width
    positions = sp_index * slot_count + jnp.arange(slot_count, dtype=jnp.int32)
    valid = (positions[None, :] < lengths[:, None]).astype(jnp.float32).reshape(tokens_dev, 1)
    small = (
        lax.all_gather(ln1_gain, ("dp", "sp"), axis=0, tiled=True),
        lax.all_gather(ln1_bias, ("dp", "sp"), axis=0, tiled=True),
        lax.all_gather(ln2_gain, ("dp", "sp"), axis=0, tiled=True),
        lax.all_gather(ln2_bias, ("dp", "sp"), axis=0, tiled=True),
        lax.all_gather(qkv_bias, ("dp", "sp"), axis=0, tiled=True),
    )
    gain_one = small[0].astype(jnp.float32)
    bias_one = small[1].astype(jnp.float32)
    gain_two = small[2].astype(jnp.float32)
    bias_two = small[3].astype(jnp.float32)
    b_qkv = small[4].astype(jnp.float32)
    qkv_cols, out_rows, gate_cols, up_cols, down_cols = (
        lax.all_gather(qkv_weight, "dp", axis=0, tiled=True),
        lax.all_gather(out_weight, "dp", axis=1, tiled=True),
        lax.all_gather(gate_weight, "dp", axis=0, tiled=True),
        lax.all_gather(up_weight, "dp", axis=0, tiled=True),
        lax.all_gather(down_weight, "dp", axis=0, tiled=True),
    )
    w_gate, w_up, w_down = (gate_cols, up_cols, down_cols)
    hidden_in = layer_input.astype(jnp.float32).reshape(tokens_dev, width)
    normed_one, unit_one, rstd_one = norm_forward(hidden_in, gain_one, bias_one)
    normed_one = normed_one.astype(jnp.bfloat16)
    cosine, sine = rotary_tables(jnp.arange(seq_len, dtype=jnp.int32))
    row_normed = lax.all_gather(
        normed_one.reshape(row_count, slot_count, width), "sp", axis=1, tiled=True
    ).reshape(row_count * seq_len, width)
    bias_local = lax.dynamic_slice_in_dim(b_qkv, sp_index * local_cols, local_cols)
    qkv_raw = (
        jnp.dot(row_normed, qkv_cols, preferred_element_type=jnp.float32) + bias_local
    ).reshape(row_count, seq_len, local_heads, 3, HEAD_DIM)
    query_heads = (
        rotate(qkv_raw[:, :, :, 0], cosine, sine, 1.0)
        .astype(jnp.bfloat16)
        .reshape(row_count, seq_len, local_width)
    )
    key_heads = (
        rotate(qkv_raw[:, :, :, 1], cosine, sine, 1.0)
        .astype(jnp.bfloat16)
        .reshape(row_count, seq_len, local_width)
    )
    value_heads = qkv_raw[:, :, :, 2].astype(jnp.bfloat16).reshape(row_count, seq_len, local_width)
    head_shape = (seq_len, local_heads, HEAD_DIM)

    def forward_row(row_data):
        row_query, row_key, row_value, row_length = row_data
        return attend_forward(
            row_query.reshape(head_shape),
            row_key.reshape(head_shape),
            row_value.reshape(head_shape),
            row_length,
            block_rows,
        )

    attended_heads, log_totals = lax.map(
        forward_row, (query_heads, key_heads, value_heads, lengths)
    )
    attended_heads = attended_heads.reshape(row_count, seq_len, local_width)
    attended_flat = attended_heads.reshape(row_count * seq_len, local_width)
    branch_part = jnp.dot(attended_flat, out_rows, preferred_element_type=jnp.float32).reshape(
        row_count, seq_len, width
    )
    branch = lax.psum_scatter(branch_part, "sp", scatter_dimension=1, tiled=True).reshape(
        tokens_dev, width
    )
    resid = hidden_in + branch
    normed_two, unit_two, rstd_two = norm_forward(resid, gain_two, bias_two)
    normed_two = normed_two.astype(jnp.bfloat16)
    out_grad = (cotangent.astype(jnp.float32).reshape(tokens_dev, width) * valid).astype(
        jnp.bfloat16
    )
    row_tokens, row_grads = (
        lax.all_gather(normed_two.reshape(row_count, slot_count, width), "sp", axis=1, tiled=True),
        lax.all_gather(out_grad.reshape(row_count, slot_count, width), "sp", axis=1, tiled=True),
    )
    mixed_part, token_grad_part, mlp_grads = feed_forward(
        row_tokens.reshape(row_count * seq_len, width),
        row_grads.reshape(row_count * seq_len, width),
        w_gate,
        w_up,
        w_down,
    )
    mixed, normed_two_grad = (
        lax.psum_scatter(
            mixed_part.reshape(row_count, seq_len, width), "sp", scatter_dimension=1, tiled=True
        ),
        lax.psum_scatter(
            token_grad_part.reshape(row_count, seq_len, width),
            "sp",
            scatter_dimension=1,
            tiled=True,
        ),
    )
    mixed = mixed.reshape(tokens_dev, width)
    normed_two_grad = normed_two_grad.reshape(tokens_dev, width)
    layer_output = (
        (valid * (resid + mixed)).astype(jnp.bfloat16).reshape(row_count, slot_count, width)
    )
    resid_part, gain_two_grad, bias_two_grad = norm_backward(
        normed_two_grad, unit_two, rstd_two, gain_two
    )
    resid_grad = out_grad.astype(jnp.float32) + resid_part
    branch_grad = resid_grad.astype(jnp.bfloat16)
    row_branch = lax.all_gather(
        branch_grad.reshape(row_count, slot_count, width), "sp", axis=1, tiled=True
    ).reshape(row_count * seq_len, width)
    out_weight_grad = contract_rows(attended_flat, row_branch)
    attended_grad_heads = (
        contract_cols(row_branch, out_rows)
        .astype(jnp.bfloat16)
        .reshape(row_count, seq_len, local_width)
    )

    def backward_row(row_data):
        row_query, row_key, row_value, row_grad, row_totals, row_length = row_data
        query_grad, key_grad, value_grad = attend_backward(
            row_query.reshape(head_shape),
            row_key.reshape(head_shape),
            row_value.reshape(head_shape),
            row_grad.reshape(head_shape),
            row_totals,
            row_length,
            block_rows,
        )
        return (
            query_grad.astype(jnp.bfloat16).reshape(seq_len, local_width),
            key_grad.astype(jnp.bfloat16).reshape(seq_len, local_width),
            value_grad.astype(jnp.bfloat16).reshape(seq_len, local_width),
        )

    query_grads, key_grads, value_grads = lax.map(
        backward_row,
        (query_heads, key_heads, value_heads, attended_grad_heads, log_totals, lengths),
    )
    row_shape = (row_count, seq_len, local_heads, HEAD_DIM)
    query_raw = rotate(query_grads.astype(jnp.float32).reshape(row_shape), cosine, sine, -1.0)
    key_raw = rotate(key_grads.astype(jnp.float32).reshape(row_shape), cosine, sine, -1.0)
    value_raw = value_grads.astype(jnp.float32).reshape(row_shape)
    qkv_grad = (
        jnp.stack([query_raw, key_raw, value_raw], axis=3)
        .reshape(row_count * seq_len, local_cols)
        .astype(jnp.bfloat16)
    )
    bias_local_grad = jnp.sum(qkv_grad.astype(jnp.float32), axis=0)
    qkv_bias_full = lax.dynamic_update_slice(
        jnp.zeros((3 * width,), jnp.float32), bias_local_grad, (sp_index * local_cols,)
    )
    qkv_weight_grad = contract_rows(row_normed, qkv_grad)
    normed_part = contract_cols(qkv_grad, qkv_cols).reshape(row_count, seq_len, width)
    normed_one_grad = (
        lax.psum_scatter(normed_part.astype(jnp.bfloat16), "sp", scatter_dimension=1, tiled=True)
        .astype(jnp.float32)
        .reshape(tokens_dev, width)
    )
    input_part, gain_one_grad, bias_one_grad = norm_backward(
        normed_one_grad, unit_one, rstd_one, gain_one
    )
    input_grad = (resid_grad + input_part).reshape(row_count, slot_count, width)
    small_sums = (
        lax.psum_scatter(gain_one_grad, ("dp", "sp"), scatter_dimension=0, tiled=True),
        lax.psum_scatter(bias_one_grad, ("dp", "sp"), scatter_dimension=0, tiled=True),
        lax.psum_scatter(gain_two_grad, ("dp", "sp"), scatter_dimension=0, tiled=True),
        lax.psum_scatter(bias_two_grad, ("dp", "sp"), scatter_dimension=0, tiled=True),
        lax.psum_scatter(qkv_bias_full, ("dp", "sp"), scatter_dimension=0, tiled=True),
    )
    row_sums = (
        lax.psum_scatter(
            qkv_weight_grad.astype(jnp.bfloat16), "dp", scatter_dimension=0, tiled=True
        ).astype(jnp.float32),
        lax.psum_scatter(
            out_weight_grad.astype(jnp.bfloat16), "dp", scatter_dimension=1, tiled=True
        ).astype(jnp.float32),
        lax.psum_scatter(
            mlp_grads[0].astype(jnp.bfloat16), "dp", scatter_dimension=0, tiled=True
        ).astype(jnp.float32),
        lax.psum_scatter(
            mlp_grads[1].astype(jnp.bfloat16), "dp", scatter_dimension=0, tiled=True
        ).astype(jnp.float32),
        lax.psum_scatter(
            mlp_grads[2].astype(jnp.bfloat16), "dp", scatter_dimension=0, tiled=True
        ).astype(jnp.float32),
    )
    return (
        layer_output,
        input_grad,
        small_sums[0],
        small_sums[1],
        small_sums[2],
        small_sums[3],
        row_sums[0],
        small_sums[4],
        row_sums[1],
        row_sums[2],
        row_sums[3],
        row_sums[4],
    )


def dot_nn(left, right):
    return lax.dot_general(left, right, (((1,), (0,)), ((), ())), preferred_element_type=F32)


def dot_nt(left, right):
    return lax.dot_general(left, right, (((1,), (1,)), ((), ())), preferred_element_type=F32)


def dot_tn(left, right):
    return lax.dot_general(left, right, (((0,), (0,)), ((), ())), preferred_element_type=F32)


def iota(shape, dim):
    return lax.broadcasted_iota(jnp.int32, shape, dim)


def tile(index, size):
    return pl.ds(pl.multiple_of(index * size, size), size)


def normalize(hidden):
    centre = hidden - jnp.mean(hidden, axis=-1, keepdims=True)
    rstd = lax.rsqrt(jnp.mean(centre * centre, axis=-1, keepdims=True) + eps_norm)
    return centre * rstd, rstd


class Plan:
    def __init__(self, dp, sp, slots, width, ff_cols):
        self.dp, self.sp, self.slots, self.width = dp, sp, slots, width
        self.chips = dp // 2
        self.chunk = 2 * slots
        self.tokens = sp * self.chunk
        self.seq = sp * slots
        self.shard = width // dp
        self.head_cols = width // sp // 2
        self.pairs = self.head_cols // 128
        self.qkv_cols = 3 * self.head_cols
        self.ff_cols = ff_cols
        lanes = ff_cols // 128
        self.ff_wide = -(-lanes // 2) * 128
        self.ff_slim = ff_cols - self.ff_wide
        self.count_send = 0
        self.count_recv = 0

    def sems(self, send, recv):
        at = (self.count_send, self.count_recv)
        self.count_send += send
        self.count_recv += recv
        return at


def layer_kernel(plan, sem_at, *refs):
    (
        x_in, cot_in, small_in, cos_in, sin_in, wqkv_in, wout_in, wg_in, wu_in, wd_in,
        out_ref, grad_ref, sums_ref, rg_qkv, rg_out, rg_gate, rg_up, rg_down, n1_hbm,
        ssem, rsem, lsem,
        w_qkv, w_out, w_gate, w_up, w_down,
        buf_a, buf_b, buf_c,
        part, part_x, part_r, mix, mix_x, mix_r,
        q_ref, k_ref, v_ref, att, raw,
        act, dgate, dup, kacc, vacc,
        resid, acc, dres,
        small, vecs, qbias, lens, colsum, biassum, send_sum, recv_sum, z_sum,
        st_qkv, st_out, st_gate, st_up, st_down,
    ) = refs
    sp, dp, slots, width, chunk = plan.sp, plan.dp, plan.slots, plan.width, plan.chunk
    d = lax.axis_index("dp")
    z = lax.axis_index("sp")
    c = d % 2
    oc = 1 - c
    chip = d // 2
    sib = (d + 1 - 2 * c, z)
    first_row = c * slots
    last = sp - 1

    def remote(src, dst, si, ri, dev):
        return pltpu.make_async_remote_copy(
            src_ref=src, dst_ref=dst, send_sem=ssem.at[si], recv_sem=rsem.at[ri],
            device_id=dev, device_id_type=MESH,
        )

    def wait_send(src, si):
        remote(src, src, si, 0, sib).wait_send()

    def wait_recv(dst, ri):
        remote(dst, dst, 0, ri, sib).wait_recv()

    def block(buf, t, core):
        return buf.at[pl.ds(pl.multiple_of(t * chunk + core * slots, slots), slots)]

    def rows_of(buf, t):
        return buf.at[tile(t, chunk)]

    def slot_block(buf, t):
        return buf.at[tile(t, slots)]

    barrier = pltpu.get_barrier_semaphore()
    for i in range(1, dp):
        pl.semaphore_signal(barrier, inc=1, device_id=((d + i) % dp, z), device_id_type=MESH)
    for i in range(1, sp):
        pl.semaphore_signal(barrier, inc=1, device_id=(d, (z + i) % sp), device_id_type=MESH)
    pl.semaphore_wait(barrier, dp + sp - 2)

    class Gather:
        def __init__(self, name, buf):
            self.s, self.r = sem_at[name]
            self.buf = buf

        def start(self, own):
            s, r = self.s, self.r
            dst = block(self.buf, z, c)

            @pl.when(z < last)
            def _():
                remote(own, dst, s, r + z, (d, z + 1)).start()

            @pl.when(z > 0)
            def _():
                remote(own, dst, s + 1, r + z, (d, z - 1)).start()

            remote(own, dst, s + 2 + sp + z, r + sp + z, sib).start()

        def hop(self, k):
            s, r = self.s, self.r
            for sign in (-1, 1):
                t = z + sign * k
                nxt = z - sign
                blk = block(self.buf, t, c)

                @pl.when((t >= 0) & (t <= last))
                def _():
                    wait_recv(blk, r + t)

                    @pl.when((nxt >= 0) & (nxt <= last))
                    def _():
                        remote(blk, blk, s + 2 + t, r + t, (d, nxt)).start()

                    remote(blk, blk, s + 2 + sp + t, r + sp + t, sib).start()

        def need(self, t):
            wait_recv(block(self.buf, t, oc), self.r + sp + t)

        def drain(self, own):
            s = self.s

            @pl.when(z < last)
            def _():
                wait_send(own, s)

            @pl.when(z > 0)
            def _():
                wait_send(own, s + 1)

            for t in range(sp):
                wait_send(own, s + 2 + sp + t)

                @pl.when(((t < z) & (z < last)) | ((t > z) & (z > 0)))
                def _():
                    wait_send(own, s + 2 + t)

    def order(i):
        low = jnp.minimum(z, last - z)
        k = jnp.where(i <= 2 * low, (i + 1) // 2, i - low)
        paired = jnp.where(i % 2 == 1, z - k, z + k)
        single = jnp.where(z < last - z, z + k, z - k)
        return jnp.where(i <= 2 * low, paired, single)

    def add_into(dst, terms):
        @pl.loop(0, slots // 32)
        def _(i):
            sl = tile(i, 32)
            total = dst[sl, :].astype(F32)
            for term in terms:
                total = total + term[sl, :].astype(F32)
            dst[sl, :] = total.astype(dst.dtype)

    class Scatter:
        def __init__(self, name, parts, from_core, from_line):
            self.s, self.r = sem_at[name]
            self.p, self.x, self.l = parts, from_core, from_line

        def core(self, t):
            remote(
                block(self.p, t, oc), slot_block(self.x, t), self.s + t, self.r + t, sib
            ).start()

        def send(self, t, from_end, nbr, slot):
            mine = block(self.p, t, c)
            xs = slot_block(self.x, t)
            wait_recv(xs, self.r + t)

            @pl.when(from_end)
            def _():
                add_into(mine, [xs])

            @pl.when(jnp.logical_not(from_end))
            def _():
                ls = slot_block(self.l, t)
                wait_recv(ls, self.r + sp + t)
                add_into(mine, [xs, ls])

            remote(
                mine, slot_block(self.l, slot), self.s + sp + t, self.r + sp + slot, (d, nbr)
            ).start()

        def step(self, n):
            left = n - (last - z)

            @pl.when((left >= 0) & (left < z))
            def _():
                self.send(left, z == last, z - 1, left)

            right = n - z

            @pl.when((right >= 0) & (right < last - z))
            def _():
                t = last - right
                self.send(t, z == 0, z + 1, jnp.where(t == z + 1, sp, t))

        def final(self, total):
            mine = block(self.p, z, c)
            xs = slot_block(self.x, z)
            wait_recv(xs, self.r + z)

            @pl.loop(0, slots // 32)
            def _(i):
                sl = tile(i, 32)
                total[sl, :] = mine[sl, :].astype(F32) + xs[sl, :].astype(F32)

            @pl.when(z < last)
            def _():
                ls = slot_block(self.l, z)
                wait_recv(ls, self.r + sp + z)
                add_into(total, [ls])

            @pl.when(z > 0)
            def _():
                ls = slot_block(self.l, sp)
                wait_recv(ls, self.r + sp + sp)
                add_into(total, [ls])

        def drain(self):
            for t in range(sp):
                wait_send(slot_block(self.x, t), self.s + t)

                @pl.when(t != z)
                def _():
                    wait_send(slot_block(self.x, t), self.s + sp + t)

    def chip_target(q):
        cx, cy = chip % 2, chip // 2
        if q % 2:
            cx = 1 - cx
        if q // 2:
            cy = 1 - cy
        return 2 * cx + 4 * cy

    def weight_window(name, src, core):
        if name == "out":
            half = plan.head_cols
            return src.at[pl.ds(core * half, half), :]
        if name == "qkv":
            return src.at[:, pl.ds(core * plan.qkv_cols, plan.qkv_cols)]
        return src.at[:, pl.ds(core * plan.ff_wide, plan.ff_slim if core else plan.ff_wide)]

    def weight_place(name, dst, owner, core):
        if name == "out":
            return dst.at[:, tile(owner, plan.shard)]
        if name == "qkv":
            return dst.at[tile(owner, plan.shard), :]
        return dst.at[tile(owner, plan.shard), pl.ds(0, plan.ff_slim if core else plan.ff_wide)]

    def weight_send(name, src, dst):
        s, r = sem_at["w_" + name]
        for q in (1, 2, 0):
            for core in (0, 1):
                target = chip_target(q) + core
                here = weight_window(name, src, core)
                there = weight_place(name, dst, d, core)
                if q:
                    remote(here, there, s + 2 * q + core, r + d, (target, z)).start()
                else:

                    @pl.when(c != core)
                    def _():
                        remote(here, there, s + core, r + d, (target, z)).start()

                    @pl.when(c == core)
                    def _():
                        pltpu.make_async_copy(here, there, lsem.at[WEIGHTS.index(name)]).start()

    def weight_forward(name, dst):
        s, r = sem_at["w_" + name]
        for core in (0, 1):

            @pl.when(c == core)
            def _():
                for k in (0, 1):
                    owner = chip_target(1 if core else 2) + k
                    place = weight_place(name, dst, owner, core)
                    wait_recv(place, r + owner)
                    target = chip_target(2 if core else 1) + core
                    remote(place, place, s + 6 + k, r + owner, (target, z)).start()

    def weight_wait(name, src, dst):
        _, r = sem_at["w_" + name]
        for core in (0, 1):

            @pl.when(c == core)
            def _():
                for q in (0, 2 if core else 1, 3):
                    for k in (0, 1):
                        if q or k != core:
                            owner = chip_target(q) + k
                            wait_recv(weight_place(name, dst, owner, core), r + owner)
                pltpu.make_async_copy(
                    weight_window(name, src, core), weight_place(name, dst, d, core),
                    lsem.at[WEIGHTS.index(name)],
                ).wait()

    def weight_drain(name, src, dst):
        s, _ = sem_at["w_" + name]
        for core in (0, 1):
            here = weight_window(name, src, core)
            wait_send(here, s + 2 + core)
            wait_send(here, s + 4 + core)

            @pl.when(c != core)
            def _():
                wait_send(here, s + core)

            @pl.when(c == core)
            def _():
                place = weight_place(name, dst, d, core)
                wait_send(place, s + 6)
                wait_send(place, s + 7)

    def wgrad_piece(name, src, owner, core):
        if name == "out":
            return src.at[:, tile(owner, plan.shard)]
        if name == "qkv":
            return src.at[tile(owner, plan.shard), :]
        return src.at[tile(owner, plan.shard), pl.ds(0, plan.ff_slim if core else plan.ff_wide)]

    def wgrad_place(name, dst, slot, core):
        if name == "out":
            return dst.at[slot, pl.ds(core * plan.head_cols, plan.head_cols), :]
        if name == "qkv":
            return dst.at[slot, :, pl.ds(core * plan.qkv_cols, plan.qkv_cols)]
        return dst.at[slot, :, pl.ds(core * plan.ff_wide, plan.ff_slim if core else plan.ff_wide)]

    def stage_place(name, stage, k, core):
        if name in ("out", "qkv"):
            return stage.at[k]
        return stage.at[k, :, pl.ds(0, plan.ff_slim if core else plan.ff_wide)]

    def wgrad_send(name, src, dst, stage):
        s, r = sem_at["g_" + name]
        for core in (0, 1):
            near = 1 if core else 2

            @pl.when(c == core)
            def _():
                for k in (0, 1):
                    remote(
                        wgrad_piece(name, src, chip_target(3) + k, core),
                        stage_place(name, stage, k, core),
                        s + k, r + 6 + k, (chip_target(near) + core, z),
                    ).start()
                for k in (0, 1):
                    target = chip_target(near) + k
                    remote(
                        wgrad_piece(name, src, target, core),
                        wgrad_place(name, dst, near, core),
                        s + 2 + k, r + 2 * near + core, (target, z),
                    ).start()
                remote(
                    wgrad_piece(name, src, d + 1 - 2 * core, core),
                    wgrad_place(name, dst, 0, core), s + 4, r + core, sib,
                ).start()
                pltpu.make_async_copy(
                    wgrad_piece(name, src, d, core), wgrad_place(name, dst, 0, core),
                    lsem.at[len(WEIGHTS) + WEIGHTS.index(name)],
                ).start()

    def wgrad_merge(name, src, dst, stage):
        s, r = sem_at["g_" + name]
        for core in (0, 1):
            far = 2 if core else 1

            @pl.when(c == core)
            def _():
                for k in (0, 1):
                    target = chip_target(far) + k
                    came = stage_place(name, stage, k, core)
                    mine = wgrad_piece(name, src, target, core)
                    wait_recv(came, r + 6 + k)

                    @pl.loop(0, came.shape[0] // 32)
                    def _(i):
                        sl = tile(i, 32)
                        mine[sl, :] = (mine[sl, :].astype(F32) + came[sl, :].astype(F32)).astype(BF16)

                    remote(
                        mine, wgrad_place(name, dst, far, core), s + 5 + k, r + 2 * far + core,
                        (target, z),
                    ).start()

    def wgrad_finish(name, src, dst):
        s, r = sem_at["g_" + name]
        for core in (0, 1):

            @pl.when(c == core)
            def _():
                here = wgrad_piece(name, src, d, core)
                for i in range(7):
                    wait_send(here, s + i)
                wait_recv(wgrad_place(name, dst, 0, 1 - core), r + 1 - core)
                for slot in (1, 2):
                    for k in (0, 1):
                        wait_recv(wgrad_place(name, dst, slot, k), r + 2 * slot + k)
                pltpu.make_async_copy(
                    here, wgrad_place(name, dst, 0, core),
                    lsem.at[len(WEIGHTS) + WEIGHTS.index(name)],
                ).wait()

    gather_x = Gather("ag_x", buf_a)
    gather_d = Gather("ag_d", buf_c)
    gather_n = Gather("ag_n", buf_a)
    gather_b = Gather("ag_b", buf_b)
    scatter_o = Scatter("rs_o", part, part_x, part_r)
    scatter_n = Scatter("rs_n", part, part_x, part_r)
    scatter_i = Scatter("rs_i", part, part_x, part_r)
    scatter_m = Scatter("rs_m", mix, mix_x, mix_r)

    sz, rz = sem_at["sm_z"]
    sd, rd = sem_at["sm_d"]
    small[d, z] = small_in[...]
    for i in range(1, sp):
        peer = (z + i) % sp
        remote(small_in, small.at[d, z], sz + i, rz + z, (d, peer)).start()
    gather_x.start(x_in)
    for i in range(1, sp):
        peer = (z + i) % sp
        wait_recv(small.at[d, peer], rz + peer)
    for i in range(1, dp):
        peer = (d + i) % dp
        remote(small.at[d], small.at[d], sd + i, rd + d, (peer, z)).start()
    weight_send("qkv", wqkv_in, w_qkv)
    weight_send("out", wout_in, w_out)

    block(buf_a, z, c)[...] = x_in[...]
    own_len = small_in[7:8, 0:1]

    @pl.loop(0, slots // 32)
    def _(i):
        sl = tile(i, 32)
        pos = (iota((32, 1), 0) + (z * slots + i * 32)).astype(F32)
        keep = jnp.where(pos < own_len, 1.0, 0.0)
        block(buf_c, z, c)[sl, :] = (cot_in[sl, :].astype(F32) * keep).astype(BF16)

    @pl.when(c == 1)
    def _():
        pad = plan.ff_wide - plan.ff_slim
        for ref in (w_gate, w_up, w_down):
            ref[:, plan.ff_slim :] = jnp.zeros((width, pad), BF16)

    for i in range(1, dp):
        peer = (d + i) % dp
        wait_recv(small.at[peer], rd + peer)
    per_dp = width // dp // 128
    for i in range(dp):
        for h in range(per_dp):
            at = (i * per_dp + h) * 128
            vecs[:, at : at + 128] = small[i, 2 * h] + small[i, 2 * h + 1]
    bias_at = 2 * z + c
    for h in range(sp // 2):
        for k in range(3):
            at = h * 384 + k * 128
            qbias[0:1, at : at + 128] = (
                small[bias_at, 2 * h, 4 + k : 5 + k, :] + small[bias_at, 2 * h + 1, 4 + k : 5 + k, :]
            )
    for r in range(2):
        lens[r : r + 1, :] = small[2 * chip + r, 0, 7:8, :]

    n1 = buf_b
    gain_one, bias_one = vecs[0:1, :], vecs[1:2, :]

    @pl.loop(0, sp)
    def _(i):
        @pl.when(i > 0)
        def _():
            gather_x.hop(i)

        @pl.when(i == last - 1)
        def _():
            weight_forward("qkv", w_qkv)

        t = order(i)
        gather_x.need(t)
        src, dst = rows_of(buf_a, t), rows_of(n1, t)

        @pl.loop(0, chunk // 32)
        def _(j):
            sl = tile(j, 32)
            unit, _ = normalize(src[sl, :].astype(F32))
            dst[sl, :] = (unit * vecs[0:1, :] + vecs[1:2, :]).astype(BF16)

    gather_d.start(block(buf_c, z, c))
    n1_copy = pltpu.make_async_copy(n1, n1_hbm, lsem.at[2 * len(WEIGHTS)])
    n1_copy.start()

    weight_forward("out", w_out)
    weight_send("gate", wg_in, w_gate)
    weight_send("up", wu_in, w_up)
    weight_wait("qkv", wqkv_in, w_qkv)
    low = iota((1, 128), 1) < 64
    first_half = iota((1, 128), 1) % 64 < ROT // 2

    def rotated(v, cosine, sine):
        swapped = jnp.where(
            first_half, pltpu.roll(v, 128 - ROT // 2, 1), pltpu.roll(v, ROT // 2, 1)
        )
        return v * cosine + swapped * sine

    @pl.loop(0, sp)
    def _(t):
        src = rows_of(n1, t)

        @pl.loop(0, plan.qkv_cols // 256)
        def _(n):
            sl = tile(n, 256)
            raw[:, sl] = dot_nn(src[...], w_qkv[:, sl]) + qbias[0:1, sl]

        here = tile(t, slots)
        cosine, sine = cos_in[here, :], sin_in[here, :]
        for r in range(2):
            rs = slice(r * slots, (r + 1) * slots)
            for p in range(plan.pairs):
                v0 = raw[rs, p * 384 : p * 384 + 128]
                v1 = raw[rs, p * 384 + 128 : p * 384 + 256]
                v2 = raw[rs, p * 384 + 256 : p * 384 + 384]
                r0 = rotated(v0, cosine, sine)
                r1 = rotated(v1, cosine, sine)
                r2 = rotated(v2, cosine, sine)
                q_ref[r, p, here, :] = jnp.where(low, r0, r1).astype(BF16)
                k_ref[r, p, here, :] = pltpu.roll(jnp.where(low, r2, r0), 64, 1).astype(BF16)
                v_ref[r, p, here, :] = jnp.where(low, v1, v2).astype(BF16)

    q_rows = min(256, plan.seq)
    q_blocks = plan.seq // q_rows
    per_q = q_rows // slots
    scale = HEAD_DIM ** (-0.5)

    def weights_of(r, p, h, qb):
        keys_to = (qb + 1) * q_rows
        mask = low if h == 0 else jnp.logical_not(low)
        qh = jnp.where(mask, q_ref[r, p, qb * q_rows : keys_to, :], 0).astype(BF16)
        scores = dot_nt(k_ref[r, p, 0:keys_to, :], qh) * scale
        key_pos = iota((keys_to, q_rows), 0)
        query_pos = iota((keys_to, q_rows), 1) + qb * q_rows
        length = lens[pl.ds(r, 1), 0:1]
        allowed = (key_pos <= query_pos) & (key_pos.astype(F32) < length)
        scores = jnp.where(allowed, scores, neg_large)
        expo = jnp.exp(scores - jnp.max(scores, axis=0, keepdims=True))
        return expo * (1.0 / jnp.sum(expo, axis=0, keepdims=True))

    def att_rows(r, t):
        return pl.ds(pl.multiple_of(t * chunk + r * slots, slots), slots)

    def attention(r, p):
        for qb in range(q_blocks):
            outs = []
            for h in range(2):
                probs = weights_of(r, p, h, qb).astype(BF16)
                outs.append(dot_tn(probs, v_ref[r, p, 0 : (qb + 1) * q_rows, :]))
            both = jnp.where(low, outs[0], outs[1]).astype(BF16)
            for i in range(per_q):
                att[att_rows(r, qb * per_q + i), p * 128 : (p + 1) * 128] = both[
                    i * slots : (i + 1) * slots
                ]

    @pl.loop(0, 2)
    def _(r):
        for p in range(plan.pairs):
            attention(r, p)

    gather_d.hop(1)
    gather_x.drain(x_in)

    weight_forward("gate", w_gate)
    weight_send("down", wd_in, w_down)
    weight_wait("out", wout_in, w_out)

    def far_first(i):
        return jnp.where(z < last - z, last - i, i)

    @pl.loop(0, sp)
    def _(i):
        t = far_first(i)
        src, dst = rows_of(att, t), rows_of(part, t)

        @pl.loop(0, width // 256)
        def _(n):
            sl = tile(n, 256)
            dst[:, sl] = dot_nn(src[...], w_out[:, sl]).astype(BF16)

        scatter_o.core(t)

    scatter_o.step(0)
    weight_forward("up", w_up)
    for k in range(1, sp - 1):
        scatter_o.step(k)
        gather_d.hop(k + 1)
    weight_forward("down", w_down)
    scatter_o.final(acc)

    own_n = block(buf_a, z, c)

    @pl.loop(0, slots // 32)
    def _(i):
        sl = tile(i, 32)
        hidden = x_in[sl, :].astype(F32) + acc[sl, :]
        resid[sl, :] = hidden
        unit, _ = normalize(hidden)
        own_n[sl, :] = (unit * vecs[2:3, :] + vecs[3:4, :]).astype(BF16)

    gather_n.start(own_n)
    for i in range(sp):
        gather_d.need(i)
    scatter_o.drain()
    n1_copy.wait()

    weight_wait("gate", wg_in, w_gate)
    weight_wait("up", wu_in, w_up)
    weight_wait("down", wd_in, w_down)

    @pl.loop(0, sp)
    def _(i):
        @pl.when(i > 0)
        def _():
            gather_n.hop(i)

        t = order(i)
        gather_n.need(t)
        tok, gout = rows_of(buf_a, t), rows_of(buf_c, t)
        act_t, dg_t, du_t = rows_of(act, t), rows_of(dgate, t), rows_of(dup, t)
        part_t, mix_t = rows_of(part, t), rows_of(mix, t)

        @pl.loop(0, plan.ff_wide // 256)
        def _(n):
            sl = tile(n, 256)
            gate = dot_nn(tok[...], w_gate[:, sl])
            up = dot_nn(tok[...], w_up[:, sl])
            d_act = dot_nn(gout[...], w_down[:, sl])
            sig = jax.nn.sigmoid(gate)
            silu = gate * sig
            act_t[:, sl] = (silu * up).astype(BF16)
            du_t[:, sl] = (d_act * silu).astype(BF16)
            dg_t[:, sl] = (d_act * up * sig * (1.0 + gate * (1.0 - sig))).astype(BF16)

        @pl.loop(0, width // 256)
        def _(n):
            sl = tile(n, 256)
            part_t[:, sl] = (
                dot_nt(dg_t[...], w_gate[sl, :]) + dot_nt(du_t[...], w_up[sl, :])
            ).astype(BF16)
            mix_t[:, sl] = dot_nt(act_t[...], w_down[sl, :]).astype(BF16)

        scatter_n.core(t)
        scatter_m.core(t)

    def wgrad(tokens, cols, dst):
        @pl.loop(0, width // 256)
        def _(n):
            sl = tile(n, 256)
            dst[sl, :] = dot_tn(tokens[:, sl], cols[...]).astype(BF16)

    scatter_n.step(0)
    weight_drain("down", wd_in, w_down)
    weight_drain("gate", wg_in, w_gate)
    weight_drain("up", wu_in, w_up)
    wgrad(buf_c, act, w_down)
    wgrad_send("down", w_down, rg_down, st_down)
    scatter_n.step(1)
    wgrad(buf_a, dgate, w_gate)
    wgrad_send("gate", w_gate, rg_gate, st_gate)
    for k in range(2, sp - 1):
        scatter_n.step(k)
    wgrad(buf_a, dup, w_up)
    wgrad_send("up", w_up, rg_up, st_up)
    scatter_n.final(acc)

    gather_n.drain(own_n)
    n1_back = pltpu.make_async_copy(n1_hbm, buf_a, lsem.at[2 * len(WEIGHTS) + 1])
    n1_back.start()
    colsum[...] = jnp.zeros_like(colsum)
    own_d, own_b = block(buf_c, z, c), block(buf_b, z, c)

    def norm_back(grad, hidden, gain, row):
        unit, rstd = normalize(hidden)
        colsum[row : row + 1, :] += jnp.sum(grad * unit, axis=0, keepdims=True)
        colsum[row + 1 : row + 2, :] += jnp.sum(grad, axis=0, keepdims=True)
        scaled = grad * gain
        return rstd * (
            scaled
            - jnp.mean(scaled, axis=-1, keepdims=True)
            - unit * jnp.mean(scaled * unit, axis=-1, keepdims=True)
        )

    @pl.loop(0, slots // 32)
    def _(i):
        sl = tile(i, 32)
        back = own_d[sl, :].astype(F32) + norm_back(acc[sl, :], resid[sl, :], vecs[2:3, :], 2)
        dres[sl, :] = back
        own_b[sl, :] = back.astype(BF16)

    gather_b.start(own_b)
    datt = dgate.at[:, pl.ds(0, plan.head_cols)]
    dqkv = act.at[:, pl.ds(0, plan.qkv_cols)]
    scatter_n.drain()
    scatter_m.step(0)
    wgrad_merge("down", w_down, rg_down, st_down)

    @pl.loop(0, sp)
    def _(i):
        @pl.when(i > 0)
        def _():
            gather_b.hop(i)

        @pl.when((i > 0) & (i < last))
        def _():
            scatter_m.step(i)

        t = order(i)
        gather_b.need(t)
        datt[tile(t, chunk), :] = dot_nt(rows_of(buf_b, t)[...], w_out[...]).astype(BF16)

    wgrad_merge("gate", w_gate, rg_gate, st_gate)

    biassum[...] = jnp.zeros_like(biassum)

    def attention_back(r, p):
        cols = slice(p * 128, (p + 1) * 128)
        for qb in range(q_blocks):
            keys_to = (qb + 1) * q_rows
            dav = jnp.concatenate(
                [datt[att_rows(r, qb * per_q + i), cols] for i in range(per_q)], axis=0
            )
            qv = q_ref[r, p, qb * q_rows : keys_to, :]
            dq, dk, dv = [], [], []
            for h in range(2):
                mask = low if h == 0 else jnp.logical_not(low)
                probs = weights_of(r, p, h, qb)
                dprobs = dot_nt(v_ref[r, p, 0:keys_to, :], jnp.where(mask, dav, 0).astype(BF16))
                delta = jnp.sum(dprobs * probs, axis=0, keepdims=True)
                dscores = (probs * (dprobs - delta)).astype(BF16)
                dv.append(dot_nn(probs.astype(BF16), dav))
                dk.append(dot_nn(dscores, qv))
                dq.append(dot_tn(dscores, k_ref[r, p, 0:keys_to, :]))
            dq_both = (jnp.where(low, dq[0], dq[1]) * scale).astype(BF16)
            dk_both = jnp.where(low, dk[0], dk[1])
            dv_both = jnp.where(low, dv[0], dv[1])
            if qb == 0:
                kacc[0:keys_to, :] = dk_both
                vacc[0:keys_to, :] = dv_both
            else:
                kept = keys_to - q_rows
                kacc[0:kept, :] += dk_both[0:kept]
                vacc[0:kept, :] += dv_both[0:kept]
                kacc[kept:keys_to, :] = dk_both[kept:keys_to]
                vacc[kept:keys_to, :] = dv_both[kept:keys_to]
            q_ref[r, p, qb * q_rows : keys_to, :] = dq_both
        for t in range(sp):
            ts = slice(t * slots, (t + 1) * slots)
            dqv = q_ref[r, p, ts, :].astype(F32)
            dkv = (kacc[ts, :] * scale).astype(BF16).astype(F32)
            dvv = vacc[ts, :].astype(BF16).astype(F32)
            swapped = pltpu.roll(dkv, 64, 1)
            cosine, sine = cos_in[ts, :], -sin_in[ts, :]
            g0 = rotated(jnp.where(low, dqv, swapped), cosine, sine)
            g1 = jnp.where(low, dvv, rotated(dqv, cosine, sine))
            g2 = jnp.where(low, rotated(swapped, cosine, sine), dvv)
            for k, g in enumerate((g0, g1, g2)):
                g = g.astype(BF16)
                dqkv[att_rows(r, t), p * 384 + k * 128 : p * 384 + (k + 1) * 128] = g
                row = 3 * p + k
                biassum[row : row + 1, :] += jnp.sum(g.astype(F32), axis=0, keepdims=True)

    @pl.loop(0, 2)
    def _(r):
        for p in range(plan.pairs):
            attention_back(r, p)

    wgrad_merge("up", w_up, rg_up, st_up)

    @pl.loop(0, sp)
    def _(i):
        t = far_first(i)
        dst, src = rows_of(part, t), rows_of(dqkv, t)

        @pl.loop(0, width // 256)
        def _(n):
            sl = tile(n, 256)
            dst[:, sl] = dot_nt(src[...], w_qkv[sl, :]).astype(BF16)

        scatter_i.core(t)

    scatter_i.step(0)
    weight_drain("qkv", wqkv_in, w_qkv)
    weight_drain("out", wout_in, w_out)
    n1_back.wait()
    wgrad(buf_a, dqkv, w_qkv)
    wgrad_send("qkv", w_qkv, rg_qkv, st_qkv)
    scatter_i.step(1)

    @pl.loop(0, width // 256)
    def _(n):
        sl = tile(n, 256)
        w_out[:, sl] = dot_tn(att[...], buf_b[:, sl]).astype(BF16)

    wgrad_send("out", w_out, rg_out, st_out)
    for k in range(2, sp - 1):
        scatter_i.step(k)
    wgrad_merge("qkv", w_qkv, rg_qkv, st_qkv)
    scatter_m.final(acc)

    @pl.loop(0, slots // 32)
    def _(i):
        sl = tile(i, 32)
        pos = (iota((32, 1), 0) + (z * slots + i * 32)).astype(F32)
        keep = jnp.where(pos < small_in[7:8, 0:1], 1.0, 0.0)
        out_ref[sl, :] = (keep * (resid[sl, :] + acc[sl, :])).astype(BF16)

    wgrad_merge("out", w_out, rg_out, st_out)
    scatter_i.final(acc)

    @pl.loop(0, slots // 32)
    def _(i):
        sl = tile(i, 32)
        back = norm_back(acc[sl, :], x_in[sl, :].astype(F32), vecs[0:1, :], 0)
        grad_ref[sl, :] = dres[sl, :] + back

    per = plan.shard
    for i in range(dp):
        send_sum[i, :, 0:per] = colsum[:, i * per : (i + 1) * per]
        send_sum[i, :, per : per + 128] = biassum[...]
    sa, ra = sem_at["su_d"]
    sb, rb = sem_at["su_z"]
    recv_sum[d] = send_sum[d]
    for i in range(1, dp):
        peer = (d + i) % dp
        remote(send_sum.at[peer], recv_sum.at[d], sa + i, ra + d, (peer, z)).start()
    for i in range(1, dp):
        peer = (d + i) % dp
        wait_recv(recv_sum.at[peer], ra + peer)
    norm_total = recv_sum[0, :, 0:per]
    for i in range(1, dp):
        norm_total = norm_total + recv_sum[i, :, 0:per]
    bias_total = recv_sum[c, :, per : per + 128]
    for i in range(1, dp // 2):
        bias_total = bias_total + recv_sum[2 * i + c, :, per : per + 128]
    z_sum[z, :, 0:per] = norm_total
    z_sum[z, :, per : per + 128] = bias_total
    for i in range(1, sp):
        peer = (z + i) % sp
        remote(z_sum.at[z], z_sum.at[z], sb + i, rb + z, (d, peer)).start()
    for i in range(1, sp):
        peer = (z + i) % sp
        wait_recv(z_sum.at[peer], rb + peer)
    norm_total = z_sum[0, :, 0:per]
    for i in range(1, sp):
        norm_total = norm_total + z_sum[i, :, 0:per]
    sums_ref[:, 0:per] = norm_total
    sums_ref[:, per : per + 128] = z_sum[chip, :, per : per + 128]

    for name, src, dst in (
        ("down", w_down, rg_down), ("gate", w_gate, rg_gate), ("up", w_up, rg_up),
        ("qkv", w_qkv, rg_qkv), ("out", w_out, rg_out),
    ):
        wgrad_finish(name, src, dst)
    gather_d.drain(own_d)
    gather_b.drain(own_b)
    scatter_m.drain()
    scatter_i.drain()
    for i in range(1, sp):
        wait_send(small_in, sz + i)
        wait_send(z_sum.at[z], sb + i)
    for i in range(1, dp):
        wait_send(small.at[d], sd + i)
        wait_send(send_sum.at[0], sa + i)


WEIGHTS = ("qkv", "out", "gate", "up", "down")


def rotary_lanes(seq_len):
    half = ROT // 2
    freq = theta ** (-(np.arange(half, dtype=np.float32) * np.float32(2.0)) / np.float32(ROT))
    angles = np.arange(seq_len, dtype=np.float32)[:, None] * freq.astype(np.float32)[None, :]
    cosine, sine = np.cos(angles), np.sin(angles)
    cos_head = np.ones((seq_len, HEAD_DIM), np.float32)
    sin_head = np.zeros((seq_len, HEAD_DIM), np.float32)
    cos_head[:, :half], cos_head[:, half:ROT] = cosine, cosine
    sin_head[:, :half], sin_head[:, half:ROT] = -sine, sine
    return np.tile(cos_head, (1, 2)), np.tile(sin_head, (1, 2))


def per_device_fast(
    layer_input, lengths, cotangent, ln1_gain, ln1_bias, ln2_gain, ln2_bias,
    qkv_weight, qkv_bias, out_weight, gate_weight, up_weight, down_weight,
):
    dp, sp = lax.axis_size("dp"), lax.axis_size("sp")
    z = lax.axis_index("sp")
    _, slots, width = layer_input.shape
    plan = Plan(dp, sp, slots, width, gate_weight.shape[1])
    sem_at = {}
    for name in WEIGHTS:
        sem_at["w_" + name] = plan.sems(8, dp)
        sem_at["g_" + name] = plan.sems(7, 8)
    for name in ("ag_x", "ag_d", "ag_n", "ag_b"):
        sem_at[name] = plan.sems(2 + 2 * sp, 2 * sp)
    for name in ("rs_o", "rs_n", "rs_i", "rs_m"):
        sem_at[name] = plan.sems(2 * sp, 2 * sp + 1)
    for name in ("sm_z", "su_z"):
        sem_at[name] = plan.sems(sp, sp)
    for name in ("sm_d", "su_d"):
        sem_at[name] = plan.sems(dp, dp)

    even = z % 2 == 0
    norms = jnp.stack([ln1_gain, ln1_bias, ln2_gain, ln2_bias]).astype(F32)
    none = jnp.zeros_like(norms)
    norm_rows = jnp.where(
        even, jnp.concatenate([norms, none], 1), jnp.concatenate([none, norms], 1)
    )
    bias = qkv_bias.astype(F32)
    none = jnp.zeros_like(bias)
    bias_rows = jnp.where(
        even, jnp.concatenate([bias, none]), jnp.concatenate([none, bias])
    ).reshape(3, 128)
    len_row = jnp.broadcast_to(lengths.astype(F32)[:, None], (1, 128))
    small = jnp.concatenate([norm_rows, bias_rows, len_row], axis=0)
    cosine, sine = rotary_lanes(sp * slots)

    vmem = pl.BlockSpec(memory_space=pltpu.VMEM)
    hbm = pl.BlockSpec(memory_space=pl.ANY)
    out_shape = [
        jax.ShapeDtypeStruct((slots, width), BF16),
        jax.ShapeDtypeStruct((slots, width), F32),
        jax.ShapeDtypeStruct((8, plan.shard + 128), F32),
        jax.ShapeDtypeStruct((3,) + qkv_weight.shape, BF16),
        jax.ShapeDtypeStruct((3,) + out_weight.shape, BF16),
        jax.ShapeDtypeStruct((3,) + gate_weight.shape, BF16),
        jax.ShapeDtypeStruct((3,) + up_weight.shape, BF16),
        jax.ShapeDtypeStruct((3,) + down_weight.shape, BF16),
        jax.ShapeDtypeStruct((plan.tokens, width), BF16),
    ]
    tokens, heads, ff = plan.tokens, plan.head_cols, plan.ff_wide
    scratch = [
        pltpu.SemaphoreType.DMA((plan.count_send,)),
        pltpu.SemaphoreType.DMA((plan.count_recv,)),
        pltpu.SemaphoreType.DMA((2 * len(WEIGHTS) + 2,)),
        pltpu.VMEM((width, plan.qkv_cols), BF16),
        pltpu.VMEM((heads, width), BF16),
        pltpu.VMEM((width, ff), BF16),
        pltpu.VMEM((width, ff), BF16),
        pltpu.VMEM((width, ff), BF16),
        pltpu.VMEM((tokens, width), BF16),
        pltpu.VMEM((tokens, width), BF16),
        pltpu.VMEM((tokens, width), BF16),
        pltpu.VMEM((tokens, width), BF16),
        pltpu.VMEM((sp * slots, width), BF16),
        pltpu.VMEM(((sp + 1) * slots, width), BF16),
        pltpu.VMEM((tokens, width), BF16),
        pltpu.VMEM((sp * slots, width), BF16),
        pltpu.VMEM(((sp + 1) * slots, width), BF16),
        pltpu.VMEM((2, plan.pairs, plan.seq, 128), BF16),
        pltpu.VMEM((2, plan.pairs, plan.seq, 128), BF16),
        pltpu.VMEM((2, plan.pairs, plan.seq, 128), BF16),
        pltpu.VMEM((tokens, heads), BF16),
        pltpu.VMEM((plan.chunk, plan.qkv_cols), F32),
        pltpu.VMEM((tokens, ff), BF16),
        pltpu.VMEM((tokens, ff), BF16),
        pltpu.VMEM((tokens, ff), BF16),
        pltpu.VMEM((plan.seq, 128), F32),
        pltpu.VMEM((plan.seq, 128), F32),
        pltpu.VMEM((slots, width), F32),
        pltpu.VMEM((slots, width), F32),
        pltpu.VMEM((slots, width), F32),
        pltpu.VMEM((dp, sp, 8, 128), F32),
        pltpu.VMEM((8, width), F32),
        pltpu.VMEM((8, plan.qkv_cols), F32),
        pltpu.VMEM((8, 128), F32),
        pltpu.VMEM((8, width), F32),
        pltpu.VMEM((8, 128), F32),
        pltpu.VMEM((dp, 8, plan.shard + 128), F32),
        pltpu.VMEM((dp, 8, plan.shard + 128), F32),
        pltpu.VMEM((sp, 8, plan.shard + 128), F32),
        pltpu.VMEM((2, plan.shard, plan.qkv_cols), BF16),
        pltpu.VMEM((2, heads, plan.shard), BF16),
        pltpu.VMEM((2, plan.shard, ff), BF16),
        pltpu.VMEM((2, plan.shard, ff), BF16),
        pltpu.VMEM((2, plan.shard, ff), BF16),
    ]
    outs = pl.pallas_call(
        functools.partial(layer_kernel, plan, sem_at),
        out_shape=out_shape,
        in_specs=[vmem] * 5 + [hbm] * 5,
        out_specs=[vmem] * 3 + [hbm] * 6,
        scratch_shapes=scratch,
        compiler_params=pltpu.CompilerParams(
            collective_id=0, has_side_effects=True, vmem_limit_bytes=63 * 1024 * 1024
        ),
    )(
        layer_input[0], cotangent[0], small, jnp.asarray(cosine), jnp.asarray(sine),
        qkv_weight, out_weight, gate_weight, up_weight, down_weight,
    )
    sums = outs[2]
    own = lax.dynamic_slice_in_dim(sums[:4, : plan.shard], z * (plan.shard // sp), plan.shard // sp, 1)
    bias_grad = lax.dynamic_slice_in_dim(
        sums[:, plan.shard :].reshape(-1), z * qkv_bias.shape[0], qkv_bias.shape[0]
    )
    grads = [jnp.sum(g.astype(F32), axis=0) for g in outs[3:8]]
    return (
        outs[0][None], outs[1][None], own[0], own[1], own[2], own[3],
        grads[0], bias_grad, grads[1], grads[2], grads[3], grads[4],
    )


def solution(mesh):
    placed = (
        P("dp", "sp", None),
        P("dp"),
        P("dp", "sp", None),
        P(("dp", "sp")),
        P(("dp", "sp")),
        P(("dp", "sp")),
        P(("dp", "sp")),
        P("dp", "sp"),
        P(("dp", "sp")),
        P("sp", "dp"),
        P("dp", "sp"),
        P("dp", "sp"),
        P("dp", "sp"),
    )
    fast = mesh.shape["dp"] == 8 and mesh.shape["sp"] == 4
    return jax.shard_map(
        per_device_fast if fast else per_device,
        mesh=mesh,
        in_specs=placed,
        out_specs=(
            P("dp", "sp", None),
            P("dp", "sp", None),
            P(("dp", "sp")),
            P(("dp", "sp")),
            P(("dp", "sp")),
            P(("dp", "sp")),
            P("dp", "sp"),
            P(("dp", "sp")),
            P("sp", "dp"),
            P("dp", "sp"),
            P("dp", "sp"),
            P("dp", "sp"),
        ),
        check_vma=False,
    )
```

```python
import functools

import jax
import jax.numpy as jnp
import numpy as np
from jax import lax
from jax.experimental import pallas as pl
from jax.experimental.pallas import tpu as pltpu
from jax.sharding import PartitionSpec as P

HEAD_DIM = 64
ROT = 16
F32 = jnp.float32
BF16 = jnp.bfloat16
MESH = pl.DeviceIdType.MESH


eps_norm = 1e-05
theta = 10000.0
neg_large = -1e30


def norm_forward(hidden, gain, bias):
    centre = hidden - jnp.mean(hidden, axis=-1, keepdims=True)
    rstd = lax.rsqrt(jnp.mean(centre * centre, axis=-1, keepdims=True) + eps_norm)
    normed = centre * rstd
    return (normed * gain + bias, normed, rstd)


def norm_backward(grad, normed, rstd, gain):
    gain_grad = jnp.sum(grad * normed, axis=0)
    bias_grad = jnp.sum(grad, axis=0)
    scaled = grad * gain
    input_part = rstd * (
        scaled
        - jnp.mean(scaled, axis=-1, keepdims=True)
        - normed * jnp.mean(scaled * normed, axis=-1, keepdims=True)
    )
    return (input_part, gain_grad, bias_grad)


def rotate(tensor, cosine, sine, direction):
    half_rot = ROT // 2
    first = tensor[..., :half_rot]
    second = tensor[..., half_rot:ROT]
    cos_part = cosine[None, :, None, :]
    sin_part = sine[None, :, None, :] * direction
    return jnp.concatenate(
        [
            first * cos_part - second * sin_part,
            second * cos_part + first * sin_part,
            tensor[..., ROT:],
        ],
        axis=-1,
    )


def rotary_tables(position_list):
    freq = theta ** (-(jnp.arange(ROT // 2, dtype=jnp.float32) * 2.0) / ROT)
    angles = position_list.astype(jnp.float32)[:, None] * freq[None, :]
    return (jnp.cos(angles), jnp.sin(angles))


def contract_rows(left, right):
    return lax.dot_general(
        left, right, (((0,), (0,)), ((), ())), preferred_element_type=jnp.float32
    )


def contract_cols(left, right):
    return lax.dot_general(
        left, right, (((1,), (1,)), ((), ())), preferred_element_type=jnp.float32
    )


def block_scores(query_block, keys, first_row, length, block_rows):
    softmax_scale = HEAD_DIM ** (-0.5)
    key_pos = jnp.arange(keys.shape[0], dtype=jnp.int32)
    query_pos = first_row + jnp.arange(block_rows, dtype=jnp.int32)
    scores = (
        jnp.einsum("qhd,khd->hqk", query_block, keys, preferred_element_type=jnp.float32)
        * softmax_scale
    )
    allowed = (key_pos[None, :] <= query_pos[:, None]) & (key_pos < length)[None, :]
    return jnp.where(allowed[None], scores, neg_large)


def attend_forward(queries, keys, values, length, block_rows):

    def one_block(block_index):
        first_row = block_index * block_rows
        query_block = lax.dynamic_slice_in_dim(queries, first_row, block_rows, 0)
        scores = block_scores(query_block, keys, first_row, length, block_rows)
        top_score = jnp.max(scores, axis=-1, keepdims=True)
        total = jnp.sum(jnp.exp(scores - top_score), axis=-1, keepdims=True)
        log_total = top_score + jnp.log(total)
        attn_weights = jnp.exp(scores - log_total).astype(jnp.bfloat16)
        result = jnp.einsum(
            "hqk,khd->qhd", attn_weights, values, preferred_element_type=jnp.float32
        )
        return (result.astype(jnp.bfloat16), log_total[..., 0])

    results, log_totals = lax.map(
        one_block, jnp.arange(queries.shape[0] // block_rows, dtype=jnp.int32)
    )
    return (results.reshape(queries.shape), log_totals)


def attend_backward(queries, keys, values, grad_out, log_totals, length, block_rows):
    softmax_scale = HEAD_DIM ** (-0.5)

    def one_block(carry, block_index):
        key_grad, value_grad = carry
        first_row = block_index * block_rows
        query_block = lax.dynamic_slice_in_dim(queries, first_row, block_rows, 0)
        grad_block = lax.dynamic_slice_in_dim(grad_out, first_row, block_rows, 0)
        scores = block_scores(query_block, keys, first_row, length, block_rows)
        weights_full = jnp.exp(scores - log_totals[block_index][..., None])
        attn_weights = weights_full.astype(jnp.bfloat16)
        weight_grad = jnp.einsum(
            "qhd,khd->hqk", grad_block, values, preferred_element_type=jnp.float32
        )
        delta = jnp.sum(weight_grad * weights_full, axis=-1, keepdims=True)
        score_grad = (weights_full * (weight_grad - delta)).astype(jnp.bfloat16)
        query_grad = (
            jnp.einsum("hqk,khd->qhd", score_grad, keys, preferred_element_type=jnp.float32)
            * softmax_scale
        )
        key_grad = (
            key_grad
            + jnp.einsum(
                "hqk,qhd->khd", score_grad, query_block, preferred_element_type=jnp.float32
            )
            * softmax_scale
        )
        value_grad = value_grad + jnp.einsum(
            "hqk,qhd->khd", attn_weights, grad_block, preferred_element_type=jnp.float32
        )
        return ((key_grad, value_grad), query_grad)

    zeros = jnp.zeros(keys.shape, jnp.float32)
    (key_grad, value_grad), query_grad = lax.scan(
        one_block, (zeros, zeros), jnp.arange(queries.shape[0] // block_rows, dtype=jnp.int32)
    )
    return (query_grad.reshape(queries.shape), key_grad, value_grad)


def feed_forward(tokens, grads_out, w_gate, w_up, w_down):
    gate = jnp.dot(tokens, w_gate, preferred_element_type=jnp.float32)
    up_proj = jnp.dot(tokens, w_up, preferred_element_type=jnp.float32)
    sigmoid_gate = jax.nn.sigmoid(gate)
    silu_gate = gate * sigmoid_gate
    hidden_act = (silu_gate * up_proj).astype(jnp.bfloat16)
    mixed = contract_cols(hidden_act, w_down)
    act_grad = jnp.dot(grads_out, w_down, preferred_element_type=jnp.float32)
    up_grad = (act_grad * silu_gate).astype(jnp.bfloat16)
    gate_grad = (act_grad * up_proj * sigmoid_gate * (1.0 + gate * (1.0 - sigmoid_gate))).astype(
        jnp.bfloat16
    )
    token_grad = contract_cols(gate_grad, w_gate) + contract_cols(up_grad, w_up)
    weight_grads = (
        contract_rows(tokens, gate_grad),
        contract_rows(tokens, up_grad),
        contract_rows(grads_out, hidden_act),
    )
    return (mixed, token_grad, weight_grads)


def per_device(
    layer_input,
    lengths,
    cotangent,
    ln1_gain,
    ln1_bias,
    ln2_gain,
    ln2_bias,
    qkv_weight,
    qkv_bias,
    out_weight,
    gate_weight,
    up_weight,
    down_weight,
):
    row_count, slot_count, width = layer_input.shape
    sp_count = lax.axis_size("sp")
    sp_index = lax.axis_index("sp")
    tokens_dev = row_count * slot_count
    seq_len = slot_count * sp_count
    block_rows = min(512, seq_len)
    local_width = width // sp_count
    local_heads = local_width // HEAD_DIM
    local_cols = 3 * local_width
    positions = sp_index * slot_count + jnp.arange(slot_count, dtype=jnp.int32)
    valid = (positions[None, :] < lengths[:, None]).astype(jnp.float32).reshape(tokens_dev, 1)
    small = (
        lax.all_gather(ln1_gain, ("dp", "sp"), axis=0, tiled=True),
        lax.all_gather(ln1_bias, ("dp", "sp"), axis=0, tiled=True),
        lax.all_gather(ln2_gain, ("dp", "sp"), axis=0, tiled=True),
        lax.all_gather(ln2_bias, ("dp", "sp"), axis=0, tiled=True),
        lax.all_gather(qkv_bias, ("dp", "sp"), axis=0, tiled=True),
    )
    gain_one = small[0].astype(jnp.float32)
    bias_one = small[1].astype(jnp.float32)
    gain_two = small[2].astype(jnp.float32)
    bias_two = small[3].astype(jnp.float32)
    b_qkv = small[4].astype(jnp.float32)
    qkv_cols, out_rows, gate_cols, up_cols, down_cols = (
        lax.all_gather(qkv_weight, "dp", axis=0, tiled=True),
        lax.all_gather(out_weight, "dp", axis=1, tiled=True),
        lax.all_gather(gate_weight, "dp", axis=0, tiled=True),
        lax.all_gather(up_weight, "dp", axis=0, tiled=True),
        lax.all_gather(down_weight, "dp", axis=0, tiled=True),
    )
    w_gate, w_up, w_down = (gate_cols, up_cols, down_cols)
    hidden_in = layer_input.astype(jnp.float32).reshape(tokens_dev, width)
    normed_one, unit_one, rstd_one = norm_forward(hidden_in, gain_one, bias_one)
    normed_one = normed_one.astype(jnp.bfloat16)
    cosine, sine = rotary_tables(jnp.arange(seq_len, dtype=jnp.int32))
    row_normed = lax.all_gather(
        normed_one.reshape(row_count, slot_count, width), "sp", axis=1, tiled=True
    ).reshape(row_count * seq_len, width)
    bias_local = lax.dynamic_slice_in_dim(b_qkv, sp_index * local_cols, local_cols)
    qkv_raw = (
        jnp.dot(row_normed, qkv_cols, preferred_element_type=jnp.float32) + bias_local
    ).reshape(row_count, seq_len, local_heads, 3, HEAD_DIM)
    query_heads = (
        rotate(qkv_raw[:, :, :, 0], cosine, sine, 1.0)
        .astype(jnp.bfloat16)
        .reshape(row_count, seq_len, local_width)
    )
    key_heads = (
        rotate(qkv_raw[:, :, :, 1], cosine, sine, 1.0)
        .astype(jnp.bfloat16)
        .reshape(row_count, seq_len, local_width)
    )
    value_heads = qkv_raw[:, :, :, 2].astype(jnp.bfloat16).reshape(row_count, seq_len, local_width)
    head_shape = (seq_len, local_heads, HEAD_DIM)

    def forward_row(row_data):
        row_query, row_key, row_value, row_length = row_data
        return attend_forward(
            row_query.reshape(head_shape),
            row_key.reshape(head_shape),
            row_value.reshape(head_shape),
            row_length,
            block_rows,
        )

    attended_heads, log_totals = lax.map(
        forward_row, (query_heads, key_heads, value_heads, lengths)
    )
    attended_heads = attended_heads.reshape(row_count, seq_len, local_width)
    attended_flat = attended_heads.reshape(row_count * seq_len, local_width)
    branch_part = jnp.dot(attended_flat, out_rows, preferred_element_type=jnp.float32).reshape(
        row_count, seq_len, width
    )
    branch = lax.psum_scatter(branch_part, "sp", scatter_dimension=1, tiled=True).reshape(
        tokens_dev, width
    )
    resid = hidden_in + branch
    normed_two, unit_two, rstd_two = norm_forward(resid, gain_two, bias_two)
    normed_two = normed_two.astype(jnp.bfloat16)
    out_grad = (cotangent.astype(jnp.float32).reshape(tokens_dev, width) * valid).astype(
        jnp.bfloat16
    )
    row_tokens, row_grads = (
        lax.all_gather(normed_two.reshape(row_count, slot_count, width), "sp", axis=1, tiled=True),
        lax.all_gather(out_grad.reshape(row_count, slot_count, width), "sp", axis=1, tiled=True),
    )
    mixed_part, token_grad_part, mlp_grads = feed_forward(
        row_tokens.reshape(row_count * seq_len, width),
        row_grads.reshape(row_count * seq_len, width),
        w_gate,
        w_up,
        w_down,
    )
    mixed, normed_two_grad = (
        lax.psum_scatter(
            mixed_part.reshape(row_count, seq_len, width), "sp", scatter_dimension=1, tiled=True
        ),
        lax.psum_scatter(
            token_grad_part.reshape(row_count, seq_len, width),
            "sp",
            scatter_dimension=1,
            tiled=True,
        ),
    )
    mixed = mixed.reshape(tokens_dev, width)
    normed_two_grad = normed_two_grad.reshape(tokens_dev, width)
    layer_output = (
        (valid * (resid + mixed)).astype(jnp.bfloat16).reshape(row_count, slot_count, width)
    )
    resid_part, gain_two_grad, bias_two_grad = norm_backward(
        normed_two_grad, unit_two, rstd_two, gain_two
    )
    resid_grad = out_grad.astype(jnp.float32) + resid_part
    branch_grad = resid_grad.astype(jnp.bfloat16)
    row_branch = lax.all_gather(
        branch_grad.reshape(row_count, slot_count, width), "sp", axis=1, tiled=True
    ).reshape(row_count * seq_len, width)
    out_weight_grad = contract_rows(attended_flat, row_branch)
    attended_grad_heads = (
        contract_cols(row_branch, out_rows)
        .astype(jnp.bfloat16)
        .reshape(row_count, seq_len, local_width)
    )

    def backward_row(row_data):
        row_query, row_key, row_value, row_grad, row_totals, row_length = row_data
        query_grad, key_grad, value_grad = attend_backward(
            row_query.reshape(head_shape),
            row_key.reshape(head_shape),
            row_value.reshape(head_shape),
            row_grad.reshape(head_shape),
            row_totals,
            row_length,
            block_rows,
        )
        return (
            query_grad.astype(jnp.bfloat16).reshape(seq_len, local_width),
            key_grad.astype(jnp.bfloat16).reshape(seq_len, local_width),
            value_grad.astype(jnp.bfloat16).reshape(seq_len, local_width),
        )

    query_grads, key_grads, value_grads = lax.map(
        backward_row,
        (query_heads, key_heads, value_heads, attended_grad_heads, log_totals, lengths),
    )
    row_shape = (row_count, seq_len, local_heads, HEAD_DIM)
    query_raw = rotate(query_grads.astype(jnp.float32).reshape(row_shape), cosine, sine, -1.0)
    key_raw = rotate(key_grads.astype(jnp.float32).reshape(row_shape), cosine, sine, -1.0)
    value_raw = value_grads.astype(jnp.float32).reshape(row_shape)
    qkv_grad = (
        jnp.stack([query_raw, key_raw, value_raw], axis=3)
        .reshape(row_count * seq_len, local_cols)
        .astype(jnp.bfloat16)
    )
    bias_local_grad = jnp.sum(qkv_grad.astype(jnp.float32), axis=0)
    qkv_bias_full = lax.dynamic_update_slice(
        jnp.zeros((3 * width,), jnp.float32), bias_local_grad, (sp_index * local_cols,)
    )
    qkv_weight_grad = contract_rows(row_normed, qkv_grad)
    normed_part = contract_cols(qkv_grad, qkv_cols).reshape(row_count, seq_len, width)
    normed_one_grad = (
        lax.psum_scatter(normed_part.astype(jnp.bfloat16), "sp", scatter_dimension=1, tiled=True)
        .astype(jnp.float32)
        .reshape(tokens_dev, width)
    )
    input_part, gain_one_grad, bias_one_grad = norm_backward(
        normed_one_grad, unit_one, rstd_one, gain_one
    )
    input_grad = (resid_grad + input_part).reshape(row_count, slot_count, width)
    small_sums = (
        lax.psum_scatter(gain_one_grad, ("dp", "sp"), scatter_dimension=0, tiled=True),
        lax.psum_scatter(bias_one_grad, ("dp", "sp"), scatter_dimension=0, tiled=True),
        lax.psum_scatter(gain_two_grad, ("dp", "sp"), scatter_dimension=0, tiled=True),
        lax.psum_scatter(bias_two_grad, ("dp", "sp"), scatter_dimension=0, tiled=True),
        lax.psum_scatter(qkv_bias_full, ("dp", "sp"), scatter_dimension=0, tiled=True),
    )
    row_sums = (
        lax.psum_scatter(
            qkv_weight_grad.astype(jnp.bfloat16), "dp", scatter_dimension=0, tiled=True
        ).astype(jnp.float32),
        lax.psum_scatter(
            out_weight_grad.astype(jnp.bfloat16), "dp", scatter_dimension=1, tiled=True
        ).astype(jnp.float32),
        lax.psum_scatter(
            mlp_grads[0].astype(jnp.bfloat16), "dp", scatter_dimension=0, tiled=True
        ).astype(jnp.float32),
        lax.psum_scatter(
            mlp_grads[1].astype(jnp.bfloat16), "dp", scatter_dimension=0, tiled=True
        ).astype(jnp.float32),
        lax.psum_scatter(
            mlp_grads[2].astype(jnp.bfloat16), "dp", scatter_dimension=0, tiled=True
        ).astype(jnp.float32),
    )
    return (
        layer_output,
        input_grad,
        small_sums[0],
        small_sums[1],
        small_sums[2],
        small_sums[3],
        row_sums[0],
        small_sums[4],
        row_sums[1],
        row_sums[2],
        row_sums[3],
        row_sums[4],
    )


def dot_nn(left, right):
    return lax.dot_general(left, right, (((1,), (0,)), ((), ())), preferred_element_type=F32)


def dot_nt(left, right):
    return lax.dot_general(left, right, (((1,), (1,)), ((), ())), preferred_element_type=F32)


def dot_tn(left, right):
    return lax.dot_general(left, right, (((0,), (0,)), ((), ())), preferred_element_type=F32)


def iota(shape, dim):
    return lax.broadcasted_iota(jnp.int32, shape, dim)


def tile(index, size):
    return pl.ds(pl.multiple_of(index * size, size), size)


def normalize(hidden):
    centre = hidden - jnp.mean(hidden, axis=-1, keepdims=True)
    rstd = lax.rsqrt(jnp.mean(centre * centre, axis=-1, keepdims=True) + eps_norm)
    return centre * rstd, rstd


class Plan:
    def __init__(self, dp, sp, slots, width, ff_cols):
        self.dp, self.sp, self.slots, self.width = dp, sp, slots, width
        self.chips = dp // 2
        self.chunk = 2 * slots
        self.tokens = sp * self.chunk
        self.seq = sp * slots
        self.shard = width // dp
        self.head_cols = width // sp // 2
        self.pairs = self.head_cols // 128
        self.qkv_cols = 3 * self.head_cols
        self.ff_cols = ff_cols
        lanes = ff_cols // 128
        self.ff_wide = -(-lanes // 2) * 128
        self.ff_slim = ff_cols - self.ff_wide
        self.count_send = 0
        self.count_recv = 0

    def sems(self, send, recv):
        at = (self.count_send, self.count_recv)
        self.count_send += send
        self.count_recv += recv
        return at


def layer_kernel(plan, sem_at, *refs):
    (
        x_in, cot_in, small_in, cos_in, sin_in, wqkv_in, wout_in, wg_in, wu_in, wd_in,
        out_ref, grad_ref, sums_ref, rg_qkv, rg_out, rg_gate, rg_up, rg_down, n1_hbm,
        ssem, rsem, lsem,
        w_qkv, w_out, w_gate, w_up, w_down,
        buf_a, buf_b, buf_c,
        part, part_x, part_r, mix, mix_x, mix_r,
        q_ref, k_ref, v_ref, att,
        act, dgate, dup,
        resid, acc, dres,
        small, vecs, qbias, lens, colsum, biassum, send_sum, recv_sum, z_sum,
        st_qkv, st_out, st_gate, st_up, st_down,
    ) = refs
    sp, dp, slots, width, chunk = plan.sp, plan.dp, plan.slots, plan.width, plan.chunk
    d = lax.axis_index("dp")
    z = lax.axis_index("sp")
    c = d % 2
    oc = 1 - c
    chip = d // 2
    sib = (d + 1 - 2 * c, z)
    first_row = c * slots
    last = sp - 1

    def remote(src, dst, si, ri, dev):
        return pltpu.make_async_remote_copy(
            src_ref=src, dst_ref=dst, send_sem=ssem.at[si], recv_sem=rsem.at[ri],
            device_id=dev, device_id_type=MESH,
        )

    def wait_send(src, si):
        remote(src, src, si, 0, sib).wait_send()

    def wait_recv(dst, ri):
        remote(dst, dst, 0, ri, sib).wait_recv()

    def block(buf, t, core):
        return buf.at[pl.ds(pl.multiple_of(t * chunk + core * slots, slots), slots)]

    def sub_block(buf, t, core, at):
        start, size = at
        return buf.at[pl.ds(pl.multiple_of(t * chunk + core * slots + start, size), size)]

    def rows_of(buf, t):
        return buf.at[tile(t, chunk)]

    def spans(size, step):
        return [slice(i, min(i + step, size)) for i in range(0, size, step)]

    def slot_block(buf, t, at):
        start, size = at
        return buf.at[pl.ds(pl.multiple_of(t * slots + start, size), size)]

    whole = (0, slots)
    def parts(count):
        return [(h * (slots // count), slots // count) for h in range(count)]


    barrier = pltpu.get_barrier_semaphore()
    for i in range(1, dp):
        pl.semaphore_signal(barrier, inc=1, device_id=((d + i) % dp, z), device_id_type=MESH)
    for i in range(1, sp):
        pl.semaphore_signal(barrier, inc=1, device_id=(d, (z + i) % sp), device_id_type=MESH)
    pl.semaphore_wait(barrier, dp + sp - 2)

    class Gather:
        def __init__(self, name, buf, at=whole):
            self.s, self.r = sem_at[name]
            self.buf, self.at = buf, at

        def start(self, own):
            s, r = self.s, self.r
            dst = sub_block(self.buf, z, c, self.at)

            @pl.when(z < last)
            def _():
                remote(own, dst, s, r + z, (d, z + 1)).start()

            @pl.when(z > 0)
            def _():
                remote(own, dst, s + 1, r + z, (d, z - 1)).start()

            remote(own, dst, s + 2 + sp + z, r + sp + z, sib).start()

        def hop(self, k):
            s, r = self.s, self.r
            for sign in (-1, 1):
                t = z + sign * k
                nxt = z - sign
                blk = sub_block(self.buf, t, c, self.at)

                @pl.when((t >= 0) & (t <= last))
                def _():
                    wait_recv(blk, r + t)

                    @pl.when((nxt >= 0) & (nxt <= last))
                    def _():
                        remote(blk, blk, s + 2 + t, r + t, (d, nxt)).start()

                    remote(blk, blk, s + 2 + sp + t, r + sp + t, sib).start()

        def need(self, t):
            wait_recv(sub_block(self.buf, t, oc, self.at), self.r + sp + t)

        def drain(self, own):
            s = self.s

            @pl.when(z < last)
            def _():
                wait_send(own, s)

            @pl.when(z > 0)
            def _():
                wait_send(own, s + 1)

            for t in range(sp):
                wait_send(own, s + 2 + sp + t)

                @pl.when(((t < z) & (z < last)) | ((t > z) & (z > 0)))
                def _():
                    wait_send(own, s + 2 + t)

    def order(i):
        low = jnp.minimum(z, last - z)
        k = jnp.where(i <= 2 * low, (i + 1) // 2, i - low)
        paired = jnp.where(i % 2 == 1, z - k, z + k)
        single = jnp.where(z < last - z, z + k, z - k)
        return jnp.where(i <= 2 * low, paired, single)

    def add_into(dst, terms):
        @pl.loop(0, dst.shape[0] // ADD_ROWS)
        def _(i):
            sl = tile(i, ADD_ROWS)
            total = dst[sl, :].astype(F32)
            for term in terms:
                total = total + term[sl, :].astype(F32)
            dst[sl, :] = total.astype(dst.dtype)

    class Scatter:
        def __init__(self, name, parts, from_core, from_line, at=whole):
            self.s, self.r = sem_at[name]
            self.p, self.x, self.l, self.at = parts, from_core, from_line, at

        def core(self, t):
            remote(
                sub_block(self.p, t, oc, self.at), slot_block(self.x, t, self.at), self.s + t, self.r + t, sib
            ).start()

        def send(self, t, from_end, nbr, slot):
            mine = sub_block(self.p, t, c, self.at)
            xs = slot_block(self.x, t, self.at)
            wait_recv(xs, self.r + t)

            @pl.when(from_end)
            def _():
                add_into(mine, [xs])

            @pl.when(jnp.logical_not(from_end))
            def _():
                ls = slot_block(self.l, t, self.at)
                wait_recv(ls, self.r + sp + t)
                add_into(mine, [xs, ls])

            remote(
                mine, slot_block(self.l, slot, self.at), self.s + sp + t, self.r + sp + slot, (d, nbr)
            ).start()

        def step(self, n):
            left = n - (last - z)

            @pl.when((left >= 0) & (left < z))
            def _():
                self.send(left, z == last, z - 1, left)

            right = n - z

            @pl.when((right >= 0) & (right < last - z))
            def _():
                t = last - right
                self.send(t, z == 0, z + 1, jnp.where(t == z + 1, sp, t))

        def final(self, total):
            total = total.at[pl.ds(*self.at)]
            mine = sub_block(self.p, z, c, self.at)
            xs = slot_block(self.x, z, self.at)
            wait_recv(xs, self.r + z)

            @pl.loop(0, self.at[1] // ADD_ROWS)
            def _(i):
                sl = tile(i, ADD_ROWS)
                total[sl, :] = mine[sl, :].astype(F32) + xs[sl, :].astype(F32)

            @pl.when(z < last)
            def _():
                ls = slot_block(self.l, z, self.at)
                wait_recv(ls, self.r + sp + z)
                add_into(total, [ls])

            @pl.when(z > 0)
            def _():
                ls = slot_block(self.l, sp, self.at)
                wait_recv(ls, self.r + sp + sp)
                add_into(total, [ls])

        def drain(self):
            for t in range(sp):
                wait_send(slot_block(self.x, t, self.at), self.s + t)

                @pl.when(t != z)
                def _():
                    wait_send(slot_block(self.x, t, self.at), self.s + sp + t)

    def chip_target(q):
        cx, cy = chip % 2, chip // 2
        if q % 2:
            cx = 1 - cx
        if q // 2:
            cy = 1 - cy
        return 2 * cx + 4 * cy

    def weight_window(name, src, core):
        if name == "out":
            half = plan.head_cols
            return src.at[pl.ds(core * half, half), :]
        if name == "qkv":
            return src.at[:, pl.ds(core * plan.qkv_cols, plan.qkv_cols)]
        return src.at[:, pl.ds(core * plan.ff_wide, plan.ff_slim if core else plan.ff_wide)]

    def weight_place(name, dst, owner, core):
        if name == "out":
            return dst.at[:, tile(owner, plan.shard)]
        if name == "qkv":
            return dst.at[tile(owner, plan.shard), :]
        return dst.at[tile(owner, plan.shard), pl.ds(0, plan.ff_slim if core else plan.ff_wide)]

    def weight_send(name, src, dst):
        s, r = sem_at["w_" + name]
        for q in (1, 2, 0):
            for core in (0, 1):
                target = chip_target(q) + core
                here = weight_window(name, src, core)
                there = weight_place(name, dst, d, core)
                if q:
                    remote(here, there, s + 2 * q + core, r + d, (target, z)).start()
                else:

                    @pl.when(c != core)
                    def _():
                        remote(here, there, s + core, r + d, (target, z)).start()

                    @pl.when(c == core)
                    def _():
                        pltpu.make_async_copy(here, there, lsem.at[WEIGHTS.index(name)]).start()

    def weight_forward(name, dst):
        s, r = sem_at["w_" + name]
        for core in (0, 1):

            @pl.when(c == core)
            def _():
                for k in (0, 1):
                    owner = chip_target(1 if core else 2) + k
                    place = weight_place(name, dst, owner, core)
                    wait_recv(place, r + owner)
                    target = chip_target(2 if core else 1) + core
                    remote(place, place, s + 6 + k, r + owner, (target, z)).start()

    def weight_wait(name, src, dst):
        _, r = sem_at["w_" + name]
        for core in (0, 1):

            @pl.when(c == core)
            def _():
                for q in (0, 2 if core else 1, 3):
                    for k in (0, 1):
                        if q or k != core:
                            owner = chip_target(q) + k
                            wait_recv(weight_place(name, dst, owner, core), r + owner)
                pltpu.make_async_copy(
                    weight_window(name, src, core), weight_place(name, dst, d, core),
                    lsem.at[WEIGHTS.index(name)],
                ).wait()

    def weight_drain(name, src, dst):
        s, _ = sem_at["w_" + name]
        for core in (0, 1):
            here = weight_window(name, src, core)
            wait_send(here, s + 2 + core)
            wait_send(here, s + 4 + core)

            @pl.when(c != core)
            def _():
                wait_send(here, s + core)

            @pl.when(c == core)
            def _():
                place = weight_place(name, dst, d, core)
                wait_send(place, s + 6)
                wait_send(place, s + 7)

    def wgrad_piece(name, src, owner, core):
        if name == "out":
            return src.at[:, tile(owner, plan.shard)]
        if name == "qkv":
            return src.at[tile(owner, plan.shard), :]
        return src.at[tile(owner, plan.shard), pl.ds(0, plan.ff_slim if core else plan.ff_wide)]

    def wgrad_place(name, dst, slot, core):
        if name == "out":
            return dst.at[slot, pl.ds(core * plan.head_cols, plan.head_cols), :]
        if name == "qkv":
            return dst.at[slot, :, pl.ds(core * plan.qkv_cols, plan.qkv_cols)]
        return dst.at[slot, :, pl.ds(core * plan.ff_wide, plan.ff_slim if core else plan.ff_wide)]

    def stage_place(name, stage, k, core):
        if name in ("out", "qkv"):
            return stage.at[k]
        return stage.at[k, :, pl.ds(0, plan.ff_slim if core else plan.ff_wide)]

    def wgrad_send(name, src, dst, stage):
        s, r = sem_at["g_" + name]
        for core in (0, 1):
            near = 1 if core else 2

            @pl.when(c == core)
            def _():
                for k in (0, 1):
                    remote(
                        wgrad_piece(name, src, chip_target(3) + k, core),
                        stage_place(name, stage, k, core),
                        s + k, r + 6 + k, (chip_target(near) + core, z),
                    ).start()
                for k in (0, 1):
                    target = chip_target(near) + k
                    remote(
                        wgrad_piece(name, src, target, core),
                        wgrad_place(name, dst, near, core),
                        s + 2 + k, r + 2 * near + core, (target, z),
                    ).start()
                remote(
                    wgrad_piece(name, src, d + 1 - 2 * core, core),
                    wgrad_place(name, dst, 0, core), s + 4, r + core, sib,
                ).start()
                pltpu.make_async_copy(
                    wgrad_piece(name, src, d, core), wgrad_place(name, dst, 0, core),
                    lsem.at[len(WEIGHTS) + WEIGHTS.index(name)],
                ).start()

    def wgrad_merge(name, src, dst, stage):
        s, r = sem_at["g_" + name]
        for core in (0, 1):
            far = 2 if core else 1

            @pl.when(c == core)
            def _():
                for k in (0, 1):
                    target = chip_target(far) + k
                    came = stage_place(name, stage, k, core)
                    mine = wgrad_piece(name, src, target, core)
                    wait_recv(came, r + 6 + k)

                    @pl.loop(0, came.shape[0] // 32)
                    def _(i):
                        sl = tile(i, 32)
                        mine[sl, :] = (mine[sl, :].astype(F32) + came[sl, :].astype(F32)).astype(BF16)

                    remote(
                        mine, wgrad_place(name, dst, far, core), s + 5 + k, r + 2 * far + core,
                        (target, z),
                    ).start()

    def wgrad_finish(name, src, dst):
        s, r = sem_at["g_" + name]
        for core in (0, 1):

            @pl.when(c == core)
            def _():
                here = wgrad_piece(name, src, d, core)
                for i in range(7):
                    wait_send(here, s + i)
                wait_recv(wgrad_place(name, dst, 0, 1 - core), r + 1 - core)
                for slot in (1, 2):
                    for k in (0, 1):
                        wait_recv(wgrad_place(name, dst, slot, k), r + 2 * slot + k)
                pltpu.make_async_copy(
                    here, wgrad_place(name, dst, 0, core),
                    lsem.at[len(WEIGHTS) + WEIGHTS.index(name)],
                ).wait()

    gather_x = Gather("ag_x", buf_a)
    gather_d = Gather("ag_d", buf_c)
    gather_n = [Gather("ag_n%d" % h, buf_a, at) for h, at in enumerate(parts(PARTS_FORWARD))]
    gather_b = [Gather("ag_b%d" % h, buf_b, at) for h, at in enumerate(parts(PARTS_BACK))]
    scatter_o = [Scatter("rs_o%d" % h, part, part_x, part_r, at) for h, at in enumerate(parts(PARTS_FORWARD))]
    scatter_n = [Scatter("rs_n%d" % h, part, part_x, part_r, at) for h, at in enumerate(parts(PARTS_BACK))]
    scatter_i = [Scatter("rs_i%d" % h, part, part_x, part_r, at) for h, at in enumerate(parts(PARTS_LAST))]
    scatter_m = Scatter("rs_m", mix, mix_x, mix_r)

    sz, rz = sem_at["sm_z"]
    sd, rd = sem_at["sm_d"]
    small[d, z] = small_in[...]
    for i in range(1, sp):
        peer = (z + i) % sp
        remote(small_in, small.at[d, z], sz + i, rz + z, (d, peer)).start()
    gather_x.start(x_in)
    for i in range(1, sp):
        peer = (z + i) % sp
        wait_recv(small.at[d, peer], rz + peer)
    for i in range(1, dp):
        peer = (d + i) % dp
        remote(small.at[d], small.at[d], sd + i, rd + d, (peer, z)).start()
    weight_send("qkv", wqkv_in, w_qkv)

    block(buf_a, z, c)[...] = x_in[...]
    own_len = small_in[7:8, 0:1]

    @pl.loop(0, slots // 32)
    def _(i):
        sl = tile(i, 32)
        pos = (iota((32, 1), 0) + (z * slots + i * 32)).astype(F32)
        keep = jnp.where(pos < own_len, 1.0, 0.0)
        block(buf_c, z, c)[sl, :] = (cot_in[sl, :].astype(F32) * keep).astype(BF16)

    @pl.when(c == 1)
    def _():
        pad = plan.ff_wide - plan.ff_slim
        for ref in (w_gate, w_up, w_down):
            ref[:, plan.ff_slim :] = jnp.zeros((width, pad), BF16)

    for i in range(1, dp):
        peer = (d + i) % dp
        wait_recv(small.at[peer], rd + peer)
    per_dp = width // dp // 128
    for i in range(dp):
        for h in range(per_dp):
            at = (i * per_dp + h) * 128
            vecs[:, at : at + 128] = small[i, 2 * h] + small[i, 2 * h + 1]
    bias_at = 2 * z + c
    for h in range(sp // 2):
        for k in range(3):
            at = h * 384 + k * 128
            qbias[0:1, at : at + 128] = (
                small[bias_at, 2 * h, 4 + k : 5 + k, :] + small[bias_at, 2 * h + 1, 4 + k : 5 + k, :]
            )
    for r in range(2):
        lens[r : r + 1, :] = small[2 * chip + r, 0, 7:8, :]

    n1 = buf_b
    gain_one, bias_one = vecs[0:1, :], vecs[1:2, :]

    @pl.loop(0, sp)
    def _(i):
        @pl.when(i == last - 1)
        def _():
            weight_forward("qkv", w_qkv)
            weight_send("out", wout_in, w_out)

        @pl.when(i == last)
        def _():
            weight_forward("out", w_out)
            weight_send("gate", wg_in, w_gate)
            weight_send("up", wu_in, w_up)

        @pl.when(i > 0)
        def _():
            gather_x.hop(i)

        t = order(i)
        gather_x.need(t)
        src, dst = rows_of(buf_a, t), rows_of(n1, t)

        @pl.loop(0, chunk // 64)
        def _(j):
            sl = tile(j, 64)
            unit, _ = normalize(src[sl, :].astype(F32))
            dst[sl, :] = (unit * vecs[0:1, :] + vecs[1:2, :]).astype(BF16)

    gather_d.start(block(buf_c, z, c))
    n1_copy = pltpu.make_async_copy(n1, n1_hbm, lsem.at[2 * len(WEIGHTS)])
    n1_copy.start()

    weight_wait("qkv", wqkv_in, w_qkv)
    low = iota((1, 128), 1) < 64
    first_half = iota((1, 128), 1) % 64 < ROT // 2

    def rotated(v, cosine, sine):
        swapped = jnp.where(
            first_half, pltpu.roll(v, 128 - ROT // 2, 1), pltpu.roll(v, ROT // 2, 1)
        )
        return v * cosine + swapped * sine

    raw = (resid, dres)

    @pl.loop(0, sp)
    def _(t):
        src = rows_of(n1, t)

        both = dot_nn(src[...], w_qkv[...]) + qbias[0:1, :]
        for r in range(2):
            raw[r][:, 0 : plan.qkv_cols] = both[r * slots : (r + 1) * slots]

        here = tile(t, slots)
        cosine, sine = cos_in[here, :], sin_in[here, :]
        for r in range(2):
            for p in range(plan.pairs):
                v0 = raw[r][:, p * 384 : p * 384 + 128]
                v1 = raw[r][:, p * 384 + 128 : p * 384 + 256]
                v2 = raw[r][:, p * 384 + 256 : p * 384 + 384]
                r0 = rotated(v0, cosine, sine)
                r1 = rotated(v1, cosine, sine)
                r2 = rotated(v2, cosine, sine)
                q_ref[r, p, here, :] = jnp.where(low, r0, r1).astype(BF16)
                k_ref[r, p, here, :] = pltpu.roll(jnp.where(low, r2, r0), 64, 1).astype(BF16)
                v_ref[r, p, here, :] = jnp.where(low, v1, v2).astype(BF16)

    q_rows = min(256, plan.seq)
    q_blocks = plan.seq // q_rows
    per_q = q_rows // slots
    scale = HEAD_DIM ** (-0.5)

    def weights_of(r, p, h, qb):
        keys_to = (qb + 1) * q_rows
        mask = low if h == 0 else jnp.logical_not(low)
        qh = jnp.where(mask, q_ref[r, p, qb * q_rows : keys_to, :], 0).astype(BF16)
        scores = dot_nt(k_ref[r, p, 0:keys_to, :], qh) * scale
        key_pos = iota((keys_to, q_rows), 0)
        query_pos = iota((keys_to, q_rows), 1) + qb * q_rows
        length = lens[pl.ds(r, 1), 0:1]
        allowed = (key_pos <= query_pos) & (key_pos.astype(F32) < length)
        scores = jnp.where(allowed, scores, neg_large)
        expo = jnp.exp(scores - jnp.max(scores, axis=0, keepdims=True))
        return expo * (1.0 / jnp.sum(expo, axis=0, keepdims=True))

    def att_rows(r, t):
        return pl.ds(pl.multiple_of(t * chunk + r * slots, slots), slots)

    def attention(r, p):
        for qb in range(q_blocks):
            outs = []
            for h in range(2):
                probs = weights_of(r, p, h, qb).astype(BF16)
                outs.append(dot_tn(probs, v_ref[r, p, 0 : (qb + 1) * q_rows, :]))
            both = jnp.where(low, outs[0], outs[1]).astype(BF16)
            for i in range(per_q):
                att[att_rows(r, qb * per_q + i), p * 128 : (p + 1) * 128] = both[
                    i * slots : (i + 1) * slots
                ]

    @pl.loop(0, 2)
    def _(r):
        for p in range(plan.pairs):
            attention(r, p)

    gather_d.hop(1)
    gather_x.drain(x_in)

    weight_forward("gate", w_gate)
    weight_send("down", wd_in, w_down)
    weight_wait("out", wout_in, w_out)

    def far_first(i):
        return jnp.where(z < last - z, last - i, i)

    @pl.loop(0, sp)
    def _(i):
        t = far_first(i)
        src, dst = rows_of(att, t), rows_of(part, t)

        for sl in spans(width, 512):
            dst[:, sl] = dot_nn(src[...], w_out[:, sl]).astype(BF16)

        for part_o in scatter_o:
            part_o.core(t)

    own_n = block(buf_a, z, c)

    def second_norm(at):
        rows = pl.ds(*at)
        x_rows, acc_rows, resid_rows, n_rows = (
            ref.at[rows] for ref in (x_in, acc, resid, own_n)
        )

        @pl.loop(0, at[1] // 32)
        def _(i):
            sl = tile(i, 32)
            hidden = x_rows[sl, :].astype(F32) + acc_rows[sl, :]
            resid_rows[sl, :] = hidden
            unit, _ = normalize(hidden)
            n_rows[sl, :] = (unit * vecs[2:3, :] + vecs[3:4, :]).astype(BF16)

    def pipeline(scatters, total, middle, gathers, buf, extra):
        scatters[0].step(0)
        for h, scatter in enumerate(scatters):
            for k in range(1, sp - 1):
                extra()
                scatter.step(k)
                if h:
                    gathers[h - 1].hop(k)
            if h + 1 < len(scatters):
                scatters[h + 1].step(0)
            extra()
            scatter.final(total)
            middle(scatter.at)
            gathers[h].start(sub_block(buf, z, c, scatter.at))
            if h:
                for k in range(sp - 1, sp):
                    gathers[h - 1].hop(k)

    def one_by_one(*steps):
        todo = list(steps)

        def extra():
            if todo:
                todo.pop(0)()

        return extra, todo

    extra, todo = one_by_one(
        lambda: None,
        lambda: (weight_forward("up", w_up), gather_d.hop(2)),
        lambda: None,
        lambda: weight_forward("down", w_down),
    )
    pipeline(scatter_o, acc, second_norm, gather_n, buf_a, extra)
    for step in todo:
        step()
    for part_o in scatter_o:
        part_o.drain()
    n1_copy.wait()

    def feed_forward(t):
        for part_n in gather_n:
            part_n.need(t)
        tok = rows_of(buf_a, t)
        act_t, dg_t, du_t = rows_of(act, t), rows_of(dgate, t), rows_of(dup, t)
        for sl in spans(plan.ff_wide, 256):
            gate = dot_nn(tok[...], w_gate[:, sl])
            up = dot_nn(tok[...], w_up[:, sl])
            sig = jax.nn.sigmoid(gate)
            silu = gate * sig
            act_t[:, sl] = (silu * up).astype(BF16)
            du_t[:, sl] = silu.astype(BF16)
            dg_t[:, sl] = (up * sig * (1.0 + gate * (1.0 - sig))).astype(BF16)

    def feed_back(t):
        gather_d.need(t)
        dg_t, du_t = rows_of(dgate, t), rows_of(dup, t)
        gout, part_t = rows_of(buf_c, t), rows_of(part, t)
        for sl in spans(plan.ff_wide, 256):
            d_act = dot_nn(gout[...], w_down[:, sl])
            du_t[:, sl] = (d_act * du_t[:, sl].astype(F32)).astype(BF16)
            dg_t[:, sl] = (d_act * dg_t[:, sl].astype(F32)).astype(BF16)
        for sl in spans(width, 512):
            part_t[:, sl] = (
                dot_nt(dg_t[...], w_gate[sl, :]) + dot_nt(du_t[...], w_up[sl, :])
            ).astype(BF16)
        for part_n in scatter_n:
            part_n.core(t)

    weight_wait("gate", wg_in, w_gate)
    weight_wait("up", wu_in, w_up)

    @pl.loop(0, sp)
    def _(i):
        @pl.when(i > 0)
        def _():
            gather_n[-1].hop(i)

        @pl.when(i == last)
        def _():
            for k in range(3, sp):
                gather_d.hop(k)

        feed_forward(order(i))

        @pl.when(i == BACK_FROM)
        def _():
            weight_wait("down", wd_in, w_down)

        first = jnp.where(i == BACK_FROM, 0, i)
        stop = jnp.where(i < BACK_FROM, 0, i + 1)

        @pl.loop(first, stop)
        def _(j):
            feed_back(order(j))

    def wgrad(tokens, cols, dst, start, stop):
        @pl.loop(start, stop)
        def _(n):
            sl = tile(n, 512)
            dst[sl, :] = dot_tn(tokens[:, sl], cols[...]).astype(BF16)

    n_tiles = width // 512
    half = n_tiles // 2
    for name, src, dst in (("down", wd_in, w_down), ("gate", wg_in, w_gate), ("up", wu_in, w_up)):
        weight_drain(name, src, dst)
    colsum[...] = jnp.zeros_like(colsum)
    own_d, own_b = block(buf_c, z, c), block(buf_b, z, c)

    def norm_back(grad, hidden, gain, row):
        unit, rstd = normalize(hidden)
        colsum[row : row + 1, :] += jnp.sum(grad * unit, axis=0, keepdims=True)
        colsum[row + 1 : row + 2, :] += jnp.sum(grad, axis=0, keepdims=True)
        scaled = grad * gain
        return rstd * (
            scaled
            - jnp.mean(scaled, axis=-1, keepdims=True)
            - unit * jnp.mean(scaled * unit, axis=-1, keepdims=True)
        )

    def second_norm_back(at):
        rows = pl.ds(*at)
        d_rows, acc_rows, resid_rows, dres_rows, b_rows = (
            ref.at[rows] for ref in (own_d, acc, resid, dres, own_b)
        )

        @pl.loop(0, at[1] // 32)
        def _(i):
            sl = tile(i, 32)
            back = d_rows[sl, :].astype(F32) + norm_back(
                acc_rows[sl, :], resid_rows[sl, :], vecs[2:3, :], 2
            )
            dres_rows[sl, :] = back
            b_rows[sl, :] = back.astype(BF16)

    def mixed():
        @pl.loop(0, sp)
        def _(i):
            t = far_first(i)
            act_t, mix_t = rows_of(act, t), rows_of(mix, t)
            for sl in spans(width, 512):
                mix_t[:, sl] = dot_nt(act_t[...], w_down[sl, :]).astype(BF16)
            scatter_m.core(t)

    def all_down():
        wgrad(buf_c, act, w_down, 0, n_tiles)
        wgrad_send("down", w_down, rg_down, st_down)

    def first_gate():
        wgrad(buf_a, dgate, w_gate, 0, half)

    def last_gate():
        wgrad(buf_a, dgate, w_gate, half, n_tiles)
        wgrad_send("gate", w_gate, rg_gate, st_gate)

    def first_up():
        wgrad(buf_a, dup, w_up, 0, half)

    def last_up():
        wgrad(buf_a, dup, w_up, half, n_tiles)
        wgrad_send("up", w_up, rg_up, st_up)

    extra, todo = one_by_one(lambda: (mixed(), all_down()), first_gate, last_gate, first_up, last_up)
    pipeline(scatter_n, acc, second_norm_back, gather_b, buf_b, extra)
    for step in todo:
        step()

    for h, part_n in enumerate(gather_n):
        part_n.drain(sub_block(buf_a, z, c, part_n.at))
    n1_back = pltpu.make_async_copy(n1_hbm, buf_a, lsem.at[2 * len(WEIGHTS) + 1])
    n1_back.start()
    datt = dgate.at[:, pl.ds(0, plan.head_cols)]
    dqkv = act.at[:, pl.ds(0, plan.qkv_cols)]
    for part_n in scatter_n:
        part_n.drain()
    scatter_m.step(0)
    wgrad_merge("down", w_down, rg_down, st_down)

    @pl.loop(0, sp)
    def _(i):
        @pl.when(i > 0)
        def _():
            gather_b[-1].hop(i)

        @pl.when((i > 0) & (i < last))
        def _():
            scatter_m.step(i)

        t = order(i)
        for part_b in gather_b:
            part_b.need(t)
        datt[tile(t, chunk), :] = dot_nt(rows_of(buf_b, t)[...], w_out[...]).astype(BF16)

    wgrad_merge("gate", w_gate, rg_gate, st_gate)

    biassum[...] = jnp.zeros_like(biassum)

    def attention_back(r, p):
        cols = slice(p * 128, (p + 1) * 128)
        for qb in range(q_blocks):
            keys_to = (qb + 1) * q_rows
            dav = jnp.concatenate(
                [datt[att_rows(r, qb * per_q + i), cols] for i in range(per_q)], axis=0
            )
            qv = q_ref[r, p, qb * q_rows : keys_to, :]
            dq, dk, dv = [], [], []
            for h in range(2):
                mask = low if h == 0 else jnp.logical_not(low)
                probs = weights_of(r, p, h, qb)
                dprobs = dot_nt(v_ref[r, p, 0:keys_to, :], jnp.where(mask, dav, 0).astype(BF16))
                delta = jnp.sum(dprobs * probs, axis=0, keepdims=True)
                dscores = (probs * (dprobs - delta)).astype(BF16)
                dv.append(dot_nn(probs.astype(BF16), dav))
                dk.append(dot_nn(dscores, qv))
                dq.append(dot_tn(dscores, k_ref[r, p, 0:keys_to, :]))
            dq_both = (jnp.where(low, dq[0], dq[1]) * scale).astype(BF16)
            dk_both = jnp.where(low, dk[0], dk[1])
            dv_both = jnp.where(low, dv[0], dv[1])
            for t in range(keys_to // slots):
                ts = slice(t * slots, (t + 1) * slots)
                for at, new in ((t, dk_both), (sp + t, dv_both)):
                    lanes = slice(at * 128, (at + 1) * 128)
                    if t * slots < qb * q_rows:
                        acc[:, lanes] += new[ts]
                    else:
                        acc[:, lanes] = new[ts]
            q_ref[r, p, qb * q_rows : keys_to, :] = dq_both
        for t in range(sp):
            ts = slice(t * slots, (t + 1) * slots)
            dqv = q_ref[r, p, ts, :].astype(F32)
            dkv = (acc[:, t * 128 : (t + 1) * 128] * scale).astype(BF16).astype(F32)
            dvv = acc[:, (sp + t) * 128 : (sp + t + 1) * 128].astype(BF16).astype(F32)
            swapped = pltpu.roll(dkv, 64, 1)
            cosine, sine = cos_in[ts, :], -sin_in[ts, :]
            g0 = rotated(jnp.where(low, dqv, swapped), cosine, sine)
            g1 = jnp.where(low, dvv, rotated(dqv, cosine, sine))
            g2 = jnp.where(low, rotated(swapped, cosine, sine), dvv)
            for k, g in enumerate((g0, g1, g2)):
                g = g.astype(BF16)
                dqkv[att_rows(r, t), p * 384 + k * 128 : p * 384 + (k + 1) * 128] = g
                row = 3 * p + k
                biassum[row : row + 1, :] += jnp.sum(g.astype(F32), axis=0, keepdims=True)

    @pl.loop(0, 2)
    def _(r):
        for p in range(plan.pairs):
            attention_back(r, p)

    wgrad_merge("up", w_up, rg_up, st_up)

    @pl.loop(0, sp)
    def _(i):
        t = far_first(i)
        dst, src = rows_of(part, t), rows_of(dqkv, t)

        for sl in spans(width, 512):
            dst[:, sl] = dot_nt(src[...], w_qkv[sl, :]).astype(BF16)

        for part_i in scatter_i:
            part_i.core(t)

    for part_i in scatter_i:
        part_i.step(0)
    weight_drain("qkv", wqkv_in, w_qkv)
    weight_drain("out", wout_in, w_out)
    n1_back.wait()
    wgrad(buf_a, dqkv, w_qkv, 0, n_tiles)
    wgrad_send("qkv", w_qkv, rg_qkv, st_qkv)
    for part_i in scatter_i:
        part_i.step(1)

    @pl.loop(0, width // 1024)
    def _(n):
        sl = tile(n, 1024)
        w_out[:, sl] = dot_tn(att[...], buf_b[:, sl]).astype(BF16)

    wgrad_send("out", w_out, rg_out, st_out)
    for k in range(2, sp - 1):
        for part_i in scatter_i:
            part_i.step(k)
    wgrad_merge("qkv", w_qkv, rg_qkv, st_qkv)
    scatter_m.final(acc)

    @pl.loop(0, slots // 32)
    def _(i):
        sl = tile(i, 32)
        pos = (iota((32, 1), 0) + (z * slots + i * 32)).astype(F32)
        keep = jnp.where(pos < small_in[7:8, 0:1], 1.0, 0.0)
        out_ref[sl, :] = (keep * (resid[sl, :] + acc[sl, :])).astype(BF16)

    wgrad_merge("out", w_out, rg_out, st_out)
    for part_i in scatter_i:
        part_i.final(acc)
        first = part_i.at[0] // 32

        @pl.loop(first, first + part_i.at[1] // 32)
        def _(i):
            sl = tile(i, 32)
            back = norm_back(acc[sl, :], x_in[sl, :].astype(F32), vecs[0:1, :], 0)
            grad_ref[sl, :] = dres[sl, :] + back

    per = plan.shard
    for i in range(dp):
        send_sum[i, :, 0:per] = colsum[:, i * per : (i + 1) * per]
        send_sum[i, :, per : per + 128] = biassum[...]
    sa, ra = sem_at["su_d"]
    sb, rb = sem_at["su_z"]
    recv_sum[d] = send_sum[d]
    for i in range(1, dp):
        peer = (d + i) % dp
        remote(send_sum.at[peer], recv_sum.at[d], sa + i, ra + d, (peer, z)).start()
    for i in range(1, dp):
        peer = (d + i) % dp
        wait_recv(recv_sum.at[peer], ra + peer)
    norm_total = recv_sum[0, :, 0:per]
    for i in range(1, dp):
        norm_total = norm_total + recv_sum[i, :, 0:per]
    bias_total = recv_sum[c, :, per : per + 128]
    for i in range(1, dp // 2):
        bias_total = bias_total + recv_sum[2 * i + c, :, per : per + 128]
    z_sum[z, :, 0:per] = norm_total
    z_sum[z, :, per : per + 128] = bias_total
    for i in range(1, sp):
        peer = (z + i) % sp
        remote(z_sum.at[z], z_sum.at[z], sb + i, rb + z, (d, peer)).start()
    for i in range(1, sp):
        peer = (z + i) % sp
        wait_recv(z_sum.at[peer], rb + peer)
    norm_total = z_sum[0, :, 0:per]
    for i in range(1, sp):
        norm_total = norm_total + z_sum[i, :, 0:per]
    sums_ref[:, 0:per] = norm_total
    sums_ref[:, per : per + 128] = z_sum[chip, :, per : per + 128]

    for name, src, dst in (
        ("down", w_down, rg_down), ("gate", w_gate, rg_gate), ("up", w_up, rg_up),
        ("qkv", w_qkv, rg_qkv), ("out", w_out, rg_out),
    ):
        wgrad_finish(name, src, dst)
    gather_d.drain(own_d)
    for h, part_b in enumerate(gather_b):
        part_b.drain(sub_block(buf_b, z, c, part_b.at))
    scatter_m.drain()
    for part_i in scatter_i:
        part_i.drain()
    for i in range(1, sp):
        wait_send(small_in, sz + i)
        wait_send(z_sum.at[z], sb + i)
    for i in range(1, dp):
        wait_send(small.at[d], sd + i)
        wait_send(send_sum.at[0], sa + i)


PARTS_FORWARD = 1
PARTS_BACK = 1
PARTS_LAST = 1
BACK_FROM = 1
ADD_ROWS = 64
WEIGHTS = ("qkv", "out", "gate", "up", "down")


def rotary_lanes(seq_len):
    half = ROT // 2
    freq = theta ** (-(np.arange(half, dtype=np.float32) * np.float32(2.0)) / np.float32(ROT))
    angles = np.arange(seq_len, dtype=np.float32)[:, None] * freq.astype(np.float32)[None, :]
    cosine, sine = np.cos(angles), np.sin(angles)
    cos_head = np.ones((seq_len, HEAD_DIM), np.float32)
    sin_head = np.zeros((seq_len, HEAD_DIM), np.float32)
    cos_head[:, :half], cos_head[:, half:ROT] = cosine, cosine
    sin_head[:, :half], sin_head[:, half:ROT] = -sine, sine
    return np.tile(cos_head, (1, 2)), np.tile(sin_head, (1, 2))


def last_sums_kernel(*refs):
    count = len(refs) // 2
    for src, dst in zip(refs[:2], refs[count : count + 2]):
        dst[...] = src[...]
    for src, dst in zip(refs[2:count], refs[count + 2 :]):
        total = src[0].astype(F32)
        for k in range(1, src.shape[0]):
            total = total + src[k].astype(F32)
        dst[...] = total


def last_sums(*arrays):
    steps = 8
    in_specs, out_specs, out_shape = [], [], []
    for i, array in enumerate(arrays):
        rows, cols = array.shape[-2:]
        block = (rows // steps, cols)
        out_specs.append(pl.BlockSpec(block, lambda j: (j, 0)))
        if i < 2:
            in_specs.append(pl.BlockSpec(block, lambda j: (j, 0)))
            out_shape.append(jax.ShapeDtypeStruct((rows, cols), array.dtype))
        else:
            in_specs.append(pl.BlockSpec((array.shape[0],) + block, lambda j: (0, j, 0)))
            out_shape.append(jax.ShapeDtypeStruct((rows, cols), F32))
    return pl.pallas_call(
        last_sums_kernel, grid=(steps,), in_specs=in_specs, out_specs=out_specs,
        out_shape=out_shape,
    )(*arrays)


def per_device_fast(
    layer_input, lengths, cotangent, ln1_gain, ln1_bias, ln2_gain, ln2_bias,
    qkv_weight, qkv_bias, out_weight, gate_weight, up_weight, down_weight,
):
    dp, sp = lax.axis_size("dp"), lax.axis_size("sp")
    z = lax.axis_index("sp")
    _, slots, width = layer_input.shape
    plan = Plan(dp, sp, slots, width, gate_weight.shape[1])
    sem_at = {}
    for name in WEIGHTS:
        sem_at["w_" + name] = plan.sems(8, dp)
        sem_at["g_" + name] = plan.sems(7, 8)
    split = (("o", PARTS_FORWARD), ("n", PARTS_BACK), ("i", PARTS_LAST))
    gathers = (("n", PARTS_FORWARD), ("b", PARTS_BACK))
    for name in ["ag_x", "ag_d"] + ["ag_%s%d" % (n, h) for n, k in gathers for h in range(k)]:
        sem_at[name] = plan.sems(2 + 2 * sp, 2 * sp)
    for name in ["rs_m"] + ["rs_%s%d" % (n, h) for n, k in split for h in range(k)]:
        sem_at[name] = plan.sems(2 * sp, 2 * sp + 1)
    for name in ("sm_z", "su_z"):
        sem_at[name] = plan.sems(sp, sp)
    for name in ("sm_d", "su_d"):
        sem_at[name] = plan.sems(dp, dp)

    even = z % 2 == 0
    norms = jnp.stack([ln1_gain, ln1_bias, ln2_gain, ln2_bias]).astype(F32)
    none = jnp.zeros_like(norms)
    norm_rows = jnp.where(
        even, jnp.concatenate([norms, none], 1), jnp.concatenate([none, norms], 1)
    )
    bias = qkv_bias.astype(F32)
    none = jnp.zeros_like(bias)
    bias_rows = jnp.where(
        even, jnp.concatenate([bias, none]), jnp.concatenate([none, bias])
    ).reshape(3, 128)
    len_row = jnp.broadcast_to(lengths.astype(F32)[:, None], (1, 128))
    small = jnp.concatenate([norm_rows, bias_rows, len_row], axis=0)
    cosine, sine = rotary_lanes(sp * slots)

    vmem = pl.BlockSpec(memory_space=pltpu.VMEM)
    hbm = pl.BlockSpec(memory_space=pl.ANY)
    out_shape = [
        jax.ShapeDtypeStruct((slots, width), BF16),
        jax.ShapeDtypeStruct((slots, width), F32),
        jax.ShapeDtypeStruct((8, plan.shard + 128), F32),
        jax.ShapeDtypeStruct((3,) + qkv_weight.shape, BF16),
        jax.ShapeDtypeStruct((3,) + out_weight.shape, BF16),
        jax.ShapeDtypeStruct((3,) + gate_weight.shape, BF16),
        jax.ShapeDtypeStruct((3,) + up_weight.shape, BF16),
        jax.ShapeDtypeStruct((3,) + down_weight.shape, BF16),
        jax.ShapeDtypeStruct((plan.tokens, width), BF16),
    ]
    tokens, heads, ff = plan.tokens, plan.head_cols, plan.ff_wide
    scratch = [
        pltpu.SemaphoreType.DMA((plan.count_send,)),
        pltpu.SemaphoreType.DMA((plan.count_recv,)),
        pltpu.SemaphoreType.DMA((2 * len(WEIGHTS) + 2,)),
        pltpu.VMEM((width, plan.qkv_cols), BF16),
        pltpu.VMEM((heads, width), BF16),
        pltpu.VMEM((width, ff), BF16),
        pltpu.VMEM((width, ff), BF16),
        pltpu.VMEM((width, ff), BF16),
        pltpu.VMEM((tokens, width), BF16),
        pltpu.VMEM((tokens, width), BF16),
        pltpu.VMEM((tokens, width), BF16),
        pltpu.VMEM((tokens, width), BF16),
        pltpu.VMEM((sp * slots, width), BF16),
        pltpu.VMEM(((sp + 1) * slots, width), BF16),
        pltpu.VMEM((tokens, width), BF16),
        pltpu.VMEM((sp * slots, width), BF16),
        pltpu.VMEM(((sp + 1) * slots, width), BF16),
        pltpu.VMEM((2, plan.pairs, plan.seq, 128), BF16),
        pltpu.VMEM((2, plan.pairs, plan.seq, 128), BF16),
        pltpu.VMEM((2, plan.pairs, plan.seq, 128), BF16),
        pltpu.VMEM((tokens, heads), BF16),
        pltpu.VMEM((tokens, ff), BF16),
        pltpu.VMEM((tokens, ff), BF16),
        pltpu.VMEM((tokens, ff), BF16),
        pltpu.VMEM((slots, width), F32),
        pltpu.VMEM((slots, width), F32),
        pltpu.VMEM((slots, width), F32),
        pltpu.VMEM((dp, sp, 8, 128), F32),
        pltpu.VMEM((8, width), F32),
        pltpu.VMEM((8, plan.qkv_cols), F32),
        pltpu.VMEM((8, 128), F32),
        pltpu.VMEM((8, width), F32),
        pltpu.VMEM((8, 128), F32),
        pltpu.VMEM((dp, 8, plan.shard + 128), F32),
        pltpu.VMEM((dp, 8, plan.shard + 128), F32),
        pltpu.VMEM((sp, 8, plan.shard + 128), F32),
        pltpu.VMEM((2, plan.shard, plan.qkv_cols), BF16),
        pltpu.VMEM((2, heads, plan.shard), BF16),
        pltpu.VMEM((2, plan.shard, ff), BF16),
        pltpu.VMEM((2, plan.shard, ff), BF16),
        pltpu.VMEM((2, plan.shard, ff), BF16),
    ]
    outs = pl.pallas_call(
        functools.partial(layer_kernel, plan, sem_at),
        out_shape=out_shape,
        in_specs=[vmem] * 5 + [hbm] * 5,
        out_specs=[vmem] * 3 + [hbm] * 6,
        scratch_shapes=scratch,
        compiler_params=pltpu.CompilerParams(
            collective_id=0, has_side_effects=True, vmem_limit_bytes=63 * 1024 * 1024
        ),
    )(
        layer_input[0], cotangent[0], small, jnp.asarray(cosine), jnp.asarray(sine),
        qkv_weight, out_weight, gate_weight, up_weight, down_weight,
    )
    sums = outs[2]
    own = lax.dynamic_slice_in_dim(sums[:4, : plan.shard], z * (plan.shard // sp), plan.shard // sp, 1)
    bias_grad = lax.dynamic_slice_in_dim(
        sums[:, plan.shard :].reshape(-1), z * qkv_bias.shape[0], qkv_bias.shape[0]
    )
    done = last_sums(outs[0], outs[1], *outs[3:8])
    return (
        done[0][None], done[1][None], own[0], own[1], own[2], own[3],
        done[2], bias_grad, done[3], done[4], done[5], done[6],
    )


def solution(mesh):
    placed = (
        P("dp", "sp", None),
        P("dp"),
        P("dp", "sp", None),
        P(("dp", "sp")),
        P(("dp", "sp")),
        P(("dp", "sp")),
        P(("dp", "sp")),
        P("dp", "sp"),
        P(("dp", "sp")),
        P("sp", "dp"),
        P("dp", "sp"),
        P("dp", "sp"),
        P("dp", "sp"),
    )
    fast = mesh.shape["dp"] == 8 and mesh.shape["sp"] == 4
    return jax.shard_map(
        per_device_fast if fast else per_device,
        mesh=mesh,
        in_specs=placed,
        out_specs=(
            P("dp", "sp", None),
            P("dp", "sp", None),
            P(("dp", "sp")),
            P(("dp", "sp")),
            P(("dp", "sp")),
            P(("dp", "sp")),
            P("dp", "sp"),
            P(("dp", "sp")),
            P("sp", "dp"),
            P("dp", "sp"),
            P("dp", "sp"),
            P("dp", "sp"),
        ),
        check_vma=False,
    )
```

```python
import functools

import jax
import jax.numpy as jnp
import numpy as np
from jax import lax
from jax.experimental import pallas as pl
from jax.experimental.pallas import tpu as pltpu
from jax.sharding import PartitionSpec as P

HEAD_DIM = 64
ROT = 16
F32 = jnp.float32
BF16 = jnp.bfloat16
MESH = pl.DeviceIdType.MESH


eps_norm = 1e-05
theta = 10000.0
neg_large = -1e30


def norm_forward(hidden, gain, bias):
    centre = hidden - jnp.mean(hidden, axis=-1, keepdims=True)
    rstd = lax.rsqrt(jnp.mean(centre * centre, axis=-1, keepdims=True) + eps_norm)
    normed = centre * rstd
    return (normed * gain + bias, normed, rstd)


def norm_backward(grad, normed, rstd, gain):
    gain_grad = jnp.sum(grad * normed, axis=0)
    bias_grad = jnp.sum(grad, axis=0)
    scaled = grad * gain
    input_part = rstd * (
        scaled
        - jnp.mean(scaled, axis=-1, keepdims=True)
        - normed * jnp.mean(scaled * normed, axis=-1, keepdims=True)
    )
    return (input_part, gain_grad, bias_grad)


def rotate(tensor, cosine, sine, direction):
    half_rot = ROT // 2
    first = tensor[..., :half_rot]
    second = tensor[..., half_rot:ROT]
    cos_part = cosine[None, :, None, :]
    sin_part = sine[None, :, None, :] * direction
    return jnp.concatenate(
        [
            first * cos_part - second * sin_part,
            second * cos_part + first * sin_part,
            tensor[..., ROT:],
        ],
        axis=-1,
    )


def rotary_tables(position_list):
    freq = theta ** (-(jnp.arange(ROT // 2, dtype=jnp.float32) * 2.0) / ROT)
    angles = position_list.astype(jnp.float32)[:, None] * freq[None, :]
    return (jnp.cos(angles), jnp.sin(angles))


def contract_rows(left, right):
    return lax.dot_general(
        left, right, (((0,), (0,)), ((), ())), preferred_element_type=jnp.float32
    )


def contract_cols(left, right):
    return lax.dot_general(
        left, right, (((1,), (1,)), ((), ())), preferred_element_type=jnp.float32
    )


def block_scores(query_block, keys, first_row, length, block_rows):
    softmax_scale = HEAD_DIM ** (-0.5)
    key_pos = jnp.arange(keys.shape[0], dtype=jnp.int32)
    query_pos = first_row + jnp.arange(block_rows, dtype=jnp.int32)
    scores = (
        jnp.einsum("qhd,khd->hqk", query_block, keys, preferred_element_type=jnp.float32)
        * softmax_scale
    )
    allowed = (key_pos[None, :] <= query_pos[:, None]) & (key_pos < length)[None, :]
    return jnp.where(allowed[None], scores, neg_large)


def attend_forward(queries, keys, values, length, block_rows):

    def one_block(block_index):
        first_row = block_index * block_rows
        query_block = lax.dynamic_slice_in_dim(queries, first_row, block_rows, 0)
        scores = block_scores(query_block, keys, first_row, length, block_rows)
        top_score = jnp.max(scores, axis=-1, keepdims=True)
        total = jnp.sum(jnp.exp(scores - top_score), axis=-1, keepdims=True)
        log_total = top_score + jnp.log(total)
        attn_weights = jnp.exp(scores - log_total).astype(jnp.bfloat16)
        result = jnp.einsum(
            "hqk,khd->qhd", attn_weights, values, preferred_element_type=jnp.float32
        )
        return (result.astype(jnp.bfloat16), log_total[..., 0])

    results, log_totals = lax.map(
        one_block, jnp.arange(queries.shape[0] // block_rows, dtype=jnp.int32)
    )
    return (results.reshape(queries.shape), log_totals)


def attend_backward(queries, keys, values, grad_out, log_totals, length, block_rows):
    softmax_scale = HEAD_DIM ** (-0.5)

    def one_block(carry, block_index):
        key_grad, value_grad = carry
        first_row = block_index * block_rows
        query_block = lax.dynamic_slice_in_dim(queries, first_row, block_rows, 0)
        grad_block = lax.dynamic_slice_in_dim(grad_out, first_row, block_rows, 0)
        scores = block_scores(query_block, keys, first_row, length, block_rows)
        weights_full = jnp.exp(scores - log_totals[block_index][..., None])
        attn_weights = weights_full.astype(jnp.bfloat16)
        weight_grad = jnp.einsum(
            "qhd,khd->hqk", grad_block, values, preferred_element_type=jnp.float32
        )
        delta = jnp.sum(weight_grad * weights_full, axis=-1, keepdims=True)
        score_grad = (weights_full * (weight_grad - delta)).astype(jnp.bfloat16)
        query_grad = (
            jnp.einsum("hqk,khd->qhd", score_grad, keys, preferred_element_type=jnp.float32)
            * softmax_scale
        )
        key_grad = (
            key_grad
            + jnp.einsum(
                "hqk,qhd->khd", score_grad, query_block, preferred_element_type=jnp.float32
            )
            * softmax_scale
        )
        value_grad = value_grad + jnp.einsum(
            "hqk,qhd->khd", attn_weights, grad_block, preferred_element_type=jnp.float32
        )
        return ((key_grad, value_grad), query_grad)

    zeros = jnp.zeros(keys.shape, jnp.float32)
    (key_grad, value_grad), query_grad = lax.scan(
        one_block, (zeros, zeros), jnp.arange(queries.shape[0] // block_rows, dtype=jnp.int32)
    )
    return (query_grad.reshape(queries.shape), key_grad, value_grad)


def feed_forward(tokens, grads_out, w_gate, w_up, w_down):
    gate = jnp.dot(tokens, w_gate, preferred_element_type=jnp.float32)
    up_proj = jnp.dot(tokens, w_up, preferred_element_type=jnp.float32)
    sigmoid_gate = jax.nn.sigmoid(gate)
    silu_gate = gate * sigmoid_gate
    hidden_act = (silu_gate * up_proj).astype(jnp.bfloat16)
    mixed = contract_cols(hidden_act, w_down)
    act_grad = jnp.dot(grads_out, w_down, preferred_element_type=jnp.float32)
    up_grad = (act_grad * silu_gate).astype(jnp.bfloat16)
    gate_grad = (act_grad * up_proj * sigmoid_gate * (1.0 + gate * (1.0 - sigmoid_gate))).astype(
        jnp.bfloat16
    )
    token_grad = contract_cols(gate_grad, w_gate) + contract_cols(up_grad, w_up)
    weight_grads = (
        contract_rows(tokens, gate_grad),
        contract_rows(tokens, up_grad),
        contract_rows(grads_out, hidden_act),
    )
    return (mixed, token_grad, weight_grads)


def per_device(
    layer_input,
    lengths,
    cotangent,
    ln1_gain,
    ln1_bias,
    ln2_gain,
    ln2_bias,
    qkv_weight,
    qkv_bias,
    out_weight,
    gate_weight,
    up_weight,
    down_weight,
):
    row_count, slot_count, width = layer_input.shape
    sp_count = lax.axis_size("sp")
    sp_index = lax.axis_index("sp")
    tokens_dev = row_count * slot_count
    seq_len = slot_count * sp_count
    block_rows = min(512, seq_len)
    local_width = width // sp_count
    local_heads = local_width // HEAD_DIM
    local_cols = 3 * local_width
    positions = sp_index * slot_count + jnp.arange(slot_count, dtype=jnp.int32)
    valid = (positions[None, :] < lengths[:, None]).astype(jnp.float32).reshape(tokens_dev, 1)
    small = (
        lax.all_gather(ln1_gain, ("dp", "sp"), axis=0, tiled=True),
        lax.all_gather(ln1_bias, ("dp", "sp"), axis=0, tiled=True),
        lax.all_gather(ln2_gain, ("dp", "sp"), axis=0, tiled=True),
        lax.all_gather(ln2_bias, ("dp", "sp"), axis=0, tiled=True),
        lax.all_gather(qkv_bias, ("dp", "sp"), axis=0, tiled=True),
    )
    gain_one = small[0].astype(jnp.float32)
    bias_one = small[1].astype(jnp.float32)
    gain_two = small[2].astype(jnp.float32)
    bias_two = small[3].astype(jnp.float32)
    b_qkv = small[4].astype(jnp.float32)
    qkv_cols, out_rows, gate_cols, up_cols, down_cols = (
        lax.all_gather(qkv_weight, "dp", axis=0, tiled=True),
        lax.all_gather(out_weight, "dp", axis=1, tiled=True),
        lax.all_gather(gate_weight, "dp", axis=0, tiled=True),
        lax.all_gather(up_weight, "dp", axis=0, tiled=True),
        lax.all_gather(down_weight, "dp", axis=0, tiled=True),
    )
    w_gate, w_up, w_down = (gate_cols, up_cols, down_cols)
    hidden_in = layer_input.astype(jnp.float32).reshape(tokens_dev, width)
    normed_one, unit_one, rstd_one = norm_forward(hidden_in, gain_one, bias_one)
    normed_one = normed_one.astype(jnp.bfloat16)
    cosine, sine = rotary_tables(jnp.arange(seq_len, dtype=jnp.int32))
    row_normed = lax.all_gather(
        normed_one.reshape(row_count, slot_count, width), "sp", axis=1, tiled=True
    ).reshape(row_count * seq_len, width)
    bias_local = lax.dynamic_slice_in_dim(b_qkv, sp_index * local_cols, local_cols)
    qkv_raw = (
        jnp.dot(row_normed, qkv_cols, preferred_element_type=jnp.float32) + bias_local
    ).reshape(row_count, seq_len, local_heads, 3, HEAD_DIM)
    query_heads = (
        rotate(qkv_raw[:, :, :, 0], cosine, sine, 1.0)
        .astype(jnp.bfloat16)
        .reshape(row_count, seq_len, local_width)
    )
    key_heads = (
        rotate(qkv_raw[:, :, :, 1], cosine, sine, 1.0)
        .astype(jnp.bfloat16)
        .reshape(row_count, seq_len, local_width)
    )
    value_heads = qkv_raw[:, :, :, 2].astype(jnp.bfloat16).reshape(row_count, seq_len, local_width)
    head_shape = (seq_len, local_heads, HEAD_DIM)

    def forward_row(row_data):
        row_query, row_key, row_value, row_length = row_data
        return attend_forward(
            row_query.reshape(head_shape),
            row_key.reshape(head_shape),
            row_value.reshape(head_shape),
            row_length,
            block_rows,
        )

    attended_heads, log_totals = lax.map(
        forward_row, (query_heads, key_heads, value_heads, lengths)
    )
    attended_heads = attended_heads.reshape(row_count, seq_len, local_width)
    attended_flat = attended_heads.reshape(row_count * seq_len, local_width)
    branch_part = jnp.dot(attended_flat, out_rows, preferred_element_type=jnp.float32).reshape(
        row_count, seq_len, width
    )
    branch = lax.psum_scatter(branch_part, "sp", scatter_dimension=1, tiled=True).reshape(
        tokens_dev, width
    )
    resid = hidden_in + branch
    normed_two, unit_two, rstd_two = norm_forward(resid, gain_two, bias_two)
    normed_two = normed_two.astype(jnp.bfloat16)
    out_grad = (cotangent.astype(jnp.float32).reshape(tokens_dev, width) * valid).astype(
        jnp.bfloat16
    )
    row_tokens, row_grads = (
        lax.all_gather(normed_two.reshape(row_count, slot_count, width), "sp", axis=1, tiled=True),
        lax.all_gather(out_grad.reshape(row_count, slot_count, width), "sp", axis=1, tiled=True),
    )
    mixed_part, token_grad_part, mlp_grads = feed_forward(
        row_tokens.reshape(row_count * seq_len, width),
        row_grads.reshape(row_count * seq_len, width),
        w_gate,
        w_up,
        w_down,
    )
    mixed, normed_two_grad = (
        lax.psum_scatter(
            mixed_part.reshape(row_count, seq_len, width), "sp", scatter_dimension=1, tiled=True
        ),
        lax.psum_scatter(
            token_grad_part.reshape(row_count, seq_len, width),
            "sp",
            scatter_dimension=1,
            tiled=True,
        ),
    )
    mixed = mixed.reshape(tokens_dev, width)
    normed_two_grad = normed_two_grad.reshape(tokens_dev, width)
    layer_output = (
        (valid * (resid + mixed)).astype(jnp.bfloat16).reshape(row_count, slot_count, width)
    )
    resid_part, gain_two_grad, bias_two_grad = norm_backward(
        normed_two_grad, unit_two, rstd_two, gain_two
    )
    resid_grad = out_grad.astype(jnp.float32) + resid_part
    branch_grad = resid_grad.astype(jnp.bfloat16)
    row_branch = lax.all_gather(
        branch_grad.reshape(row_count, slot_count, width), "sp", axis=1, tiled=True
    ).reshape(row_count * seq_len, width)
    out_weight_grad = contract_rows(attended_flat, row_branch)
    attended_grad_heads = (
        contract_cols(row_branch, out_rows)
        .astype(jnp.bfloat16)
        .reshape(row_count, seq_len, local_width)
    )

    def backward_row(row_data):
        row_query, row_key, row_value, row_grad, row_totals, row_length = row_data
        query_grad, key_grad, value_grad = attend_backward(
            row_query.reshape(head_shape),
            row_key.reshape(head_shape),
            row_value.reshape(head_shape),
            row_grad.reshape(head_shape),
            row_totals,
            row_length,
            block_rows,
        )
        return (
            query_grad.astype(jnp.bfloat16).reshape(seq_len, local_width),
            key_grad.astype(jnp.bfloat16).reshape(seq_len, local_width),
            value_grad.astype(jnp.bfloat16).reshape(seq_len, local_width),
        )

    query_grads, key_grads, value_grads = lax.map(
        backward_row,
        (query_heads, key_heads, value_heads, attended_grad_heads, log_totals, lengths),
    )
    row_shape = (row_count, seq_len, local_heads, HEAD_DIM)
    query_raw = rotate(query_grads.astype(jnp.float32).reshape(row_shape), cosine, sine, -1.0)
    key_raw = rotate(key_grads.astype(jnp.float32).reshape(row_shape), cosine, sine, -1.0)
    value_raw = value_grads.astype(jnp.float32).reshape(row_shape)
    qkv_grad = (
        jnp.stack([query_raw, key_raw, value_raw], axis=3)
        .reshape(row_count * seq_len, local_cols)
        .astype(jnp.bfloat16)
    )
    bias_local_grad = jnp.sum(qkv_grad.astype(jnp.float32), axis=0)
    qkv_bias_full = lax.dynamic_update_slice(
        jnp.zeros((3 * width,), jnp.float32), bias_local_grad, (sp_index * local_cols,)
    )
    qkv_weight_grad = contract_rows(row_normed, qkv_grad)
    normed_part = contract_cols(qkv_grad, qkv_cols).reshape(row_count, seq_len, width)
    normed_one_grad = (
        lax.psum_scatter(normed_part.astype(jnp.bfloat16), "sp", scatter_dimension=1, tiled=True)
        .astype(jnp.float32)
        .reshape(tokens_dev, width)
    )
    input_part, gain_one_grad, bias_one_grad = norm_backward(
        normed_one_grad, unit_one, rstd_one, gain_one
    )
    input_grad = (resid_grad + input_part).reshape(row_count, slot_count, width)
    small_sums = (
        lax.psum_scatter(gain_one_grad, ("dp", "sp"), scatter_dimension=0, tiled=True),
        lax.psum_scatter(bias_one_grad, ("dp", "sp"), scatter_dimension=0, tiled=True),
        lax.psum_scatter(gain_two_grad, ("dp", "sp"), scatter_dimension=0, tiled=True),
        lax.psum_scatter(bias_two_grad, ("dp", "sp"), scatter_dimension=0, tiled=True),
        lax.psum_scatter(qkv_bias_full, ("dp", "sp"), scatter_dimension=0, tiled=True),
    )
    row_sums = (
        lax.psum_scatter(
            qkv_weight_grad.astype(jnp.bfloat16), "dp", scatter_dimension=0, tiled=True
        ).astype(jnp.float32),
        lax.psum_scatter(
            out_weight_grad.astype(jnp.bfloat16), "dp", scatter_dimension=1, tiled=True
        ).astype(jnp.float32),
        lax.psum_scatter(
            mlp_grads[0].astype(jnp.bfloat16), "dp", scatter_dimension=0, tiled=True
        ).astype(jnp.float32),
        lax.psum_scatter(
            mlp_grads[1].astype(jnp.bfloat16), "dp", scatter_dimension=0, tiled=True
        ).astype(jnp.float32),
        lax.psum_scatter(
            mlp_grads[2].astype(jnp.bfloat16), "dp", scatter_dimension=0, tiled=True
        ).astype(jnp.float32),
    )
    return (
        layer_output,
        input_grad,
        small_sums[0],
        small_sums[1],
        small_sums[2],
        small_sums[3],
        row_sums[0],
        small_sums[4],
        row_sums[1],
        row_sums[2],
        row_sums[3],
        row_sums[4],
    )


def dot_nn(left, right):
    return lax.dot_general(left, right, (((1,), (0,)), ((), ())), preferred_element_type=F32)


def dot_nt(left, right):
    return lax.dot_general(left, right, (((1,), (1,)), ((), ())), preferred_element_type=F32)


def dot_tn(left, right):
    return lax.dot_general(left, right, (((0,), (0,)), ((), ())), preferred_element_type=F32)


def iota(shape, dim):
    return lax.broadcasted_iota(jnp.int32, shape, dim)


def tile(index, size):
    return pl.ds(pl.multiple_of(index * size, size), size)


def normalize(hidden):
    centre = hidden - jnp.mean(hidden, axis=-1, keepdims=True)
    rstd = lax.rsqrt(jnp.mean(centre * centre, axis=-1, keepdims=True) + eps_norm)
    return centre * rstd, rstd


class Plan:
    def __init__(self, dp, sp, slots, width, ff_cols):
        self.dp, self.sp, self.slots, self.width = dp, sp, slots, width
        self.chips = dp // 2
        self.chunk = 2 * slots
        self.tokens = sp * self.chunk
        self.seq = sp * slots
        self.shard = width // dp
        self.head_cols = width // sp // 2
        self.pairs = self.head_cols // 128
        self.qkv_cols = 3 * self.head_cols
        self.ff_cols = ff_cols
        lanes = ff_cols // 128
        self.ff_wide = -(-lanes // 2) * 128
        self.ff_slim = ff_cols - self.ff_wide
        self.count_send = 0
        self.count_recv = 0

    def sems(self, send, recv):
        at = (self.count_send, self.count_recv)
        self.count_send += send
        self.count_recv += recv
        return at


def layer_kernel(plan, sem_at, *refs):
    (
        x_in, cot_in, small_in, cos_in, sin_in, wqkv_in, wout_in, wg_in, wu_in, wd_in,
        out_ref, grad_ref, sums_ref, rg_qkv, rg_out, rg_gate, rg_up, rg_down, n1_hbm,
        ssem, rsem, lsem,
        w_qkv, w_out, w_gate, w_up, w_down,
        buf_a, buf_b, buf_c,
        part, part_x, part_r, mix, mix_x, mix_r,
        q_ref, k_ref, v_ref, att,
        act, dgate, dup,
        resid, acc, dres,
        small, vecs, qbias, lens, colsum, biassum, send_sum, recv_sum, z_sum,
        st_qkv, st_out, st_gate, st_up, st_down,
    ) = refs
    sp, dp, slots, width, chunk = plan.sp, plan.dp, plan.slots, plan.width, plan.chunk
    d = lax.axis_index("dp")
    z = lax.axis_index("sp")
    c = d % 2
    oc = 1 - c
    chip = d // 2
    sib = (d + 1 - 2 * c, z)
    first_row = c * slots
    last = sp - 1

    def remote(src, dst, si, ri, dev):
        return pltpu.make_async_remote_copy(
            src_ref=src, dst_ref=dst, send_sem=ssem.at[si], recv_sem=rsem.at[ri],
            device_id=dev, device_id_type=MESH,
        )

    def wait_send(src, si):
        remote(src, src, si, 0, sib).wait_send()

    def wait_recv(dst, ri):
        remote(dst, dst, 0, ri, sib).wait_recv()

    def block(buf, t, core):
        return buf.at[pl.ds(pl.multiple_of(t * chunk + core * slots, slots), slots)]

    def sub_block(buf, t, core, at):
        start, size = at
        return buf.at[pl.ds(pl.multiple_of(t * chunk + core * slots + start, size), size)]

    def rows_of(buf, t):
        return buf.at[tile(t, chunk)]

    def spans(size, step):
        return [slice(i, min(i + step, size)) for i in range(0, size, step)]

    def slot_block(buf, t, at):
        start, size = at
        return buf.at[pl.ds(pl.multiple_of(t * slots + start, size), size)]

    whole = (0, slots)
    def parts(count):
        return [(h * (slots // count), slots // count) for h in range(count)]


    barrier = pltpu.get_barrier_semaphore()
    for i in range(1, dp):
        pl.semaphore_signal(barrier, inc=1, device_id=((d + i) % dp, z), device_id_type=MESH)
    for i in range(1, sp):
        pl.semaphore_signal(barrier, inc=1, device_id=(d, (z + i) % sp), device_id_type=MESH)
    pl.semaphore_wait(barrier, dp + sp - 2)

    class Gather:
        def __init__(self, name, buf, at=whole):
            self.s, self.r = sem_at[name]
            self.buf, self.at = buf, at

        def start(self, own):
            s, r = self.s, self.r
            dst = sub_block(self.buf, z, c, self.at)

            @pl.when(z < last)
            def _():
                remote(own, dst, s, r + z, (d, z + 1)).start()

            @pl.when(z > 0)
            def _():
                remote(own, dst, s + 1, r + z, (d, z - 1)).start()

            remote(own, dst, s + 2 + sp + z, r + sp + z, sib).start()

        def hop(self, k):
            s, r = self.s, self.r
            for sign in (-1, 1):
                t = z + sign * k
                nxt = z - sign
                blk = sub_block(self.buf, t, c, self.at)

                @pl.when((t >= 0) & (t <= last))
                def _():
                    wait_recv(blk, r + t)

                    @pl.when((nxt >= 0) & (nxt <= last))
                    def _():
                        remote(blk, blk, s + 2 + t, r + t, (d, nxt)).start()

                    remote(blk, blk, s + 2 + sp + t, r + sp + t, sib).start()

        def need(self, t):
            wait_recv(sub_block(self.buf, t, oc, self.at), self.r + sp + t)

        def drain(self, own):
            s = self.s

            @pl.when(z < last)
            def _():
                wait_send(own, s)

            @pl.when(z > 0)
            def _():
                wait_send(own, s + 1)

            for t in range(sp):
                wait_send(own, s + 2 + sp + t)

                @pl.when(((t < z) & (z < last)) | ((t > z) & (z > 0)))
                def _():
                    wait_send(own, s + 2 + t)

    def order(i):
        low = jnp.minimum(z, last - z)
        k = jnp.where(i <= 2 * low, (i + 1) // 2, i - low)
        paired = jnp.where(i % 2 == 1, z - k, z + k)
        single = jnp.where(z < last - z, z + k, z - k)
        return jnp.where(i <= 2 * low, paired, single)

    def add_into(dst, terms):
        @pl.loop(0, dst.shape[0] // ADD_ROWS)
        def _(i):
            sl = tile(i, ADD_ROWS)
            total = dst[sl, :].astype(F32)
            for term in terms:
                total = total + term[sl, :].astype(F32)
            dst[sl, :] = total.astype(dst.dtype)

    class Scatter:
        def __init__(self, name, parts, from_core, from_line, at=whole):
            self.s, self.r = sem_at[name]
            self.p, self.x, self.l, self.at = parts, from_core, from_line, at

        def core(self, t):
            remote(
                sub_block(self.p, t, oc, self.at), slot_block(self.x, t, self.at), self.s + t, self.r + t, sib
            ).start()

        def send(self, t, from_end, nbr, slot):
            mine = sub_block(self.p, t, c, self.at)
            xs = slot_block(self.x, t, self.at)
            wait_recv(xs, self.r + t)

            @pl.when(from_end)
            def _():
                add_into(mine, [xs])

            @pl.when(jnp.logical_not(from_end))
            def _():
                ls = slot_block(self.l, t, self.at)
                wait_recv(ls, self.r + sp + t)
                add_into(mine, [xs, ls])

            remote(
                mine, slot_block(self.l, slot, self.at), self.s + sp + t, self.r + sp + slot, (d, nbr)
            ).start()

        def step(self, n):
            left = n - (last - z)

            @pl.when((left >= 0) & (left < z))
            def _():
                self.send(left, z == last, z - 1, left)

            right = n - z

            @pl.when((right >= 0) & (right < last - z))
            def _():
                t = last - right
                self.send(t, z == 0, z + 1, jnp.where(t == z + 1, sp, t))

        def final(self, total):
            total = total.at[pl.ds(*self.at)]
            mine = sub_block(self.p, z, c, self.at)
            xs = slot_block(self.x, z, self.at)
            wait_recv(xs, self.r + z)

            @pl.loop(0, self.at[1] // ADD_ROWS)
            def _(i):
                sl = tile(i, ADD_ROWS)
                total[sl, :] = mine[sl, :].astype(F32) + xs[sl, :].astype(F32)

            @pl.when(z < last)
            def _():
                ls = slot_block(self.l, z, self.at)
                wait_recv(ls, self.r + sp + z)
                add_into(total, [ls])

            @pl.when(z > 0)
            def _():
                ls = slot_block(self.l, sp, self.at)
                wait_recv(ls, self.r + sp + sp)
                add_into(total, [ls])

        def drain(self):
            for t in range(sp):
                wait_send(slot_block(self.x, t, self.at), self.s + t)

                @pl.when(t != z)
                def _():
                    wait_send(slot_block(self.x, t, self.at), self.s + sp + t)

    def chip_target(q):
        cx, cy = chip % 2, chip // 2
        if q % 2:
            cx = 1 - cx
        if q // 2:
            cy = 1 - cy
        return 2 * cx + 4 * cy

    def weight_window(name, src, core):
        if name == "out":
            half = plan.head_cols
            return src.at[pl.ds(core * half, half), :]
        if name == "qkv":
            return src.at[:, pl.ds(core * plan.qkv_cols, plan.qkv_cols)]
        return src.at[:, pl.ds(core * plan.ff_wide, plan.ff_slim if core else plan.ff_wide)]

    def weight_place(name, dst, owner, core):
        if name == "out":
            return dst.at[:, tile(owner, plan.shard)]
        if name == "qkv":
            return dst.at[tile(owner, plan.shard), :]
        return dst.at[tile(owner, plan.shard), pl.ds(0, plan.ff_slim if core else plan.ff_wide)]

    def weight_send(name, src, dst):
        s, r = sem_at["w_" + name]
        for q in (1, 2, 0):
            for core in (0, 1):
                target = chip_target(q) + core
                here = weight_window(name, src, core)
                there = weight_place(name, dst, d, core)
                if q:
                    remote(here, there, s + 2 * q + core, r + d, (target, z)).start()
                else:

                    @pl.when(c != core)
                    def _():
                        remote(here, there, s + core, r + d, (target, z)).start()

                    @pl.when(c == core)
                    def _():
                        pltpu.make_async_copy(here, there, lsem.at[WEIGHTS.index(name)]).start()

    def weight_forward(name, dst):
        s, r = sem_at["w_" + name]
        for core in (0, 1):

            @pl.when(c == core)
            def _():
                for k in (0, 1):
                    owner = chip_target(1 if core else 2) + k
                    place = weight_place(name, dst, owner, core)
                    wait_recv(place, r + owner)
                    target = chip_target(2 if core else 1) + core
                    remote(place, place, s + 6 + k, r + owner, (target, z)).start()

    def weight_wait(name, src, dst):
        _, r = sem_at["w_" + name]
        for core in (0, 1):

            @pl.when(c == core)
            def _():
                for q in (0, 2 if core else 1, 3):
                    for k in (0, 1):
                        if q or k != core:
                            owner = chip_target(q) + k
                            wait_recv(weight_place(name, dst, owner, core), r + owner)
                pltpu.make_async_copy(
                    weight_window(name, src, core), weight_place(name, dst, d, core),
                    lsem.at[WEIGHTS.index(name)],
                ).wait()

    def weight_drain(name, src, dst):
        s, _ = sem_at["w_" + name]
        for core in (0, 1):
            here = weight_window(name, src, core)
            wait_send(here, s + 2 + core)
            wait_send(here, s + 4 + core)

            @pl.when(c != core)
            def _():
                wait_send(here, s + core)

            @pl.when(c == core)
            def _():
                place = weight_place(name, dst, d, core)
                wait_send(place, s + 6)
                wait_send(place, s + 7)

    def wgrad_piece(name, src, owner, core):
        if name == "out":
            return src.at[:, tile(owner, plan.shard)]
        if name == "qkv":
            return src.at[tile(owner, plan.shard), :]
        return src.at[tile(owner, plan.shard), pl.ds(0, plan.ff_slim if core else plan.ff_wide)]

    def wgrad_place(name, dst, slot, core):
        if name == "out":
            return dst.at[slot, pl.ds(core * plan.head_cols, plan.head_cols), :]
        if name == "qkv":
            return dst.at[slot, :, pl.ds(core * plan.qkv_cols, plan.qkv_cols)]
        return dst.at[slot, :, pl.ds(core * plan.ff_wide, plan.ff_slim if core else plan.ff_wide)]

    def stage_place(name, stage, k, core):
        if name in ("out", "qkv"):
            return stage.at[k]
        return stage.at[k, :, pl.ds(0, plan.ff_slim if core else plan.ff_wide)]

    def wgrad_send(name, src, dst, stage):
        s, r = sem_at["g_" + name]
        for core in (0, 1):
            near = 1 if core else 2

            @pl.when(c == core)
            def _():
                for k in (0, 1):
                    remote(
                        wgrad_piece(name, src, chip_target(3) + k, core),
                        stage_place(name, stage, k, core),
                        s + k, r + 6 + k, (chip_target(near) + core, z),
                    ).start()
                for k in (0, 1):
                    target = chip_target(near) + k
                    remote(
                        wgrad_piece(name, src, target, core),
                        wgrad_place(name, dst, near, core),
                        s + 2 + k, r + 2 * near + core, (target, z),
                    ).start()
                remote(
                    wgrad_piece(name, src, d + 1 - 2 * core, core),
                    wgrad_place(name, dst, 0, core), s + 4, r + core, sib,
                ).start()
                pltpu.make_async_copy(
                    wgrad_piece(name, src, d, core), wgrad_place(name, dst, 0, core),
                    lsem.at[len(WEIGHTS) + WEIGHTS.index(name)],
                ).start()

    def wgrad_merge(name, src, dst, stage):
        s, r = sem_at["g_" + name]
        for core in (0, 1):
            far = 2 if core else 1

            @pl.when(c == core)
            def _():
                for k in (0, 1):
                    target = chip_target(far) + k
                    came = stage_place(name, stage, k, core)
                    mine = wgrad_piece(name, src, target, core)
                    wait_recv(came, r + 6 + k)

                    @pl.loop(0, came.shape[0] // 32)
                    def _(i):
                        sl = tile(i, 32)
                        mine[sl, :] = (mine[sl, :].astype(F32) + came[sl, :].astype(F32)).astype(BF16)

                    remote(
                        mine, wgrad_place(name, dst, far, core), s + 5 + k, r + 2 * far + core,
                        (target, z),
                    ).start()

    def wgrad_finish(name, src, dst):
        s, r = sem_at["g_" + name]
        for core in (0, 1):

            @pl.when(c == core)
            def _():
                here = wgrad_piece(name, src, d, core)
                for i in range(7):
                    wait_send(here, s + i)
                wait_recv(wgrad_place(name, dst, 0, 1 - core), r + 1 - core)
                for slot in (1, 2):
                    for k in (0, 1):
                        wait_recv(wgrad_place(name, dst, slot, k), r + 2 * slot + k)
                pltpu.make_async_copy(
                    here, wgrad_place(name, dst, 0, core),
                    lsem.at[len(WEIGHTS) + WEIGHTS.index(name)],
                ).wait()

    gather_x = Gather("ag_x", buf_a)
    gather_d = Gather("ag_d", buf_c)
    gather_n = [Gather("ag_n%d" % h, buf_a, at) for h, at in enumerate(parts(PARTS_FORWARD))]
    gather_b = [Gather("ag_b%d" % h, buf_b, at) for h, at in enumerate(parts(PARTS_BACK))]
    scatter_o = [Scatter("rs_o%d" % h, part, part_x, part_r, at) for h, at in enumerate(parts(PARTS_FORWARD))]
    scatter_n = [Scatter("rs_n%d" % h, part, part_x, part_r, at) for h, at in enumerate(parts(PARTS_BACK))]
    scatter_i = [Scatter("rs_i%d" % h, part, part_x, part_r, at) for h, at in enumerate(parts(PARTS_LAST))]
    scatter_m = Scatter("rs_m", mix, mix_x, mix_r)

    sz, rz = sem_at["sm_z"]
    sd, rd = sem_at["sm_d"]
    small[d, z] = small_in[...]
    for i in range(1, sp):
        peer = (z + i) % sp
        remote(small_in, small.at[d, z], sz + i, rz + z, (d, peer)).start()
    gather_x.start(x_in)
    for i in range(1, sp):
        peer = (z + i) % sp
        wait_recv(small.at[d, peer], rz + peer)
    for i in range(1, dp):
        peer = (d + i) % dp
        remote(small.at[d], small.at[d], sd + i, rd + d, (peer, z)).start()
    weight_send("qkv", wqkv_in, w_qkv)

    block(buf_a, z, c)[...] = x_in[...]
    own_len = small_in[7:8, 0:1]

    @pl.loop(0, slots // 32)
    def _(i):
        sl = tile(i, 32)
        pos = (iota((32, 1), 0) + (z * slots + i * 32)).astype(F32)
        keep = jnp.where(pos < own_len, 1.0, 0.0)
        block(buf_c, z, c)[sl, :] = (cot_in[sl, :].astype(F32) * keep).astype(BF16)

    @pl.when(c == 1)
    def _():
        pad = plan.ff_wide - plan.ff_slim
        for ref in (w_gate, w_up, w_down):
            ref[:, plan.ff_slim :] = jnp.zeros((width, pad), BF16)

    for i in range(1, dp):
        peer = (d + i) % dp
        wait_recv(small.at[peer], rd + peer)
    per_dp = width // dp // 128
    for i in range(dp):
        for h in range(per_dp):
            at = (i * per_dp + h) * 128
            vecs[:, at : at + 128] = small[i, 2 * h] + small[i, 2 * h + 1]
    bias_at = 2 * z + c
    for h in range(sp // 2):
        for k in range(3):
            at = h * 384 + k * 128
            qbias[0:1, at : at + 128] = (
                small[bias_at, 2 * h, 4 + k : 5 + k, :] + small[bias_at, 2 * h + 1, 4 + k : 5 + k, :]
            )
    for r in range(2):
        lens[r : r + 1, :] = small[2 * chip + r, 0, 7:8, :]

    n1 = buf_b
    gain_one, bias_one = vecs[0:1, :], vecs[1:2, :]

    @pl.loop(0, sp)
    def _(i):
        @pl.when(i == last - 1)
        def _():
            weight_forward("qkv", w_qkv)
            weight_send("out", wout_in, w_out)

        @pl.when(i == last)
        def _():
            weight_forward("out", w_out)
            weight_send("gate", wg_in, w_gate)
            weight_send("up", wu_in, w_up)

        @pl.when(i > 0)
        def _():
            gather_x.hop(i)

        t = order(i)
        gather_x.need(t)
        src, dst = rows_of(buf_a, t), rows_of(n1, t)

        @pl.loop(0, chunk // 64)
        def _(j):
            sl = tile(j, 64)
            unit, _ = normalize(src[sl, :].astype(F32))
            dst[sl, :] = (unit * vecs[0:1, :] + vecs[1:2, :]).astype(BF16)

    gather_d.start(block(buf_c, z, c))
    n1_copy = pltpu.make_async_copy(n1, n1_hbm, lsem.at[2 * len(WEIGHTS)])
    n1_copy.start()

    weight_wait("qkv", wqkv_in, w_qkv)
    low = iota((1, 128), 1) < 64
    first_half = iota((1, 128), 1) % 64 < ROT // 2

    def rotated(v, cosine, sine):
        swapped = jnp.where(
            first_half, pltpu.roll(v, 128 - ROT // 2, 1), pltpu.roll(v, ROT // 2, 1)
        )
        return v * cosine + swapped * sine

    raw = (resid, dres)

    @pl.loop(0, sp)
    def _(t):
        src = rows_of(n1, t)

        both = dot_nn(src[...], w_qkv[...]) + qbias[0:1, :]
        for r in range(2):
            raw[r][:, 0 : plan.qkv_cols] = both[r * slots : (r + 1) * slots]

        here = tile(t, slots)
        cosine, sine = cos_in[here, :], sin_in[here, :]
        for r in range(2):
            for p in range(plan.pairs):
                v0 = raw[r][:, p * 384 : p * 384 + 128]
                v1 = raw[r][:, p * 384 + 128 : p * 384 + 256]
                v2 = raw[r][:, p * 384 + 256 : p * 384 + 384]
                r0 = rotated(v0, cosine, sine)
                r1 = rotated(v1, cosine, sine)
                r2 = rotated(v2, cosine, sine)
                q_ref[r, p, here, :] = jnp.where(low, r0, r1).astype(BF16)
                k_ref[r, p, here, :] = pltpu.roll(jnp.where(low, r2, r0), 64, 1).astype(BF16)
                v_ref[r, p, here, :] = jnp.where(low, v1, v2).astype(BF16)

    q_rows = min(256, plan.seq)
    q_blocks = plan.seq // q_rows
    per_q = q_rows // slots
    scale = HEAD_DIM ** (-0.5)

    def weights_of(r, p, h, qb):
        keys_to = (qb + 1) * q_rows
        mask = low if h == 0 else jnp.logical_not(low)
        qh = jnp.where(mask, q_ref[r, p, qb * q_rows : keys_to, :], 0).astype(BF16)
        scores = dot_nt(k_ref[r, p, 0:keys_to, :], qh) * scale
        key_pos = iota((keys_to, q_rows), 0)
        query_pos = iota((keys_to, q_rows), 1) + qb * q_rows
        length = lens[pl.ds(r, 1), 0:1]
        allowed = (key_pos <= query_pos) & (key_pos.astype(F32) < length)
        scores = jnp.where(allowed, scores, neg_large)
        expo = jnp.exp(scores - jnp.max(scores, axis=0, keepdims=True))
        return expo * (1.0 / jnp.sum(expo, axis=0, keepdims=True))

    def att_rows(r, t):
        return pl.ds(pl.multiple_of(t * chunk + r * slots, slots), slots)

    def attention(r, p):
        for qb in range(q_blocks):
            outs = []
            for h in range(2):
                probs = weights_of(r, p, h, qb).astype(BF16)
                outs.append(dot_tn(probs, v_ref[r, p, 0 : (qb + 1) * q_rows, :]))
            both = jnp.where(low, outs[0], outs[1]).astype(BF16)
            for i in range(per_q):
                att[att_rows(r, qb * per_q + i), p * 128 : (p + 1) * 128] = both[
                    i * slots : (i + 1) * slots
                ]

    @pl.loop(0, 2)
    def _(r):
        for p in range(plan.pairs):
            attention(r, p)

    gather_d.hop(1)
    gather_x.drain(x_in)

    weight_forward("gate", w_gate)
    weight_send("down", wd_in, w_down)
    weight_wait("out", wout_in, w_out)

    def far_first(i):
        return jnp.where(z < last - z, last - i, i)

    @pl.loop(0, sp)
    def _(i):
        t = far_first(i)
        src, dst = rows_of(att, t), rows_of(part, t)

        for sl in spans(width, 512):
            dst[:, sl] = dot_nn(src[...], w_out[:, sl]).astype(BF16)

        for part_o in scatter_o:
            part_o.core(t)

        @pl.when(i == 1)
        def _():
            scatter_o[0].step(0)

    own_n = block(buf_a, z, c)

    def second_norm(at):
        rows = pl.ds(*at)
        x_rows, acc_rows, resid_rows, n_rows = (
            ref.at[rows] for ref in (x_in, acc, resid, own_n)
        )

        @pl.loop(0, at[1] // 32)
        def _(i):
            sl = tile(i, 32)
            hidden = x_rows[sl, :].astype(F32) + acc_rows[sl, :]
            resid_rows[sl, :] = hidden
            unit, _ = normalize(hidden)
            n_rows[sl, :] = (unit * vecs[2:3, :] + vecs[3:4, :]).astype(BF16)

    def pipeline(scatters, total, middle, gathers, buf, extra, started=False):
        if not started:
            scatters[0].step(0)
        for h, scatter in enumerate(scatters):
            for k in range(1, sp - 1):
                extra()
                scatter.step(k)
                if h:
                    gathers[h - 1].hop(k)
            if h + 1 < len(scatters):
                scatters[h + 1].step(0)
            extra()
            scatter.final(total)
            middle(scatter.at)
            gathers[h].start(sub_block(buf, z, c, scatter.at))
            if h:
                for k in range(sp - 1, sp):
                    gathers[h - 1].hop(k)

    def one_by_one(*steps):
        todo = list(steps)

        def extra():
            if todo:
                todo.pop(0)()

        return extra, todo

    extra, todo = one_by_one(
        lambda: None,
        lambda: (weight_forward("up", w_up), gather_d.hop(2)),
        lambda: None,
        lambda: weight_forward("down", w_down),
    )
    pipeline(scatter_o, acc, second_norm, gather_n, buf_a, extra, True)
    for step in todo:
        step()
    for part_o in scatter_o:
        part_o.drain()
    n1_copy.wait()

    def feed_forward(t):
        for part_n in gather_n:
            part_n.need(t)
        tok = rows_of(buf_a, t)
        act_t, dg_t, du_t = rows_of(act, t), rows_of(dgate, t), rows_of(dup, t)
        for sl in spans(plan.ff_wide, 256):
            gate = dot_nn(tok[...], w_gate[:, sl])
            up = dot_nn(tok[...], w_up[:, sl])
            sig = jax.nn.sigmoid(gate)
            silu = gate * sig
            act_t[:, sl] = (silu * up).astype(BF16)
            du_t[:, sl] = silu.astype(BF16)
            dg_t[:, sl] = (up * sig * (1.0 + gate * (1.0 - sig))).astype(BF16)

    def feed_back(t):
        gather_d.need(t)
        dg_t, du_t = rows_of(dgate, t), rows_of(dup, t)
        gout, part_t = rows_of(buf_c, t), rows_of(part, t)
        for sl in spans(plan.ff_wide, 256):
            d_act = dot_nn(gout[...], w_down[:, sl])
            du_t[:, sl] = (d_act * du_t[:, sl].astype(F32)).astype(BF16)
            dg_t[:, sl] = (d_act * dg_t[:, sl].astype(F32)).astype(BF16)
        for sl in spans(width, 512):
            part_t[:, sl] = (
                dot_nt(dg_t[...], w_gate[sl, :]) + dot_nt(du_t[...], w_up[sl, :])
            ).astype(BF16)
        for part_n in scatter_n:
            part_n.core(t)

    weight_wait("gate", wg_in, w_gate)
    weight_wait("up", wu_in, w_up)

    @pl.loop(0, sp)
    def _(i):
        @pl.when(i > 0)
        def _():
            gather_n[-1].hop(i)

        @pl.when(i == last)
        def _():
            for k in range(3, sp):
                gather_d.hop(k)

        feed_forward(order(i))

        @pl.when(i == BACK_FROM)
        def _():
            weight_wait("down", wd_in, w_down)

        first = jnp.where(i == BACK_FROM, 0, i)
        stop = jnp.where(i < BACK_FROM, 0, i + 1)

        @pl.loop(first, stop)
        def _(j):
            feed_back(order(j))

    def wgrad(tokens, cols, dst, start, stop):
        @pl.loop(start, stop)
        def _(n):
            sl = tile(n, 512)
            dst[sl, :] = dot_tn(tokens[:, sl], cols[...]).astype(BF16)

    n_tiles = width // 512
    half = n_tiles // 2
    for name, src, dst in (("down", wd_in, w_down), ("gate", wg_in, w_gate), ("up", wu_in, w_up)):
        weight_drain(name, src, dst)
    colsum[...] = jnp.zeros_like(colsum)
    own_d, own_b = block(buf_c, z, c), block(buf_b, z, c)

    def norm_back(grad, hidden, gain, row):
        unit, rstd = normalize(hidden)
        colsum[row : row + 1, :] += jnp.sum(grad * unit, axis=0, keepdims=True)
        colsum[row + 1 : row + 2, :] += jnp.sum(grad, axis=0, keepdims=True)
        scaled = grad * gain
        return rstd * (
            scaled
            - jnp.mean(scaled, axis=-1, keepdims=True)
            - unit * jnp.mean(scaled * unit, axis=-1, keepdims=True)
        )

    def second_norm_back(at):
        rows = pl.ds(*at)
        d_rows, acc_rows, resid_rows, dres_rows, b_rows = (
            ref.at[rows] for ref in (own_d, acc, resid, dres, own_b)
        )

        @pl.loop(0, at[1] // 32)
        def _(i):
            sl = tile(i, 32)
            back = d_rows[sl, :].astype(F32) + norm_back(
                acc_rows[sl, :], resid_rows[sl, :], vecs[2:3, :], 2
            )
            dres_rows[sl, :] = back
            b_rows[sl, :] = back.astype(BF16)

    def mixed():
        @pl.loop(0, sp)
        def _(i):
            t = far_first(i)
            act_t, mix_t = rows_of(act, t), rows_of(mix, t)
            for sl in spans(width, 512):
                mix_t[:, sl] = dot_nt(act_t[...], w_down[sl, :]).astype(BF16)
            scatter_m.core(t)

    def all_down():
        wgrad(buf_c, act, w_down, 0, n_tiles)
        wgrad_send("down", w_down, rg_down, st_down)

    def first_gate():
        wgrad(buf_a, dgate, w_gate, 0, half)

    def last_gate():
        wgrad(buf_a, dgate, w_gate, half, n_tiles)
        wgrad_send("gate", w_gate, rg_gate, st_gate)

    def first_up():
        wgrad(buf_a, dup, w_up, 0, half)

    def last_up():
        wgrad(buf_a, dup, w_up, half, n_tiles)
        wgrad_send("up", w_up, rg_up, st_up)

    extra, todo = one_by_one(lambda: (mixed(), all_down()), first_gate, last_gate, first_up, last_up)
    pipeline(scatter_n, acc, second_norm_back, gather_b, buf_b, extra)
    for step in todo:
        step()

    for h, part_n in enumerate(gather_n):
        part_n.drain(sub_block(buf_a, z, c, part_n.at))
    n1_back = pltpu.make_async_copy(n1_hbm, buf_a, lsem.at[2 * len(WEIGHTS) + 1])
    n1_back.start()
    datt = dgate.at[:, pl.ds(0, plan.head_cols)]
    dqkv = act.at[:, pl.ds(0, plan.qkv_cols)]
    for part_n in scatter_n:
        part_n.drain()
    scatter_m.step(0)
    wgrad_merge("down", w_down, rg_down, st_down)

    @pl.loop(0, sp)
    def _(i):
        @pl.when(i > 0)
        def _():
            gather_b[-1].hop(i)

        @pl.when((i > 0) & (i < last))
        def _():
            scatter_m.step(i)

        t = order(i)
        for part_b in gather_b:
            part_b.need(t)
        datt[tile(t, chunk), :] = dot_nt(rows_of(buf_b, t)[...], w_out[...]).astype(BF16)

    wgrad_merge("gate", w_gate, rg_gate, st_gate)

    biassum[...] = jnp.zeros_like(biassum)

    def attention_back(r, p):
        cols = slice(p * 128, (p + 1) * 128)
        for qb in range(q_blocks):
            keys_to = (qb + 1) * q_rows
            dav = jnp.concatenate(
                [datt[att_rows(r, qb * per_q + i), cols] for i in range(per_q)], axis=0
            )
            qv = q_ref[r, p, qb * q_rows : keys_to, :]
            dq, dk, dv = [], [], []
            for h in range(2):
                mask = low if h == 0 else jnp.logical_not(low)
                probs = weights_of(r, p, h, qb)
                dprobs = dot_nt(v_ref[r, p, 0:keys_to, :], jnp.where(mask, dav, 0).astype(BF16))
                delta = jnp.sum(dprobs * probs, axis=0, keepdims=True)
                dscores = (probs * (dprobs - delta)).astype(BF16)
                dv.append(dot_nn(probs.astype(BF16), dav))
                dk.append(dot_nn(dscores, qv))
                dq.append(dot_tn(dscores, k_ref[r, p, 0:keys_to, :]))
            dq_both = (jnp.where(low, dq[0], dq[1]) * scale).astype(BF16)
            dk_both = jnp.where(low, dk[0], dk[1])
            dv_both = jnp.where(low, dv[0], dv[1])
            for t in range(keys_to // slots):
                ts = slice(t * slots, (t + 1) * slots)
                for at, new in ((t, dk_both), (sp + t, dv_both)):
                    lanes = slice(at * 128, (at + 1) * 128)
                    if t * slots < qb * q_rows:
                        acc[:, lanes] += new[ts]
                    else:
                        acc[:, lanes] = new[ts]
            q_ref[r, p, qb * q_rows : keys_to, :] = dq_both
        for t in range(sp):
            ts = slice(t * slots, (t + 1) * slots)
            dqv = q_ref[r, p, ts, :].astype(F32)
            dkv = (acc[:, t * 128 : (t + 1) * 128] * scale).astype(BF16).astype(F32)
            dvv = acc[:, (sp + t) * 128 : (sp + t + 1) * 128].astype(BF16).astype(F32)
            swapped = pltpu.roll(dkv, 64, 1)
            cosine, sine = cos_in[ts, :], -sin_in[ts, :]
            g0 = rotated(jnp.where(low, dqv, swapped), cosine, sine)
            g1 = jnp.where(low, dvv, rotated(dqv, cosine, sine))
            g2 = jnp.where(low, rotated(swapped, cosine, sine), dvv)
            for k, g in enumerate((g0, g1, g2)):
                g = g.astype(BF16)
                dqkv[att_rows(r, t), p * 384 + k * 128 : p * 384 + (k + 1) * 128] = g
                row = 3 * p + k
                biassum[row : row + 1, :] += jnp.sum(g.astype(F32), axis=0, keepdims=True)

    @pl.loop(0, 2)
    def _(r):
        for p in range(plan.pairs):
            attention_back(r, p)

    wgrad_merge("up", w_up, rg_up, st_up)

    @pl.loop(0, sp)
    def _(i):
        t = far_first(i)
        dst, src = rows_of(part, t), rows_of(dqkv, t)

        for sl in spans(width, 512):
            dst[:, sl] = dot_nt(src[...], w_qkv[sl, :]).astype(BF16)

        for part_i in scatter_i:
            part_i.core(t)

        @pl.when(i == 1)
        def _():
            for part_i in scatter_i:
                part_i.step(0)

    weight_drain("qkv", wqkv_in, w_qkv)
    weight_drain("out", wout_in, w_out)
    n1_back.wait()
    wgrad(buf_a, dqkv, w_qkv, 0, n_tiles)
    wgrad_send("qkv", w_qkv, rg_qkv, st_qkv)
    for part_i in scatter_i:
        part_i.step(1)

    @pl.loop(0, width // 1024)
    def _(n):
        sl = tile(n, 1024)
        w_out[:, sl] = dot_tn(att[...], buf_b[:, sl]).astype(BF16)

    wgrad_send("out", w_out, rg_out, st_out)
    for k in range(2, sp - 1):
        for part_i in scatter_i:
            part_i.step(k)
    wgrad_merge("qkv", w_qkv, rg_qkv, st_qkv)
    scatter_m.final(acc)

    @pl.loop(0, slots // 32)
    def _(i):
        sl = tile(i, 32)
        pos = (iota((32, 1), 0) + (z * slots + i * 32)).astype(F32)
        keep = jnp.where(pos < small_in[7:8, 0:1], 1.0, 0.0)
        out_ref[sl, :] = (keep * (resid[sl, :] + acc[sl, :])).astype(BF16)

    wgrad_merge("out", w_out, rg_out, st_out)
    for part_i in scatter_i:
        part_i.final(acc)
        first = part_i.at[0] // 32

        @pl.loop(first, first + part_i.at[1] // 32)
        def _(i):
            sl = tile(i, 32)
            back = norm_back(acc[sl, :], x_in[sl, :].astype(F32), vecs[0:1, :], 0)
            grad_ref[sl, :] = dres[sl, :] + back

    per = plan.shard
    for i in range(dp):
        send_sum[i, :, 0:per] = colsum[:, i * per : (i + 1) * per]
        send_sum[i, :, per : per + 128] = biassum[...]
    sa, ra = sem_at["su_d"]
    sb, rb = sem_at["su_z"]
    recv_sum[d] = send_sum[d]
    for i in range(1, dp):
        peer = (d + i) % dp
        remote(send_sum.at[peer], recv_sum.at[d], sa + i, ra + d, (peer, z)).start()
    for i in range(1, dp):
        peer = (d + i) % dp
        wait_recv(recv_sum.at[peer], ra + peer)
    norm_total = recv_sum[0, :, 0:per]
    for i in range(1, dp):
        norm_total = norm_total + recv_sum[i, :, 0:per]
    bias_total = recv_sum[c, :, per : per + 128]
    for i in range(1, dp // 2):
        bias_total = bias_total + recv_sum[2 * i + c, :, per : per + 128]
    z_sum[z, :, 0:per] = norm_total
    z_sum[z, :, per : per + 128] = bias_total
    for i in range(1, sp):
        peer = (z + i) % sp
        remote(z_sum.at[z], z_sum.at[z], sb + i, rb + z, (d, peer)).start()
    for i in range(1, sp):
        peer = (z + i) % sp
        wait_recv(z_sum.at[peer], rb + peer)
    norm_total = z_sum[0, :, 0:per]
    for i in range(1, sp):
        norm_total = norm_total + z_sum[i, :, 0:per]
    sums_ref[:, 0:per] = norm_total
    sums_ref[:, per : per + 128] = z_sum[chip, :, per : per + 128]

    for name, src, dst in (
        ("down", w_down, rg_down), ("gate", w_gate, rg_gate), ("up", w_up, rg_up),
        ("qkv", w_qkv, rg_qkv), ("out", w_out, rg_out),
    ):
        wgrad_finish(name, src, dst)
    gather_d.drain(own_d)
    for h, part_b in enumerate(gather_b):
        part_b.drain(sub_block(buf_b, z, c, part_b.at))
    scatter_m.drain()
    for part_i in scatter_i:
        part_i.drain()
    for i in range(1, sp):
        wait_send(small_in, sz + i)
        wait_send(z_sum.at[z], sb + i)
    for i in range(1, dp):
        wait_send(small.at[d], sd + i)
        wait_send(send_sum.at[0], sa + i)


PARTS_FORWARD = 1
PARTS_BACK = 1
PARTS_LAST = 1
BACK_FROM = 1
ADD_ROWS = 64
WEIGHTS = ("qkv", "out", "gate", "up", "down")


def rotary_lanes(seq_len):
    half = ROT // 2
    freq = theta ** (-(np.arange(half, dtype=np.float32) * np.float32(2.0)) / np.float32(ROT))
    angles = np.arange(seq_len, dtype=np.float32)[:, None] * freq.astype(np.float32)[None, :]
    cosine, sine = np.cos(angles), np.sin(angles)
    cos_head = np.ones((seq_len, HEAD_DIM), np.float32)
    sin_head = np.zeros((seq_len, HEAD_DIM), np.float32)
    cos_head[:, :half], cos_head[:, half:ROT] = cosine, cosine
    sin_head[:, :half], sin_head[:, half:ROT] = -sine, sine
    return np.tile(cos_head, (1, 2)), np.tile(sin_head, (1, 2))


def last_sums_kernel(*refs):
    count = len(refs) // 2
    for src, dst in zip(refs[:2], refs[count : count + 2]):
        dst[...] = src[...]
    for src, dst in zip(refs[2:count], refs[count + 2 :]):
        total = src[0].astype(F32)
        for k in range(1, src.shape[0]):
            total = total + src[k].astype(F32)
        dst[...] = total


def last_sums(*arrays):
    steps = 4
    in_specs, out_specs, out_shape = [], [], []
    for i, array in enumerate(arrays):
        rows, cols = array.shape[-2:]
        block = (rows // steps, cols)
        out_specs.append(pl.BlockSpec(block, lambda j: (j, 0)))
        if i < 2:
            in_specs.append(pl.BlockSpec(block, lambda j: (j, 0)))
            out_shape.append(jax.ShapeDtypeStruct((rows, cols), array.dtype))
        else:
            in_specs.append(pl.BlockSpec((array.shape[0],) + block, lambda j: (0, j, 0)))
            out_shape.append(jax.ShapeDtypeStruct((rows, cols), F32))
    return pl.pallas_call(
        last_sums_kernel, grid=(steps,), in_specs=in_specs, out_specs=out_specs,
        out_shape=out_shape,
    )(*arrays)


def per_device_fast(
    layer_input, lengths, cotangent, ln1_gain, ln1_bias, ln2_gain, ln2_bias,
    qkv_weight, qkv_bias, out_weight, gate_weight, up_weight, down_weight,
):
    dp, sp = lax.axis_size("dp"), lax.axis_size("sp")
    z = lax.axis_index("sp")
    _, slots, width = layer_input.shape
    plan = Plan(dp, sp, slots, width, gate_weight.shape[1])
    sem_at = {}
    for name in WEIGHTS:
        sem_at["w_" + name] = plan.sems(8, dp)
        sem_at["g_" + name] = plan.sems(7, 8)
    split = (("o", PARTS_FORWARD), ("n", PARTS_BACK), ("i", PARTS_LAST))
    gathers = (("n", PARTS_FORWARD), ("b", PARTS_BACK))
    for name in ["ag_x", "ag_d"] + ["ag_%s%d" % (n, h) for n, k in gathers for h in range(k)]:
        sem_at[name] = plan.sems(2 + 2 * sp, 2 * sp)
    for name in ["rs_m"] + ["rs_%s%d" % (n, h) for n, k in split for h in range(k)]:
        sem_at[name] = plan.sems(2 * sp, 2 * sp + 1)
    for name in ("sm_z", "su_z"):
        sem_at[name] = plan.sems(sp, sp)
    for name in ("sm_d", "su_d"):
        sem_at[name] = plan.sems(dp, dp)

    even = z % 2 == 0
    norms = jnp.stack([ln1_gain, ln1_bias, ln2_gain, ln2_bias]).astype(F32)
    none = jnp.zeros_like(norms)
    norm_rows = jnp.where(
        even, jnp.concatenate([norms, none], 1), jnp.concatenate([none, norms], 1)
    )
    bias = qkv_bias.astype(F32)
    none = jnp.zeros_like(bias)
    bias_rows = jnp.where(
        even, jnp.concatenate([bias, none]), jnp.concatenate([none, bias])
    ).reshape(3, 128)
    len_row = jnp.broadcast_to(lengths.astype(F32)[:, None], (1, 128))
    small = jnp.concatenate([norm_rows, bias_rows, len_row], axis=0)
    cosine, sine = rotary_lanes(sp * slots)

    vmem = pl.BlockSpec(memory_space=pltpu.VMEM)
    hbm = pl.BlockSpec(memory_space=pl.ANY)
    out_shape = [
        jax.ShapeDtypeStruct((slots, width), BF16),
        jax.ShapeDtypeStruct((slots, width), F32),
        jax.ShapeDtypeStruct((8, plan.shard + 128), F32),
        jax.ShapeDtypeStruct((3,) + qkv_weight.shape, BF16),
        jax.ShapeDtypeStruct((3,) + out_weight.shape, BF16),
        jax.ShapeDtypeStruct((3,) + gate_weight.shape, BF16),
        jax.ShapeDtypeStruct((3,) + up_weight.shape, BF16),
        jax.ShapeDtypeStruct((3,) + down_weight.shape, BF16),
        jax.ShapeDtypeStruct((plan.tokens, width), BF16),
    ]
    tokens, heads, ff = plan.tokens, plan.head_cols, plan.ff_wide
    scratch = [
        pltpu.SemaphoreType.DMA((plan.count_send,)),
        pltpu.SemaphoreType.DMA((plan.count_recv,)),
        pltpu.SemaphoreType.DMA((2 * len(WEIGHTS) + 2,)),
        pltpu.VMEM((width, plan.qkv_cols), BF16),
        pltpu.VMEM((heads, width), BF16),
        pltpu.VMEM((width, ff), BF16),
        pltpu.VMEM((width, ff), BF16),
        pltpu.VMEM((width, ff), BF16),
        pltpu.VMEM((tokens, width), BF16),
        pltpu.VMEM((tokens, width), BF16),
        pltpu.VMEM((tokens, width), BF16),
        pltpu.VMEM((tokens, width), BF16),
        pltpu.VMEM((sp * slots, width), BF16),
        pltpu.VMEM(((sp + 1) * slots, width), BF16),
        pltpu.VMEM((tokens, width), BF16),
        pltpu.VMEM((sp * slots, width), BF16),
        pltpu.VMEM(((sp + 1) * slots, width), BF16),
        pltpu.VMEM((2, plan.pairs, plan.seq, 128), BF16),
        pltpu.VMEM((2, plan.pairs, plan.seq, 128), BF16),
        pltpu.VMEM((2, plan.pairs, plan.seq, 128), BF16),
        pltpu.VMEM((tokens, heads), BF16),
        pltpu.VMEM((tokens, ff), BF16),
        pltpu.VMEM((tokens, ff), BF16),
        pltpu.VMEM((tokens, ff), BF16),
        pltpu.VMEM((slots, width), F32),
        pltpu.VMEM((slots, width), F32),
        pltpu.VMEM((slots, width), F32),
        pltpu.VMEM((dp, sp, 8, 128), F32),
        pltpu.VMEM((8, width), F32),
        pltpu.VMEM((8, plan.qkv_cols), F32),
        pltpu.VMEM((8, 128), F32),
        pltpu.VMEM((8, width), F32),
        pltpu.VMEM((8, 128), F32),
        pltpu.VMEM((dp, 8, plan.shard + 128), F32),
        pltpu.VMEM((dp, 8, plan.shard + 128), F32),
        pltpu.VMEM((sp, 8, plan.shard + 128), F32),
        pltpu.VMEM((2, plan.shard, plan.qkv_cols), BF16),
        pltpu.VMEM((2, heads, plan.shard), BF16),
        pltpu.VMEM((2, plan.shard, ff), BF16),
        pltpu.VMEM((2, plan.shard, ff), BF16),
        pltpu.VMEM((2, plan.shard, ff), BF16),
    ]
    outs = pl.pallas_call(
        functools.partial(layer_kernel, plan, sem_at),
        out_shape=out_shape,
        in_specs=[vmem] * 5 + [hbm] * 5,
        out_specs=[vmem] * 3 + [hbm] * 6,
        scratch_shapes=scratch,
        compiler_params=pltpu.CompilerParams(
            collective_id=0, has_side_effects=True, vmem_limit_bytes=63 * 1024 * 1024
        ),
    )(
        layer_input[0], cotangent[0], small, jnp.asarray(cosine), jnp.asarray(sine),
        qkv_weight, out_weight, gate_weight, up_weight, down_weight,
    )
    sums = outs[2]
    own = lax.dynamic_slice_in_dim(sums[:4, : plan.shard], z * (plan.shard // sp), plan.shard // sp, 1)
    bias_grad = lax.dynamic_slice_in_dim(
        sums[:, plan.shard :].reshape(-1), z * qkv_bias.shape[0], qkv_bias.shape[0]
    )
    done = last_sums(outs[0], outs[1], *outs[3:8])
    return (
        done[0][None], done[1][None], own[0], own[1], own[2], own[3],
        done[2], bias_grad, done[3], done[4], done[5], done[6],
    )


def solution(mesh):
    placed = (
        P("dp", "sp", None),
        P("dp"),
        P("dp", "sp", None),
        P(("dp", "sp")),
        P(("dp", "sp")),
        P(("dp", "sp")),
        P(("dp", "sp")),
        P("dp", "sp"),
        P(("dp", "sp")),
        P("sp", "dp"),
        P("dp", "sp"),
        P("dp", "sp"),
        P("dp", "sp"),
    )
    fast = mesh.shape["dp"] == 8 and mesh.shape["sp"] == 4
    return jax.shard_map(
        per_device_fast if fast else per_device,
        mesh=mesh,
        in_specs=placed,
        out_specs=(
            P("dp", "sp", None),
            P("dp", "sp", None),
            P(("dp", "sp")),
            P(("dp", "sp")),
            P(("dp", "sp")),
            P(("dp", "sp")),
            P("dp", "sp"),
            P(("dp", "sp")),
            P("sp", "dp"),
            P("dp", "sp"),
            P("dp", "sp"),
            P("dp", "sp"),
        ),
        check_vma=False,
    )
```
